128 devices in a mesh: rep: 4 (over z), fsdp: 32 (over x, y, core).
Axes of the slice: x: 4, y: 4, z: 4, core: 2. Of those that a mesh axis runs over, the one named last changes fastest.
Arguments:
- momentum: float32 [4, 3, 2048, 8192], P('rep', None, 'fsdp'), may hold values from -43 to 43, as said below
- gradient: float32 [4, 3, 2048, 8192], P('rep', None, 'fsdp'), may hold values from -6 to 6
- basis: float32 [8192, 384], P(('rep', 'fsdp')), may hold values from -1 to 1
Outputs:
- momentum_next: float32 [4, 3, 2048, 8192], P('rep', None, 'fsdp')
- update: float32 [3, 2048, 8192], P(None, 'fsdp')
- basis_next: float32 [8192, 384], P(('rep', 'fsdp'))
The draws below stay inside these ranges and needn't reach their ends.
Inputs may be any that keep to these rules, and one draw needn't show every extreme that they name: momentum of each replica group, rows and columns with different scales.
All inputs are finite; a program needn't handle non-finite values.
Results may differ from the reference program's by a relative error of at most 0.0003.
Values sent between devices are 32-bit elements; how exact they have to be, the bound alone decides.
A program may use at most 192 MiB of HBM per device.

```python
import jax
import jax.numpy as jnp
from jax import lax

D = 8192
RANK = 128
ROWS_ALL = 2048
N_REP = 4


def draw_momentum(key, part):
    key = jax.random.fold_in(key, 11)
    keys = jax.random.split(key, 3)
    place = jnp.arange(ROWS_ALL, dtype=jnp.float32) / ROWS_ALL
    col_place = jnp.arange(D, dtype=jnp.float32) / D
    row_power = 0.5 * place[None, :] + 0.5 * jax.random.uniform(keys[1], (3, ROWS_ALL), jnp.float32)
    col_power = 0.5 * col_place[None, :] + 0.5 * jax.random.uniform(keys[2], (3, D), jnp.float32) - 0.5
    noise = jnp.clip(jax.random.normal(keys[0], (N_REP, 3, ROWS_ALL, D), jnp.float32), -4.0, 4.0)
    scaled = noise * jnp.power(10.0, row_power)[None, :, :, None] * jnp.power(10.0, col_power)[None, :, None, :]
    return scaled / 3.0


def draw_basis(key, part):
    key = jax.random.fold_in(key, 23)
    keys = jax.random.split(key, 3)
    perm_keys = jax.random.split(keys[0], 3)
    ranking = jnp.stack([jax.random.permutation(perm_keys[index], RANK) for index in range(3)])
    strength = jnp.power(0.03, ranking.astype(jnp.float32) / (RANK - 1))
    shared = jax.random.normal(keys[1], (D, 3, 1), jnp.float32)
    single = jax.random.normal(keys[2], (D, 3, RANK), jnp.float32)
    combined = jnp.clip(shared + strength[None, :, :] * single, -4.0, 4.0)
    return (0.25 * combined).reshape(D, 3 * RANK)


def block_scale(key, dims, cuts, low, largest):
    def one(position, parts):
        heights = jax.random.uniform(jax.random.fold_in(jax.random.fold_in(key, 6), position), (parts,), jnp.float32, low / len(cuts), largest / len(cuts))
        return jnp.repeat(jnp.exp(heights), dims[position] // parts).reshape((-1,) + (1,) * (len(dims) - position - 1))

    level = one(*cuts[0])
    for cut in cuts[1:]:
        level = level * one(*cut)
    return level


def gaussian(key, shape, scale, reach, pieces=(), kind=jnp.bfloat16):
    factor_of = block_scale(key, shape, pieces, -0.22, 0.18) if pieces else 1.0
    values = jax.random.normal(key, shape, jnp.float32) * scale * factor_of
    return jnp.minimum(jnp.maximum(values, -reach), reach).astype(kind)


def setup_inputs(seed: int = 0) -> dict:
    seeds = jax.random.split(jax.random.key(seed), 4)
    momentum = draw_momentum(jax.random.fold_in(seeds[3], 71), 0)
    gradient = gaussian(seeds[1], (N_REP, 3, ROWS_ALL, D), 1.0, 6.0, ((0, 4), (2, 32)), jnp.float32)
    basis = draw_basis(jax.random.fold_in(seeds[3], 71), 0)
    return {"momentum": momentum, "gradient": gradient, "basis": basis}


HIGH = lax.Precision.HIGHEST

def reference(momentum, gradient, basis):
    blend = momentum + gradient
    right = basis.reshape(D, 3, RANK)
    projected = jnp.einsum('gkrc,cks->krs', blend, right, precision=HIGH) / N_REP
    for sweep in range(2):
        gram = jnp.einsum('krs,krt->kst', projected, projected, precision=HIGH)
        lower = jnp.linalg.cholesky(gram)
        solved = jax.scipy.linalg.solve_triangular(lower, jnp.transpose(projected, (0, 2, 1)), lower=True)
        projected = jnp.transpose(solved, (0, 2, 1))
    column_term = jnp.einsum('gkrc,krs->cks', blend, projected, precision=HIGH) / N_REP
    flat = column_term.reshape(D, 3 * RANK)
    sums = lax.optimization_barrier(jnp.sum(flat * flat, axis=0))
    basis_next = flat / jnp.sqrt(sums + 1e-06)
    feedback = jnp.einsum('krs,cks->krc', projected, column_term, precision=HIGH)
    momentum_next = blend - 0.05 * feedback[None]
    gain = jnp.sqrt(jnp.float32(ROWS_ALL * D / RANK))
    update = gain * jnp.einsum('krs,cks->krc', projected, basis_next.reshape(D, 3, RANK), precision=HIGH)
    return (momentum_next, update, basis_next)
```

```python
import functools

import jax
import jax.numpy as jnp
from jax import lax
from jax.experimental import pallas as pl
from jax.experimental.pallas import tpu as pltpu
from jax.sharding import PartitionSpec as P

MESH = pl.DeviceIdType.MESH
HIGH = lax.Precision.HIGHEST
F32 = jnp.float32
BF16 = jnp.bfloat16
RANK = 128
N = 4
OFF = (0, 1, 3, 2)
ANY = pl.BlockSpec(memory_space=pl.ANY)
VMEM = pl.BlockSpec(memory_space=pltpu.VMEM)


def axis_of(third, phase):
    return (2, 1, 0)[(third + phase) % 3]


class Place:
    def __init__(self):
        self.rep = lax.axis_index("rep")
        self.fsdp = lax.axis_index("fsdp")
        self.core = lax.rem(self.fsdp, 2)
        self.at = (self.rep, lax.div(self.fsdp, 8), lax.rem(lax.div(self.fsdp, 2), N))

    def far(self, axis, distance):
        if isinstance(distance, int) and distance == 0:
            return self.at[axis]
        return lax.rem(self.at[axis] + distance, N)

    def chip(self, axis, distance):
        at = list(self.at)
        at[axis] = self.far(axis, distance)
        return (at[0], (at[1] * N + at[2]) * 2 + self.core)

    def sibling(self):
        return (self.rep, self.fsdp + 1 - 2 * self.core)

    def line(self, third, j1, j2, i):
        off1, off2 = dyn_off(j1), dyn_off(j2)
        places = []
        for t in range(3):
            where = [None] * 3
            where[axis_of(t, 0)] = i
            where[axis_of(t, 1)] = self.far(axis_of(t, 1), off1)
            where[axis_of(t, 2)] = self.far(axis_of(t, 2), off2)
            places.append(where)
        return [jnp.where(third == 0, a, jnp.where(third == 1, b, c)) for a, b, c in zip(*places)]


def dyn_off(j):
    return OFF[j] if isinstance(j, int) else j + (j // 2) * (5 - 2 * j)


def greet(place, distances):
    barrier = pltpu.get_barrier_semaphore()
    peers = [place.sibling()] + [place.chip(axis, d) for axis, d in distances]
    for peer in peers:
        pl.semaphore_signal(barrier, inc=1, device_id=peer, device_id_type=MESH)
    pl.semaphore_wait(barrier, len(peers))


NEAR = [(axis, d) for axis in range(3) for d in (1, 3)]


def gather_sems():
    dma = pltpu.SemaphoreType.DMA
    return [dma((3, 3, 4, 2))] * 4 + [dma((3, 4, 4))] * 2


def gather(place, buf, sems, hook=None):
    send_a, recv_a, send_b, recv_b, send_d, recv_d = sems
    core = place.core
    rows = buf.shape[5]
    half = rows // 2

    def index(t, p, j, da, part=None):
        where = [None] * 3
        for q in range(3):
            axis = axis_of(t, q)
            if q < p - 1:
                where[axis] = slice(None)
            elif q == p - 1:
                where[axis] = place.far(axis, dyn_off(j))
            elif q == p:
                where[axis] = place.far(axis, da)
            else:
                where[axis] = place.at[axis]
        span = slice(None) if part is None else pl.ds(part * half, half)
        return (t, *where, core, span)

    def copy_a(t, p, j, d, da):
        spot = buf.at[index(t, p, j, da)]
        return pltpu.make_async_remote_copy(
            spot, spot, send_a.at[t, p, j, d], recv_a.at[t, p, j, d],
            device_id=place.chip(axis_of(t, p), 1 if d == 0 else 3), device_id_type=MESH)

    def copy_b(t, p, j, d, da):
        spot = buf.at[index(t, p, j, da, d)]
        return pltpu.make_async_remote_copy(
            spot, spot, send_b.at[t, p, j, d], recv_b.at[t, p, j, d],
            device_id=place.chip(axis_of(t, p), 1 if d == 0 else 3), device_id_type=MESH)

    def copy_d(t, j1, j2, whose):
        where = [None] * 3
        where[axis_of(t, 0)] = slice(None)
        where[axis_of(t, 1)] = place.far(axis_of(t, 1), dyn_off(j1))
        where[axis_of(t, 2)] = place.far(axis_of(t, 2), dyn_off(j2))
        spot = buf.at[(t, *where, whose)]
        return pltpu.make_async_remote_copy(
            spot, spot, send_d.at[t, j1, j2], recv_d.at[t, j1, j2],
            device_id=place.sibling(), device_id_type=MESH)

    def start_a(t, p, j):
        for d in range(2):
            copy_a(t, p, j, d, 0).start()

    def land_a(t, p, j, d):
        copy_a(t, p, j, d, 3 if d == 0 else 1).wait_recv()
        copy_b(t, p, j, d, 3 if d == 0 else 1).start()

    def land_b(t, p, j):
        for d in range(2):
            copy_b(t, p, j, d, 2).wait_recv()

    def line_done(j1, j2):
        for t in range(3):
            copy_d(t, j1, j2, 1 - core).wait_recv()
        if hook is not None:
            hook(j1, j2)

    thirds = range(3)
    for t in thirds:
        start_a(t, 0, 0)
    for t in thirds:
        start_a(t, 1, 0)
    yield
    for d in range(2):
        for t in thirds:
            land_a(t, 0, 0, d)
            start_a(t, 1, 2 - d)
    yield
    for t in thirds:
        land_b(t, 0, 0)
        start_a(t, 1, 3)
    for t in thirds:
        start_a(t, 2, 0)
        copy_d(t, 0, 0, core).start()
    yield
    for j in range(4):
        for t in thirds:
            for d in range(2):
                land_a(t, 1, j, d)
        yield
    for j1 in (1, 2):
        for t in thirds:
            start_a(t, 2, j1)
            copy_d(t, j1, 0, core).start()
    for j in range(4):
        for t in thirds:
            land_b(t, 1, j)
    for t in thirds:
        start_a(t, 2, 3)
        copy_d(t, 3, 0, core).start()
    yield

    @pl.loop(0, 4)
    def _(j):
        for t in thirds:
            for d in range(2):
                land_a(t, 2, j, d)
                copy_d(t, j, 2 - d, core).start()
        line_done(j, 0)

    @pl.loop(0, 4)
    def _(j):
        for t in thirds:
            land_b(t, 2, j)
            copy_d(t, j, 3, core).start()
        line_done(j, 1)
        line_done(j, 2)

        @pl.when(j >= 1)
        def _():
            line_done(j - 1, 3)

    line_done(3, 3)

    for t in thirds:
        for p in range(3):
            for j in range(1 if p == 0 else 4):
                for d in range(2):
                    copy_a(t, p, j, d, 0).wait_send()
                    copy_b(t, p, j, d, 3 if d == 0 else 1).wait_send()

    @pl.loop(0, 4)
    def _(j1):
        @pl.loop(0, 4)
        def _(j2):
            for t in thirds:
                copy_d(t, j1, j2, core).wait_send()


def split(values, parts):
    out = []
    for _ in range(parts):
        out.append(values.astype(BF16))
        values = values - out[-1].astype(F32)
    return out


def dot(left, right, dims=((1,), (0,)), precision=None):
    return lax.dot_general(left, right, (dims, ((), ())), precision=precision, preferred_element_type=F32)


NT = ((1,), (1,))
TN = ((0,), (0,))


def factor_block(both, step):
    count, size, _ = both.shape
    block = 8
    shape = (count, block, size)
    sub = lax.broadcasted_iota(jnp.int32, shape, 1)
    lane = lax.broadcasted_iota(jnp.int32, shape, 2)
    base = pl.multiple_of(step * block, block)
    spread = lambda a, i: jnp.broadcast_to(a[:, i:i + 1, :], shape)
    band = both[:, pl.ds(base, block), :]
    upper, lower = band[:, :, :size], band[:, :, size:]
    turned = jnp.stack([pltpu.roll(upper[k], lax.rem(size - base, size), 1) for k in range(count)])
    columns = [jnp.broadcast_to(turned[:, :, i:i + 1], shape) for i in range(block)]
    inverse = jnp.zeros(shape, F32)
    for i in range(block):
        recip = 1.0 / spread(columns[i], i)
        factor = jnp.where(sub > i, columns[i] * recip, 0.0)
        inverse = jnp.where(sub == i, recip, inverse)
        for q in range(i + 1, block):
            columns[q] = columns[q] - factor * spread(columns[q], i)
        upper = upper - factor * spread(upper, i)
        lower = lower - factor * spread(lower, i)
    factors = jnp.where(lane >= base + block, upper * inverse, 0.0)
    rows = jnp.concatenate([upper, lower], 2)
    less = []
    for k in range(count):
        h, m, l = [p.astype(F32) for p in split(factors[k], 3)]
        first = jnp.concatenate([h, h, h, m, m, l], 0).astype(BF16)
        h, m, l = [p.astype(F32) for p in split(rows[k], 3)]
        less.append(dot(first, jnp.concatenate([h, m, l, h, m, h], 0).astype(BF16), TN))
    for k in range(count):
        both[k] = both[k] - less[k]
    both[:, pl.ds(base, block), :] = jnp.concatenate([upper, lower * jnp.sqrt(inverse)], 2)


def main_kernel(m_hbm, g_hbm, q_hbm, parts, qbuf, left_ref, scale_ref,
                mbuf, gbuf, part, zbuf, raw, stacked, both, full, other,
                ra0, rb0, ra1, rb1, ra2, rb2, pair, mix, squares, wide,
                q_sem, load_sem, z_send, z_recv, d_send, d_recv, s_send, s_recv, x_send, x_recv, *sems):
    place = Place()
    z, x, y = place.at
    core = place.core
    sems_q, sems_raw, sems_term = sems[:6], sems[6:12], sems[12:]
    count, stack_rows, width = parts.shape
    slots, _, rows, span = mbuf.shape
    chunks = width // span

    def columns(i):
        return pl.ds(pl.multiple_of(i * span, span), span)

    def load(i):
        slot = lax.rem(i, slots)
        return (pltpu.make_async_copy(m_hbm.at[:, :, columns(i)], mbuf.at[slot], load_sem.at[0, slot]),
                pltpu.make_async_copy(g_hbm.at[:, :, columns(i)], gbuf.at[slot], load_sem.at[1, slot]))

    def blend(first, last):
        @pl.loop(first, last)
        def _(i):
            slot = lax.rem(i, slots)
            for copy in load(i):
                copy.wait()
            for t in range(count):
                parts[t, :, columns(i)] = jnp.concatenate(split(mbuf[slot, t] + gbuf[slot, t], 3), 0)

            @pl.when(i + slots < chunks)
            def _():
                for copy in load(i + slots):
                    copy.start()

    loads = [pltpu.make_async_copy(q_hbm.at[:, pl.ds(t * RANK, RANK)], qbuf.at[t, z, x, y, core], q_sem.at[t])
             for t in range(3)]
    for copy in loads:
        copy.start()
    for i in range(slots):
        for copy in load(i):
            copy.start()
    greet(place, NEAR + [(0, 2)])
    for copy in loads:
        copy.wait()
    part[...] = jnp.zeros_like(part)

    def hook(j1, j2):
        @pl.loop(0, 3)
        def _(t):
            left, right = [], []
            for i in range(N):
                cz, cx, cy = place.line(t, j1, j2, i)
                column = pl.multiple_of(((cz * N + cx) * N + cy) * RANK, RANK)
                left.append(parts[t, :, pl.ds(column, RANK)])
                right.append(qbuf[t, cz, cx, cy].reshape(RANK, RANK))
            left = jnp.concatenate(left, 1)
            h, m, l = split(jnp.concatenate(right, 0), 3)
            out = dot(left, jnp.concatenate([h, m], 1))
            tile = lambda i, j: out[i * rows:(i + 1) * rows, j * RANK:(j + 1) * RANK]
            small = (tile(2, 0) + tile(1, 1)) + dot(left[:rows], l)
            part[t] += (small + (tile(1, 0) + tile(0, 1))) + tile(0, 0)

    done = 0
    for _ in gather(place, qbuf, sems_q, hook):
        if done < chunks:
            blend(done, min(done + 3, chunks))
            done += 3

    quarter = rows // N
    sends = []
    for d in (1, 2, 3):
        to = place.far(0, d)
        sends.append(pltpu.make_async_remote_copy(
            part.at[:, pl.ds(pl.multiple_of(to * quarter, quarter), quarter)], zbuf.at[d],
            z_send.at[d], z_recv.at[d], device_id=place.chip(0, d), device_id_type=MESH))
        sends[-1].start()
    zbuf[0] = part[:, pl.ds(pl.multiple_of(z * quarter, quarter), quarter)]
    for send in sends:
        send.wait_recv()
    total = ((zbuf[0] + zbuf[1]) + (zbuf[2] + zbuf[3])) * (1.0 / N)
    for t in range(3):
        raw[t, z, x, y, core] = total[t]
    for send in sends:
        send.wait_send()
    for _ in gather(place, raw, sems_raw):
        pass

    eye = (lax.broadcasted_iota(jnp.int32, (RANK, RANK), 0) == lax.broadcasted_iota(jnp.int32, (RANK, RANK), 1)).astype(F32)
    for t in range(3):
        h, m, l = [p.astype(F32) for p in split(raw[t, :, x, y, core].reshape(rows, RANK), 3)]
        none = jnp.zeros_like(h)
        pairs = [jnp.concatenate(pair, 1) for pair in ((h, l), (h, m), (h, none), (m, none))]
        stacked[t] = jnp.concatenate(pairs, 0).T.astype(BF16)

    def grams(inverse):
        if inverse:
            for t in range(3):
                h, m, l = split(mix[t].T, 3)
                wide[t] = jnp.concatenate([jnp.concatenate([h, m, l], 1), jnp.concatenate([m, h, h], 1)], 0)

        def add(i, grams):
            out = []
            for t in range(3):
                whole, low = grams[t]
                some = raw[t, i].reshape(512, RANK)
                h, m, l = split(some, 3)
                if inverse:
                    main = dot(jnp.concatenate([h, m], 1), wide[t, :, :2 * RANK])
                    rest = dot(jnp.concatenate([h, l], 1), wide[t, :, 2 * RANK:])
                    h, m, l = split(main[:, :RANK] + (main[:, RANK:] + rest), 3)
                all_ = dot(jnp.concatenate([h, m, l], 1), jnp.concatenate([h, m], 1), TN)
                tile = lambda i, j: all_[i * RANK:(i + 1) * RANK, j * RANK:(j + 1) * RANK]
                out.append((whole + (tile(0, 0) + ((tile(0, 1) + tile(1, 0)) + tile(1, 1))), low + tile(2, 0)))
            return tuple(out)

        zero = jnp.zeros((RANK, RANK), F32)
        for t, (whole, low) in enumerate(lax.fori_loop(0, N, add, ((zero, zero),) * 3)):
            both[t, :, :RANK] = whole + (low + low.T)
            both[t, :, RANK:] = eye

    grams(False)

    def swap(t, cz, cx):
        return pltpu.make_async_remote_copy(
            full.at[t, cz, cx, :, 1 - core], other.at[t, cz, cx], d_send.at[t, cz, cx], d_recv.at[t, cz, cx],
            device_id=place.sibling(), device_id_type=MESH)

    @pl.loop(0, N * N)
    def _(i):
        cz, cx = i // N, lax.rem(i, N)
        column = pl.multiple_of(i * (N * RANK), N * RANK)
        for t in range(3):
            right = parts[t, :, pl.ds(column, N * RANK)]
            out = dot(stacked[t], jnp.concatenate([right, right[:rows]], 0))
            out = out[:RANK] + out[RANK:]
            for cy in range(N):
                full[t, cz, cx, cy] = out[:, cy * RANK:(cy + 1) * RANK].reshape(2, RANK // 2, RANK)
        factor_block(both, i)
        for t in range(3):
            swap(t, cz, cx).start()

    for t in range(3):
        mix[t] = both[t, :, RANK:]
    grams(True)

    @pl.loop(0, N * N)
    def _(i):
        cz, cx = i // N, lax.rem(i, N)
        for t in range(3):
            swap(t, cz, cx).wait_recv()
            full[t, cz, cx, :, core] += other[t, cz, cx]

    half = RANK // 4
    first = (ra0, ra1, ra2)
    whole = (rb0, rb1, rb2)

    def index(t, q, da, part=None):
        where = [None] * 3
        for p in range(3):
            axis = axis_of(t, p)
            if p < 2 - q:
                where[axis] = slice(None)
            elif p == 2 - q:
                where[axis] = place.far(axis, da)
            else:
                where[axis] = place.at[axis]
        span = slice(None) if part is None else pl.ds(part * half, half)
        return (t, *where, core, span)

    def hop_a(t, q, d):
        return pltpu.make_async_remote_copy(
            full.at[index(t, q, 2, d)], first[q].at[t, d], s_send.at[t, q, 0, d], s_recv.at[t, q, 0, d],
            device_id=place.chip(axis_of(t, 2 - q), 1 if d == 0 else 3), device_id_type=MESH)

    def hop_b(t, q, d):
        return pltpu.make_async_remote_copy(
            full.at[index(t, q, 1 if d == 0 else 3)], whole[q].at[t, d], s_send.at[t, q, 1, d], s_recv.at[t, q, 1, d],
            device_id=place.chip(axis_of(t, 2 - q), 1 if d == 0 else 3), device_id_type=MESH)

    for q in range(3):
        for t in range(3):
            for d in range(2):
                hop_a(t, q, d).start()
        if q == 0:
            pl.loop(0, 8)(lambda i: factor_block(both, i))
        for t in range(3):
            for d in range(2):
                hop_a(t, q, d).wait_recv()
                spot = index(t, q, 1 if d == 0 else 3, d)
                full[spot] = full[spot] + first[q][t, d]
                hop_b(t, q, d).start()
        if q == 0:
            pl.loop(8, 16)(lambda i: factor_block(both, i))
            for t in range(3):
                left = dot(raw[t, :, x, y, core].reshape(rows, RANK), mix[t], NT, HIGH)
                inv = both[t, :, RANK:]
                left_ref[t] = dot(left, inv, NT, HIGH)
                mix[t] = dot(inv, mix[t], precision=HIGH) * (1.0 / N)
        for t in range(3):
            spot = index(t, q, 0)
            for d in range(2):
                hop_b(t, q, d).wait_recv()
                full[spot] = full[spot] + whole[q][t, d]

    for t in range(3):
        pair[t, core] = full[t, z, x, y, core]
    half_swap = pltpu.make_async_remote_copy(
        pair.at[:, core], pair.at[:, core], x_send, x_recv, device_id=place.sibling(), device_id_type=MESH)
    half_swap.start()
    pltpu.make_async_remote_copy(
        pair.at[:, 1 - core], pair.at[:, 1 - core], x_send, x_recv, device_id=place.sibling(),
        device_id_type=MESH).wait_recv()
    half_swap.wait_send()
    term = qbuf
    mine = pl.ds(pl.multiple_of(core * (RANK // 2), RANK // 2), RANK // 2)
    for t in range(3):
        term[t, z, x, y, core] = dot(mix[t, mine, :], pair[t].reshape(RANK, RANK), precision=HIGH)
    ones = jnp.ones((8, RANK), F32)

    def keep(j1, j2):
        for t in range(3):
            where = [slice(None)] * 3
            for p, j in ((1, j1), (2, j2)):
                where[axis_of(t, p)] = place.far(axis_of(t, p), dyn_off(j))
            block = term[(t, *where)].reshape(N, RANK, RANK)
            block = block * block
            total = (block[0] + block[1]) + (block[2] + block[3])
            squares[t, where[axis_of(t, 1)], where[axis_of(t, 2)]] = dot(ones, total, NT, HIGH)

    for _ in gather(place, term, sems_term, keep):
        pass
    for t in range(3):
        total = jnp.sum(squares[t].reshape(N * N, 8, RANK), axis=0)
        scale_ref[t] = 1.0 / jnp.sqrt(total + 1e-6)
    for q in range(3):
        for t in range(3):
            for d in range(2):
                hop_a(t, q, d).wait_send()
                hop_b(t, q, d).wait_send()

    @pl.loop(0, N)
    def _(cz):
        @pl.loop(0, N)
        def _(cx):
            for t in range(3):
                swap(t, cz, cx).wait_send()


def last_kernel(gain, parts_ref, term_ref, left_ref, scale_ref, next_ref, update_ref, basis_ref):
    t, i = pl.program_id(0), pl.program_id(1)
    rows, span = update_ref.shape[1:]
    scale = scale_ref[t, 0:1, :]
    left = left_ref[t]
    high, low = split(jnp.concatenate([left * 0.05, left * (scale * gain)], 0), 2)
    lhs = jnp.concatenate([jnp.concatenate([high, high], 1), jnp.concatenate([low, jnp.zeros_like(low)], 1)], 0)
    chips = span // RANK
    for j in range(chips // N):
        line = i * (chips // N) + j
        block = term_ref[t, line // N, lax.rem(line, N)].reshape(N, RANK, RANK)
        high, low = split(jnp.concatenate([block[c] for c in range(N)], 1), 2)
        out = dot(lhs, jnp.concatenate([high, low], 0))
        out = out[:2 * rows] + out[2 * rows:]
        here = slice(j * N * RANK, (j + 1) * N * RANK)
        column = pl.multiple_of(line * (N * RANK), N * RANK)
        h, m, l = [parts_ref[t, k * rows:(k + 1) * rows, pl.ds(column, N * RANK)].astype(F32) for k in range(3)]
        next_ref[0, 0, :, here] = (h + (m + l)) - out[:rows]
        update_ref[0, :, here] = out[rows:]

    @pl.when(i == 0)
    def _():
        place = Place()
        z, x, y = place.at
        basis = term_ref[t, z, x, y].reshape(RANK, RANK).T * scale
        basis_ref[...] = jnp.where(place.core == 0, basis[:64], basis[64:])


def body(momentum, gradient, basis):
    momentum, gradient = momentum[0], gradient[0]
    count, rows, width = momentum.shape
    chips = (N, N, N, 2)
    dma = pltpu.SemaphoreType.DMA
    f32 = lambda *shape: jax.ShapeDtypeStruct(shape, F32)
    room = lambda *shape: pltpu.VMEM(shape, F32)
    kept = [pltpu.VMEM((count, 3 * rows, width), BF16), room(3, *chips, 64, RANK)]
    parts, term, left, scale = pl.pallas_call(
        main_kernel,
        name="dion",
        out_shape=kept + [room(3, rows, RANK), room(3, 8, RANK)],
        in_specs=[ANY] * 3,
        out_specs=[VMEM] * 4,
        scratch_shapes=[
            room(4, count, rows, 512), room(4, count, rows, 512),
            room(count, rows, RANK), room(N, 3, 16, RANK), room(3, *chips, 16, RANK),
            pltpu.VMEM((3, 2 * RANK, 4 * rows), BF16), room(3, RANK, 2 * RANK),
            room(3, *chips, 64, RANK), room(3, N, N, N, 64, RANK),
            room(3, 2, N, N, 32, RANK), room(3, 2, N, N, 64, RANK),
            room(3, 2, N, 32, RANK), room(3, 2, N, 64, RANK),
            room(3, 2, 32, RANK), room(3, 2, 64, RANK),
            room(3, 2, 64, RANK), room(3, RANK, RANK), room(3, N, N, 8, RANK),
            pltpu.VMEM((3, 2 * RANK, 3 * RANK), BF16),
            dma((3,)), dma((2, 4)), dma((4,)), dma((4,)),
            dma((3, N, N)), dma((3, N, N)), dma((3, 3, 2, 2)), dma((3, 3, 2, 2)), dma, dma] + gather_sems() * 3,
        compiler_params=pltpu.CompilerParams(collective_id=0, has_side_effects=True, vmem_limit_bytes=40 * 2 ** 20),
    )(momentum, gradient, basis)
    gain = float((2048 * 8192 / RANK) ** 0.5)
    span = 2048
    parts, term, left, scale = [pltpu.with_memory_space_constraint(a, pltpu.VMEM) for a in (parts, term, left, scale)]
    return pl.pallas_call(
        functools.partial(last_kernel, gain),
        name="outputs",
        grid=(3, width // span),
        out_shape=[f32(1, count, rows, width), f32(count, rows, width), f32(64, 3 * RANK)],
        in_specs=[VMEM] * 4,
        out_specs=[
            pl.BlockSpec((1, 1, rows, span), lambda t, i: (0, t, 0, i)),
            pl.BlockSpec((1, rows, span), lambda t, i: (t, 0, i)),
            pl.BlockSpec((64, RANK), lambda t, i: (0, t)),
        ],
        compiler_params=pltpu.CompilerParams(vmem_limit_bytes=16 * 2 ** 20),
    )(parts, term, left, scale)


def solution(mesh):
    placed = (P("rep", None, "fsdp", None), P("rep", None, "fsdp", None), P(("rep", "fsdp"), None))
    return jax.shard_map(
        body,
        mesh=mesh,
        in_specs=placed,
        out_specs=(P("rep", None, "fsdp", None), P(None, "fsdp", None), P(("rep", "fsdp"), None)),
        check_vma=False,
    )
```

```python
import functools

import jax
import jax.numpy as jnp
from jax import lax
from jax.experimental import pallas as pl
from jax.experimental.pallas import tpu as pltpu
from jax.sharding import PartitionSpec as P

MESH = pl.DeviceIdType.MESH
HIGH = lax.Precision.HIGHEST
F32 = jnp.float32
BF16 = jnp.bfloat16
RANK = 128
N = 4
OFF = (0, 1, 3, 2)
ANY = pl.BlockSpec(memory_space=pl.ANY)
VMEM = pl.BlockSpec(memory_space=pltpu.VMEM)


def axis_of(third, phase):
    return (2, 1, 0)[(third + phase) % 3]


class Place:
    def __init__(self):
        self.rep = lax.axis_index("rep")
        self.fsdp = lax.axis_index("fsdp")
        self.core = lax.rem(self.fsdp, 2)
        self.at = (self.rep, lax.div(self.fsdp, 8), lax.rem(lax.div(self.fsdp, 2), N))

    def far(self, axis, distance):
        if isinstance(distance, int) and distance == 0:
            return self.at[axis]
        return lax.rem(self.at[axis] + distance, N)

    def chip(self, axis, distance):
        at = list(self.at)
        at[axis] = self.far(axis, distance)
        return (at[0], (at[1] * N + at[2]) * 2 + self.core)

    def sibling(self):
        return (self.rep, self.fsdp + 1 - 2 * self.core)

    def line(self, third, j1, j2, i):
        off1, off2 = dyn_off(j1), dyn_off(j2)
        places = []
        for t in range(3):
            where = [None] * 3
            where[axis_of(t, 0)] = i
            where[axis_of(t, 1)] = self.far(axis_of(t, 1), off1)
            where[axis_of(t, 2)] = self.far(axis_of(t, 2), off2)
            places.append(where)
        return [jnp.where(third == 0, a, jnp.where(third == 1, b, c)) for a, b, c in zip(*places)]


def dyn_off(j):
    return OFF[j] if isinstance(j, int) else j + (j // 2) * (5 - 2 * j)


def greet(place, distances):
    barrier = pltpu.get_barrier_semaphore()
    peers = [place.sibling()] + [place.chip(axis, d) for axis, d in distances]
    for peer in peers:
        pl.semaphore_signal(barrier, inc=1, device_id=peer, device_id_type=MESH)
    pl.semaphore_wait(barrier, len(peers))


NEAR = [(axis, d) for axis in range(3) for d in (1, 3)]


def gather_sems():
    dma = pltpu.SemaphoreType.DMA
    return [dma((3, 3, 4, 2))] * 4 + [dma((3, 4, 4))] * 2


def gather(place, buf, sems, hook=None, stepwise=False):
    send_a, recv_a, send_b, recv_b, send_d, recv_d = sems
    core = place.core
    rows = buf.shape[5]
    half = rows // 2

    def index(t, p, j, da, part=None):
        where = [None] * 3
        for q in range(3):
            axis = axis_of(t, q)
            if q < p - 1:
                where[axis] = slice(None)
            elif q == p - 1:
                where[axis] = place.far(axis, dyn_off(j))
            elif q == p:
                where[axis] = place.far(axis, da)
            else:
                where[axis] = place.at[axis]
        span = slice(None) if part is None else pl.ds(part * half, half)
        return (t, *where, core, span)

    def copy_a(t, p, j, d, da):
        spot = buf.at[index(t, p, j, da)]
        return pltpu.make_async_remote_copy(
            spot, spot, send_a.at[t, p, j, d], recv_a.at[t, p, j, d],
            device_id=place.chip(axis_of(t, p), 1 if d == 0 else 3), device_id_type=MESH)

    def copy_b(t, p, j, d, da):
        spot = buf.at[index(t, p, j, da, d)]
        return pltpu.make_async_remote_copy(
            spot, spot, send_b.at[t, p, j, d], recv_b.at[t, p, j, d],
            device_id=place.chip(axis_of(t, p), 1 if d == 0 else 3), device_id_type=MESH)

    def copy_d(t, j1, j2, whose):
        where = [None] * 3
        where[axis_of(t, 0)] = slice(None)
        where[axis_of(t, 1)] = place.far(axis_of(t, 1), dyn_off(j1))
        where[axis_of(t, 2)] = place.far(axis_of(t, 2), dyn_off(j2))
        spot = buf.at[(t, *where, whose)]
        return pltpu.make_async_remote_copy(
            spot, spot, send_d.at[t, j1, j2], recv_d.at[t, j1, j2],
            device_id=place.sibling(), device_id_type=MESH)

    def start_a(t, p, j):
        for d in range(2):
            copy_a(t, p, j, d, 0).start()

    def land_a(t, p, j, d):
        copy_a(t, p, j, d, 3 if d == 0 else 1).wait_recv()
        copy_b(t, p, j, d, 3 if d == 0 else 1).start()

    def land_b(t, p, j):
        for d in range(2):
            copy_b(t, p, j, d, 2).wait_recv()

    def line_done(j1, j2):
        for t in range(3):
            copy_d(t, j1, j2, 1 - core).wait_recv()
        if hook is not None:
            hook(j1, j2)

    thirds = range(3)
    for t in thirds:
        start_a(t, 0, 0)
    for t in thirds:
        start_a(t, 1, 0)
    yield
    for d in range(2):
        for t in thirds:
            land_a(t, 0, 0, d)
            start_a(t, 1, 2 - d)
    yield
    for t in thirds:
        land_b(t, 0, 0)
        start_a(t, 1, 3)
    for t in thirds:
        start_a(t, 2, 0)
        copy_d(t, 0, 0, core).start()
    yield
    for j in range(4):
        for t in thirds:
            for d in range(2):
                land_a(t, 1, j, d)
        yield
    for j1 in (1, 2):
        for t in thirds:
            start_a(t, 2, j1)
            copy_d(t, j1, 0, core).start()
    for j in range(4):
        for t in thirds:
            land_b(t, 1, j)
    for t in thirds:
        start_a(t, 2, 3)
        copy_d(t, 3, 0, core).start()
    yield

    def near(j):
        for t in thirds:
            for d in range(2):
                land_a(t, 2, j, d)
                copy_d(t, j, 2 - d, core).start()
        line_done(j, 0)

    def opposite(j):
        for t in thirds:
            land_b(t, 2, j)
            copy_d(t, j, 3, core).start()
        line_done(j, 1)
        line_done(j, 2)
        if not isinstance(j, int):
            pl.when(j >= 1)(lambda: line_done(j - 1, 3))
        elif j >= 1:
            line_done(j - 1, 3)

    if stepwise:
        for step in (near, opposite):
            for j in range(4):
                step(j)
                yield
    else:
        pl.loop(0, 4)(near)
        pl.loop(0, 4)(opposite)
    line_done(3, 3)

    for t in thirds:
        for p in range(3):
            for j in range(1 if p == 0 else 4):
                for d in range(2):
                    copy_a(t, p, j, d, 0).wait_send()
                    copy_b(t, p, j, d, 3 if d == 0 else 1).wait_send()

    @pl.loop(0, 4)
    def _(j1):
        @pl.loop(0, 4)
        def _(j2):
            for t in thirds:
                copy_d(t, j1, j2, core).wait_send()


def split(values, parts):
    out = []
    for _ in range(parts):
        out.append(values.astype(BF16))
        values = values - out[-1].astype(F32)
    return out


def dot(left, right, dims=((1,), (0,)), precision=None):
    return lax.dot_general(left, right, (dims, ((), ())), precision=precision, preferred_element_type=F32)


NT = ((1,), (1,))
TN = ((0,), (0,))


def factor_block(both, step):
    count, size, _ = both.shape
    block, piece = 16, 8
    lane = lax.broadcasted_iota(jnp.int32, (count, block, size), 2)
    base = pl.multiple_of(step * block, block)
    band = both[:, pl.ds(base, block), :]
    upper, lower = band[:, :, :size], band[:, :, size:]
    inverses, done = [], []
    for part in range(block // piece):
        rows = block - part * piece
        shape = (count, rows, size)
        sub = lax.broadcasted_iota(jnp.int32, shape, 1)
        spread = lambda a, i: jnp.broadcast_to(a[:, i:i + 1, :], shape)
        turned = jnp.stack([pltpu.roll(upper[k], lax.rem(size - base, size), 1) for k in range(count)])
        columns = [jnp.broadcast_to(turned[:, :, part * piece + i:part * piece + i + 1], shape) for i in range(piece)]
        inverse = jnp.zeros((count, piece, size), F32)
        for i in range(piece):
            pivot = jnp.broadcast_to(columns[i][:, i:i + 1, :], (count, piece, size))
            recip = pl.reciprocal(pivot, approx=True)
            recip = recip * (2.0 - pivot * recip)
            recip = recip * (2.0 - pivot * recip)
            inverse = jnp.where(sub[:, :piece] == i, recip, inverse)
            factor = jnp.where(sub > i, columns[i] * jnp.concatenate([recip] * (rows // piece), 1), 0.0)
            for q in range(i + 1, piece):
                columns[q] = columns[q] - factor * spread(columns[q], i)
            upper = upper - factor * spread(upper, i)
            lower = lower - factor * spread(lower, i)
        inverses.append(inverse)
        done.append((upper[:, :piece], lower[:, :piece]))
        upper, lower = upper[:, piece:], lower[:, piece:]
    upper, lower = [jnp.concatenate(half, 1) for half in zip(*done)]
    inverse = jnp.concatenate(inverses, 1)
    factors = jnp.where(lane >= base + block, upper * inverse, 0.0)
    rows = jnp.concatenate([upper, lower], 2)
    less = []
    for k in range(count):
        h, m, l = split(factors[k], 3)
        first = jnp.concatenate([h, h, h, m, m, l], 0)
        h, m, l = split(rows[k], 3)
        less.append(dot(first, jnp.concatenate([h, m, l, h, m, h], 0), TN))
    for k in range(count):
        both[k] = both[k] - less[k]
    both[:, pl.ds(base, block), :] = jnp.concatenate([upper, lower * jnp.sqrt(inverse)], 2)


def main_kernel(m_hbm, g_hbm, q_hbm, parts, qbuf, left_ref, scale_ref,
                mbuf, gbuf, part, zbuf, zown, raw, stacked, both, full, other,
                ra0, rb0, ra1, rb1, ra2, rb2, pair, mix, squares, wide,
                q_sem, load_sem, z_send, z_recv, d_send, d_recv, s_send, s_recv, x_send, x_recv, *sems):
    place = Place()
    z, x, y = place.at
    core = place.core
    sems_q, sems_raw, sems_term = sems[:6], sems[6:12], sems[12:]
    count, stack_rows, width = parts.shape
    slots, _, rows, span = mbuf.shape
    chunks = width // span

    def columns(i):
        return pl.ds(pl.multiple_of(i * span, span), span)

    def load(i):
        slot = lax.rem(i, slots)
        return (pltpu.make_async_copy(m_hbm.at[:, :, columns(i)], mbuf.at[slot], load_sem.at[0, slot]),
                pltpu.make_async_copy(g_hbm.at[:, :, columns(i)], gbuf.at[slot], load_sem.at[1, slot]))

    def blend(first, last):
        @pl.loop(first, last)
        def _(i):
            slot = lax.rem(i, slots)
            for copy in load(i):
                copy.wait()
            for t in range(count):
                parts[t, :, columns(i)] = jnp.concatenate(split(mbuf[slot, t] + gbuf[slot, t], 3), 0)

            @pl.when(i + slots < chunks)
            def _():
                for copy in load(i + slots):
                    copy.start()

    loads = [pltpu.make_async_copy(q_hbm.at[:, pl.ds(t * RANK, RANK)], qbuf.at[t, z, x, y, core], q_sem.at[t])
             for t in range(3)]
    for copy in loads:
        copy.start()
    for i in range(slots):
        for copy in load(i):
            copy.start()
    greet(place, NEAR + [(0, 2)])
    for copy in loads:
        copy.wait()
    part[...] = jnp.zeros_like(part)

    def hook(j1, j2):
        @pl.loop(0, 3)
        def _(t):
            left, right = [], []
            for i in range(N):
                cz, cx, cy = place.line(t, j1, j2, i)
                column = pl.multiple_of(((cz * N + cx) * N + cy) * RANK, RANK)
                left.append(parts[t, :, pl.ds(column, RANK)])
                right.append(qbuf[t, cz, cx, cy].reshape(RANK, RANK))
            left = jnp.concatenate(left, 1)
            h, m, l = split(jnp.concatenate(right, 0), 3)
            out = dot(left, jnp.concatenate([h, m], 1))
            tile = lambda i, j: out[i * rows:(i + 1) * rows, j * RANK:(j + 1) * RANK]
            small = (tile(2, 0) + tile(1, 1)) + dot(left[:rows], l)
            part[t] += (small + (tile(1, 0) + tile(0, 1))) + tile(0, 0)

    done = 0
    for _ in gather(place, qbuf, sems_q, hook):
        if done < chunks:
            blend(done, min(done + 3, chunks))
            done += 3

    quarter = rows // N
    sends = []
    for d in (1, 2, 3):
        to = place.far(0, d)
        sends.append(pltpu.make_async_remote_copy(
            part.at[:, pl.ds(pl.multiple_of(to * quarter, quarter), quarter)], zbuf.at[d],
            z_send.at[0, d], z_recv.at[0, d], device_id=place.chip(0, d), device_id_type=MESH))
        sends[-1].start()
    zbuf[0] = part[:, pl.ds(pl.multiple_of(z * quarter, quarter), quarter)]
    for send in sends:
        send.wait_recv()
    total = ((zbuf[0] + zbuf[1]) + (zbuf[2] + zbuf[3])) * (1.0 / N)
    zown[z] = total
    for t in range(3):
        raw[t, z, x, y, core] = total[t]
    for d in (1, 2, 3):
        sends.append(pltpu.make_async_remote_copy(
            zown.at[z], zown.at[z], z_send.at[1, d], z_recv.at[1, d],
            device_id=place.chip(0, d), device_id_type=MESH))
        sends[-1].start()
    rest = gather(place, raw, sems_raw, stepwise=True)
    next(rest)
    for d in (1, 2, 3):
        spot = zown.at[place.far(0, N - d)]
        pltpu.make_async_remote_copy(spot, spot, z_send.at[1, d], z_recv.at[1, d],
                                     device_id=place.chip(0, d), device_id_type=MESH).wait_recv()
    eye = (lax.broadcasted_iota(jnp.int32, (RANK, RANK), 0) == lax.broadcasted_iota(jnp.int32, (RANK, RANK), 1)).astype(F32)
    for t in range(3):
        h, m, l = [p.astype(F32) for p in split(zown[:, t].reshape(rows, RANK), 3)]
        none = jnp.zeros_like(h)
        pairs = [jnp.concatenate(pair, 1) for pair in ((h, l), (h, m), (h, none), (m, none))]
        stacked[t] = jnp.concatenate(pairs, 0).T.astype(BF16)

    half = RANK // 4

    def spot(t, j1, j2, whose, part=None):
        where = [slice(None)] * 3
        for p, j in ((1, j1), (2, j2)):
            where[axis_of(t, p)] = place.far(axis_of(t, p), OFF[j])
        return (t, *where, whose, slice(None) if part is None else pl.ds(part * half, half))

    def unit(t, j, part=None):
        where = list(place.at)
        where[axis_of(t, 0)] = place.far(axis_of(t, 0), OFF[j])
        return (t, *where, core, slice(None) if part is None else pl.ds(part * half, half))

    def swap(t, j1, j2):
        return pltpu.make_async_remote_copy(
            full.at[spot(t, j1, j2, 1 - core)], other.at[t, j1, j2], d_send.at[t, j1, j2], d_recv.at[t, j1, j2],
            device_id=place.sibling(), device_id_type=MESH)

    def hop(t, p, d, kind, j, src, dst):
        return pltpu.make_async_remote_copy(
            src, dst, s_send.at[t, p, kind, j, d], s_recv.at[t, p, kind, j, d],
            device_id=place.chip(axis_of(t, p), 1 if d == 0 else 3), device_id_type=MESH)

    def far_a(t, j, d):
        return hop(t, 2, d, 0, j, full.at[spot(t, j, 3, core, d)], ra0.at[t, d, j])

    def far_b(t, j, d):
        return hop(t, 2, d, 1, j, full.at[spot(t, j, d + 1, core)], rb0.at[t, d, j])

    def mid_a(t, d):
        return hop(t, 1, d, 0, 0, full.at[spot(t, 3, 0, core, d)], ra1.at[t, d])

    def mid_b(t, d):
        return hop(t, 1, d, 1, 0, full.at[spot(t, d + 1, 0, core)], rb1.at[t, d])

    def end_a(t, d):
        return hop(t, 0, d, 0, 0, full.at[unit(t, 3, d)], ra2.at[t, d])

    def end_b(t, d):
        return hop(t, 0, d, 1, 0, full.at[unit(t, d + 1)], rb2.at[t, d])

    def multiply(j1, j2):
        @pl.loop(0, 3)
        def _(t):
            where = [place.line(t, j1, j2, i) for i in range(N)]
            right = [parts[t, :, pl.ds(pl.multiple_of(((cz * N + cx) * N + cy) * RANK, RANK), RANK)] for cz, cx, cy in where]
            right = jnp.concatenate(right, 1)
            out = dot(stacked[t], jnp.concatenate([right, right[:rows]], 0))
            out = out[:RANK] + out[RANK:]
            for i, (cz, cx, cy) in enumerate(where):
                full[t, cz, cx, cy] = out[:, i * RANK:(i + 1) * RANK].reshape(2, RANK // 2, RANK)
        for t in range(3):
            swap(t, j1, j2).start()

    def settle(j1, j2):
        for t in range(3):
            swap(t, j1, j2).wait_recv()
            here = spot(t, j1, j2, core)
            full[here] = full[here] + other[t, j1, j2]
            if j2 == 3:
                for d in range(2):
                    far_a(t, j1, d).start()
            elif j2 > 0:
                d = j2 - 1
                far_a(t, j1, d).wait_recv()
                here = spot(t, j1, j2, core, d)
                full[here] = full[here] + ra0[t, d, j1]
                far_b(t, j1, d).start()

    lines = [(j1, j2) for j2 in (3, 2, 1, 0) for j1 in (3, 2, 1, 0)]
    for i, line in enumerate(lines):
        multiply(*line)
        if i:
            settle(*lines[i - 1])
        next(rest, None)
    settle(*lines[-1])
    for _ in rest:
        pass

    def ring_ends():
        for j in (3, 2, 1, 0):
            for t in range(3):
                here = spot(t, j, 0, core)
                for d in range(2):
                    far_b(t, j, d).wait_recv()
                full[here] = full[here] + (rb0[t, 0, j] + rb0[t, 1, j])
                if j == 3:
                    for d in range(2):
                        mid_a(t, d).start()
        yield
        for t in range(3):
            for d in range(2):
                mid_a(t, d).wait_recv()
                here = spot(t, d + 1, 0, core, d)
                full[here] = full[here] + ra1[t, d]
                mid_b(t, d).start()
        yield
        for t in range(3):
            here = spot(t, 0, 0, core)
            for d in range(2):
                mid_b(t, d).wait_recv()
            full[here] = full[here] + (rb1[t, 0] + rb1[t, 1])
            for d in range(2):
                end_a(t, d).start()
        yield
        for t in range(3):
            for d in range(2):
                end_a(t, d).wait_recv()
                here = unit(t, d + 1, d)
                full[here] = full[here] + ra2[t, d]
                end_b(t, d).start()
        yield
        for t in range(3):
            here = unit(t, 0)
            for d in range(2):
                end_b(t, d).wait_recv()
            pair[t, core] = full[here] + (rb2[t, 0] + rb2[t, 1])
        half_swap.start()
        yield

    half_swap = pltpu.make_async_remote_copy(
        pair.at[:, core], pair.at[:, core], x_send, x_recv, device_id=place.sibling(), device_id_type=MESH)

    def grams(inverse):
        if inverse:
            for t in range(3):
                h, m, l = split(mix[t].T, 3)
                wide[t] = jnp.concatenate([jnp.concatenate([h, m, l], 1), jnp.concatenate([m, h, h], 1)], 0)

        def add(i, grams):
            out = []
            for t in range(3):
                whole, low = grams[t]
                some = raw[t, i].reshape(512, RANK)
                h, m, l = split(some, 3)
                if inverse:
                    main = dot(jnp.concatenate([h, m], 1), wide[t, :, :2 * RANK])
                    rest = dot(jnp.concatenate([h, l], 1), wide[t, :, 2 * RANK:])
                    h, m, l = split(main[:, :RANK] + (main[:, RANK:] + rest), 3)
                all_ = dot(jnp.concatenate([h, m, l], 1), jnp.concatenate([h, m], 1), TN)
                tile = lambda i, j: all_[i * RANK:(i + 1) * RANK, j * RANK:(j + 1) * RANK]
                out.append((whole + (tile(0, 0) + ((tile(0, 1) + tile(1, 0)) + tile(1, 1))), low + tile(2, 0)))
            return tuple(out)

        zero = jnp.zeros((RANK, RANK), F32)
        for t, (whole, low) in enumerate(lax.fori_loop(0, N, add, ((zero, zero),) * 3)):
            both[t, :, :RANK] = whole + (low + low.T)
            both[t, :, RANK:] = eye

    grams(False)
    ends = ring_ends()
    for i in range(0, 8, 2):
        pl.loop(i, i + 2)(lambda i: factor_block(both, i))
        next(ends)
    for t in range(3):
        mix[t] = both[t, :, RANK:]
    grams(True)
    next(ends)
    pl.loop(0, 8)(lambda i: factor_block(both, i))
    for t in range(3):
        left = dot(zown[:, t].reshape(rows, RANK), mix[t], NT, HIGH)
        inv = both[t, :, RANK:]
        left_ref[t] = dot(left, inv, NT, HIGH)
        mix[t] = dot(inv, mix[t], precision=HIGH) * (1.0 / N)
    pltpu.make_async_remote_copy(
        pair.at[:, 1 - core], pair.at[:, 1 - core], x_send, x_recv, device_id=place.sibling(),
        device_id_type=MESH).wait_recv()
    half_swap.wait_send()
    term = qbuf
    mine = pl.ds(pl.multiple_of(core * (RANK // 2), RANK // 2), RANK // 2)
    for t in range(3):
        term[t, z, x, y, core] = dot(mix[t, mine, :], pair[t].reshape(RANK, RANK), precision=HIGH)
    ones = jnp.ones((8, RANK), F32)

    def keep(j1, j2):
        for t in range(3):
            where = [slice(None)] * 3
            for p, j in ((1, j1), (2, j2)):
                where[axis_of(t, p)] = place.far(axis_of(t, p), dyn_off(j))
            block = term[(t, *where)].reshape(N, RANK, RANK)
            block = block * block
            total = (block[0] + block[1]) + (block[2] + block[3])
            squares[t, where[axis_of(t, 1)], where[axis_of(t, 2)]] = dot(ones, total, NT, HIGH)

    for _ in gather(place, term, sems_term, keep):
        pass
    for t in range(3):
        total = jnp.sum(squares[t].reshape(N * N, 8, RANK), axis=0)
        scale_ref[t] = 1.0 / jnp.sqrt(total + 1e-6)
    for send in sends:
        send.wait_send()
    for t in range(3):
        for d in range(2):
            for j in range(N):
                far_a(t, j, d).wait_send()
                far_b(t, j, d).wait_send()
            for copy in (mid_a, mid_b, end_a, end_b):
                copy(t, d).wait_send()
        for j1, j2 in lines:
            swap(t, j1, j2).wait_send()


def last_kernel(gain, parts_ref, term_ref, left_ref, scale_ref, next_ref, update_ref, basis_ref):
    t, i = pl.program_id(0), pl.program_id(1)
    rows, span = update_ref.shape[1:]
    scale = scale_ref[t, 0:1, :]
    left = left_ref[t]
    high, low = split(jnp.concatenate([left * 0.05, left * (scale * gain)], 0), 2)
    lhs = jnp.concatenate([jnp.concatenate([high, high], 1), jnp.concatenate([low, jnp.zeros_like(low)], 1)], 0)
    chips = span // RANK
    for j in range(chips // N):
        line = i * (chips // N) + j
        block = term_ref[t, line // N, lax.rem(line, N)].reshape(N, RANK, RANK)
        high, low = split(jnp.concatenate([block[c] for c in range(N)], 1), 2)
        out = dot(lhs, jnp.concatenate([high, low], 0))
        out = out[:2 * rows] + out[2 * rows:]
        here = slice(j * N * RANK, (j + 1) * N * RANK)
        column = pl.multiple_of(line * (N * RANK), N * RANK)
        h, m, l = [parts_ref[t, k * rows:(k + 1) * rows, pl.ds(column, N * RANK)].astype(F32) for k in range(3)]
        next_ref[0, 0, :, here] = (h + (m + l)) - out[:rows]
        update_ref[0, :, here] = out[rows:]

    @pl.when(i == 0)
    def _():
        place = Place()
        z, x, y = place.at
        basis = term_ref[t, z, x, y].reshape(RANK, RANK).T * scale
        basis_ref[...] = jnp.where(place.core == 0, basis[:64], basis[64:])


def body(momentum, gradient, basis):
    momentum, gradient = momentum[0], gradient[0]
    count, rows, width = momentum.shape
    chips = (N, N, N, 2)
    dma = pltpu.SemaphoreType.DMA
    f32 = lambda *shape: jax.ShapeDtypeStruct(shape, F32)
    room = lambda *shape: pltpu.VMEM(shape, F32)
    kept = [pltpu.VMEM((count, 3 * rows, width), BF16), room(3, *chips, 64, RANK)]
    parts, term, left, scale = pl.pallas_call(
        main_kernel,
        name="dion",
        out_shape=kept + [room(3, rows, RANK), room(3, 8, RANK)],
        in_specs=[ANY] * 3,
        out_specs=[VMEM] * 4,
        scratch_shapes=[
            room(4, count, rows, 512), room(4, count, rows, 512),
            room(count, rows, RANK), room(N, 3, 16, RANK), room(N, 3, 16, RANK), room(3, *chips, 16, RANK),
            pltpu.VMEM((3, 2 * RANK, 4 * rows), BF16), room(3, RANK, 2 * RANK),
            room(3, *chips, 64, RANK), room(3, N, N, N, 64, RANK),
            room(3, 2, N, N, 32, RANK), room(3, 2, N, N, 64, RANK),
            room(3, 2, N, 32, RANK), room(3, 2, N, 64, RANK),
            room(3, 2, 32, RANK), room(3, 2, 64, RANK),
            room(3, 2, 64, RANK), room(3, RANK, RANK), room(3, N, N, 8, RANK),
            pltpu.VMEM((3, 2 * RANK, 3 * RANK), BF16),
            dma((3,)), dma((2, 4)), dma((2, 4)), dma((2, 4)),
            dma((3, N, N)), dma((3, N, N)), dma((3, 3, 2, N, 2)), dma((3, 3, 2, N, 2)), dma, dma] + gather_sems() * 3,
        compiler_params=pltpu.CompilerParams(collective_id=0, has_side_effects=True, vmem_limit_bytes=40 * 2 ** 20),
    )(momentum, gradient, basis)
    gain = float((2048 * 8192 / RANK) ** 0.5)
    span = 2048
    parts, term, left, scale = [pltpu.with_memory_space_constraint(a, pltpu.VMEM) for a in (parts, term, left, scale)]
    return pl.pallas_call(
        functools.partial(last_kernel, gain),
        name="outputs",
        grid=(3, width // span),
        out_shape=[f32(1, count, rows, width), f32(count, rows, width), f32(64, 3 * RANK)],
        in_specs=[VMEM] * 4,
        out_specs=[
            pl.BlockSpec((1, 1, rows, span), lambda t, i: (0, t, 0, i)),
            pl.BlockSpec((1, rows, span), lambda t, i: (t, 0, i)),
            pl.BlockSpec((64, RANK), lambda t, i: (0, t)),
        ],
        compiler_params=pltpu.CompilerParams(vmem_limit_bytes=16 * 2 ** 20),
    )(parts, term, left, scale)


def solution(mesh):
    placed = (P("rep", None, "fsdp", None), P("rep", None, "fsdp", None), P(("rep", "fsdp"), None))
    return jax.shard_map(
        body,
        mesh=mesh,
        in_specs=placed,
        out_specs=(P("rep", None, "fsdp", None), P(None, "fsdp", None), P(("rep", "fsdp"), None)),
        check_vma=False,
    )
```

```python
import functools

import jax
import jax.numpy as jnp
from jax import lax
from jax.experimental import pallas as pl
from jax.experimental.pallas import tpu as pltpu
from jax.sharding import PartitionSpec as P

MESH = pl.DeviceIdType.MESH
HIGH = lax.Precision.HIGHEST
F32 = jnp.float32
BF16 = jnp.bfloat16
RANK = 128
N = 4
OFF = (0, 1, 3, 2)
ANY = pl.BlockSpec(memory_space=pl.ANY)
VMEM = pl.BlockSpec(memory_space=pltpu.VMEM)


def axis_of(third, phase):
    return (2, 1, 0)[(third + phase) % 3]


class Place:
    def __init__(self):
        self.rep = lax.axis_index("rep")
        self.fsdp = lax.axis_index("fsdp")
        self.core = lax.rem(self.fsdp, 2)
        self.at = (self.rep, lax.div(self.fsdp, 8), lax.rem(lax.div(self.fsdp, 2), N))

    def far(self, axis, distance):
        if isinstance(distance, int) and distance == 0:
            return self.at[axis]
        return lax.rem(self.at[axis] + distance, N)

    def chip(self, axis, distance):
        at = list(self.at)
        at[axis] = self.far(axis, distance)
        return (at[0], (at[1] * N + at[2]) * 2 + self.core)

    def sibling(self):
        return (self.rep, self.fsdp + 1 - 2 * self.core)

    def line(self, third, j1, j2, i):
        off1, off2 = dyn_off(j1), dyn_off(j2)
        places = []
        for t in range(3):
            where = [None] * 3
            where[axis_of(t, 0)] = i
            where[axis_of(t, 1)] = self.far(axis_of(t, 1), off1)
            where[axis_of(t, 2)] = self.far(axis_of(t, 2), off2)
            places.append(where)
        return [jnp.where(third == 0, a, jnp.where(third == 1, b, c)) for a, b, c in zip(*places)]


def dyn_off(j):
    return OFF[j] if isinstance(j, int) else j + (j // 2) * (5 - 2 * j)


def greet(place, distances):
    barrier = pltpu.get_barrier_semaphore()
    peers = [place.sibling()] + [place.chip(axis, d) for axis, d in distances]
    for peer in peers:
        pl.semaphore_signal(barrier, inc=1, device_id=peer, device_id_type=MESH)
    pl.semaphore_wait(barrier, len(peers))


NEAR = [(axis, d) for axis in range(3) for d in (1, 3)]


def gather_sems():
    dma = pltpu.SemaphoreType.DMA
    return [dma((3, 3, 4, 2))] * 4 + [dma((3, 4, 4))] * 2


def gather(place, buf, sems, hook=None, stepwise=False):
    send_a, recv_a, send_b, recv_b, send_d, recv_d = sems
    core = place.core
    rows = buf.shape[5]
    half = rows // 2

    def index(t, p, j, da, part=None):
        where = [None] * 3
        for q in range(3):
            axis = axis_of(t, q)
            if q < p - 1:
                where[axis] = slice(None)
            elif q == p - 1:
                where[axis] = place.far(axis, dyn_off(j))
            elif q == p:
                where[axis] = place.far(axis, da)
            else:
                where[axis] = place.at[axis]
        span = slice(None) if part is None else pl.ds(part * half, half)
        return (t, *where, core, span)

    def copy_a(t, p, j, d, da):
        spot = buf.at[index(t, p, j, da)]
        return pltpu.make_async_remote_copy(
            spot, spot, send_a.at[t, p, j, d], recv_a.at[t, p, j, d],
            device_id=place.chip(axis_of(t, p), 1 if d == 0 else 3), device_id_type=MESH)

    def copy_b(t, p, j, d, da):
        spot = buf.at[index(t, p, j, da, d)]
        return pltpu.make_async_remote_copy(
            spot, spot, send_b.at[t, p, j, d], recv_b.at[t, p, j, d],
            device_id=place.chip(axis_of(t, p), 1 if d == 0 else 3), device_id_type=MESH)

    def copy_d(t, j1, j2, whose):
        where = [None] * 3
        where[axis_of(t, 0)] = slice(None)
        where[axis_of(t, 1)] = place.far(axis_of(t, 1), dyn_off(j1))
        where[axis_of(t, 2)] = place.far(axis_of(t, 2), dyn_off(j2))
        spot = buf.at[(t, *where, whose)]
        return pltpu.make_async_remote_copy(
            spot, spot, send_d.at[t, j1, j2], recv_d.at[t, j1, j2],
            device_id=place.sibling(), device_id_type=MESH)

    def start_a(t, p, j):
        for d in range(2):
            copy_a(t, p, j, d, 0).start()

    def land_a(t, p, j, d):
        copy_a(t, p, j, d, 3 if d == 0 else 1).wait_recv()
        copy_b(t, p, j, d, 3 if d == 0 else 1).start()

    def land_b(t, p, j):
        for d in range(2):
            copy_b(t, p, j, d, 2).wait_recv()

    def line_done(j1, j2):
        for t in range(3):
            copy_d(t, j1, j2, 1 - core).wait_recv()
        if hook is not None:
            hook(j1, j2)

    thirds = range(3)
    for t in thirds:
        start_a(t, 0, 0)
    for t in thirds:
        start_a(t, 1, 0)
    yield
    for d in range(2):
        for t in thirds:
            land_a(t, 0, 0, d)
            start_a(t, 1, 2 - d)
    yield
    for t in thirds:
        land_b(t, 0, 0)
        start_a(t, 1, 3)
    for t in thirds:
        start_a(t, 2, 0)
        copy_d(t, 0, 0, core).start()
    yield
    for j in range(4):
        for t in thirds:
            for d in range(2):
                land_a(t, 1, j, d)
        yield
    for j1 in (1, 2):
        for t in thirds:
            start_a(t, 2, j1)
            copy_d(t, j1, 0, core).start()
    for j in range(4):
        for t in thirds:
            land_b(t, 1, j)
    for t in thirds:
        start_a(t, 2, 3)
        copy_d(t, 3, 0, core).start()
    yield

    def near(j):
        for t in thirds:
            for d in range(2):
                land_a(t, 2, j, d)
                copy_d(t, j, 2 - d, core).start()
        line_done(j, 0)

    def opposite(j):
        for t in thirds:
            land_b(t, 2, j)
            copy_d(t, j, 3, core).start()
        line_done(j, 1)
        line_done(j, 2)
        if not isinstance(j, int):
            pl.when(j >= 1)(lambda: line_done(j - 1, 3))
        elif j >= 1:
            line_done(j - 1, 3)

    if stepwise:
        for step in (near, opposite):
            for j in range(4):
                step(j)
                yield
    else:
        pl.loop(0, 4)(near)
        pl.loop(0, 4)(opposite)
    line_done(3, 3)

    for t in thirds:
        for p in range(3):
            for j in range(1 if p == 0 else 4):
                for d in range(2):
                    copy_a(t, p, j, d, 0).wait_send()
                    copy_b(t, p, j, d, 3 if d == 0 else 1).wait_send()

    @pl.loop(0, 4)
    def _(j1):
        @pl.loop(0, 4)
        def _(j2):
            for t in thirds:
                copy_d(t, j1, j2, core).wait_send()


def split(values, parts):
    out = []
    for _ in range(parts):
        out.append(values.astype(BF16))
        values = values - out[-1].astype(F32)
    return out


def dot(left, right, dims=((1,), (0,)), precision=None):
    return lax.dot_general(left, right, (dims, ((), ())), precision=precision, preferred_element_type=F32)


NT = ((1,), (1,))
TN = ((0,), (0,))


def factor_block(both, step):
    count, size, _ = both.shape
    block, piece = 16, 8
    lane = lax.broadcasted_iota(jnp.int32, (count, block, size), 2)
    base = pl.multiple_of(step * block, block)
    band = both[:, pl.ds(base, block), :]
    upper, lower = band[:, :, :size], band[:, :, size:]
    inverses, done = [], []
    for part in range(block // piece):
        rows = block - part * piece
        shape = (count, rows, size)
        sub = lax.broadcasted_iota(jnp.int32, shape, 1)
        spread = lambda a, i: jnp.broadcast_to(a[:, i:i + 1, :], shape)
        turned = jnp.stack([pltpu.roll(upper[k], lax.rem(size - base, size), 1) for k in range(count)])
        columns = [jnp.broadcast_to(turned[:, :, part * piece + i:part * piece + i + 1], shape) for i in range(piece)]
        inverse = jnp.zeros((count, piece, size), F32)
        for i in range(piece):
            pivot = jnp.broadcast_to(columns[i][:, i:i + 1, :], (count, piece, size))
            recip = pl.reciprocal(pivot, approx=True)
            recip = recip * (2.0 - pivot * recip)
            recip = recip * (2.0 - pivot * recip)
            inverse = jnp.where(sub[:, :piece] == i, recip, inverse)
            factor = jnp.where(sub > i, columns[i] * jnp.concatenate([recip] * (rows // piece), 1), 0.0)
            for q in range(i + 1, piece):
                columns[q] = columns[q] - factor * spread(columns[q], i)
            upper = upper - factor * spread(upper, i)
            lower = lower - factor * spread(lower, i)
        inverses.append(inverse)
        done.append((upper[:, :piece], lower[:, :piece]))
        upper, lower = upper[:, piece:], lower[:, piece:]
    upper, lower = [jnp.concatenate(half, 1) for half in zip(*done)]
    inverse = jnp.concatenate(inverses, 1)
    factors = jnp.where(lane >= base + block, upper * inverse, 0.0)
    rows = jnp.concatenate([upper, lower], 2)
    less = []
    for k in range(count):
        h, m, l = split(factors[k], 3)
        first = jnp.concatenate([h, h, h, m, m, l], 0)
        h, m, l = split(rows[k], 3)
        less.append(dot(first, jnp.concatenate([h, m, l, h, m, h], 0), TN))
    for k in range(count):
        both[k] = both[k] - less[k]
    both[:, pl.ds(base, block), :] = jnp.concatenate([upper, lower * jnp.sqrt(inverse)], 2)


def main_kernel(gain, m_hbm, g_hbm, q_hbm, full, basis_ref, parts, qbuf, left_ref, lhs, norms,
                mbuf, gbuf, part, zbuf, zown, raw, stacked, both, other,
                ra0, rb0, ra1, rb1, ra2, rb2, pair, mix, wide,
                q_sem, load_sem, z_send, z_recv, d_send, d_recv, s_send, s_recv, x_send, x_recv, n_send, n_recv, *sems):
    place = Place()
    z, x, y = place.at
    core = place.core
    sems_q, sems_raw, sems_term = sems[:6], sems[6:12], sems[12:]
    count, stack_rows, width = parts.shape
    slots, _, rows, span = mbuf.shape
    chunks = width // span

    def columns(i):
        return pl.ds(pl.multiple_of(i * span, span), span)

    def load(i):
        slot = lax.rem(i, slots)
        return (pltpu.make_async_copy(m_hbm.at[:, :, columns(i)], mbuf.at[slot], load_sem.at[0, slot]),
                pltpu.make_async_copy(g_hbm.at[:, :, columns(i)], gbuf.at[slot], load_sem.at[1, slot]))

    def blend(first, last):
        @pl.loop(first, last)
        def _(i):
            slot = lax.rem(i, slots)
            for copy in load(i):
                copy.wait()
            for t in range(count):
                parts[t, :, columns(i)] = jnp.concatenate(split(mbuf[slot, t] + gbuf[slot, t], 3), 0)

            @pl.when(i + slots < chunks)
            def _():
                for copy in load(i + slots):
                    copy.start()

    loads = [pltpu.make_async_copy(q_hbm.at[:, pl.ds(t * RANK, RANK)], qbuf.at[t, z, x, y, core], q_sem.at[t])
             for t in range(3)]
    for copy in loads:
        copy.start()
    for i in range(slots):
        for copy in load(i):
            copy.start()
    greet(place, NEAR + [(0, 2), (1, 2), (2, 2)])
    for copy in loads:
        copy.wait()
    part[...] = jnp.zeros_like(part)

    def hook(j1, j2):
        @pl.loop(0, 3)
        def _(t):
            left, right = [], []
            for i in range(N):
                cz, cx, cy = place.line(t, j1, j2, i)
                column = pl.multiple_of(((cz * N + cx) * N + cy) * RANK, RANK)
                left.append(parts[t, :, pl.ds(column, RANK)])
                right.append(qbuf[t, cz, cx, cy].reshape(RANK, RANK))
            left = jnp.concatenate(left, 1)
            h, m, l = split(jnp.concatenate(right, 0), 3)
            out = dot(left, jnp.concatenate([h, m], 1))
            tile = lambda i, j: out[i * rows:(i + 1) * rows, j * RANK:(j + 1) * RANK]
            small = (tile(2, 0) + tile(1, 1)) + dot(left[:rows], l)
            part[t] += (small + (tile(1, 0) + tile(0, 1))) + tile(0, 0)

    done = 0
    for _ in gather(place, qbuf, sems_q, hook):
        if done < chunks:
            blend(done, min(done + 3, chunks))
            done += 3

    quarter = rows // N
    sends = []
    for d in (1, 2, 3):
        to = place.far(0, d)
        sends.append(pltpu.make_async_remote_copy(
            part.at[:, pl.ds(pl.multiple_of(to * quarter, quarter), quarter)], zbuf.at[d],
            z_send.at[0, d], z_recv.at[0, d], device_id=place.chip(0, d), device_id_type=MESH))
        sends[-1].start()
    zbuf[0] = part[:, pl.ds(pl.multiple_of(z * quarter, quarter), quarter)]
    for send in sends:
        send.wait_recv()
    total = ((zbuf[0] + zbuf[1]) + (zbuf[2] + zbuf[3])) * (1.0 / N)
    zown[z] = total
    for t in range(3):
        raw[t, z, x, y, core] = total[t]
    for d in (1, 2, 3):
        sends.append(pltpu.make_async_remote_copy(
            zown.at[z], zown.at[z], z_send.at[1, d], z_recv.at[1, d],
            device_id=place.chip(0, d), device_id_type=MESH))
        sends[-1].start()
    rest = gather(place, raw, sems_raw, stepwise=True)
    next(rest)
    for d in (1, 2, 3):
        spot = zown.at[place.far(0, N - d)]
        pltpu.make_async_remote_copy(spot, spot, z_send.at[1, d], z_recv.at[1, d],
                                     device_id=place.chip(0, d), device_id_type=MESH).wait_recv()
    eye = (lax.broadcasted_iota(jnp.int32, (RANK, RANK), 0) == lax.broadcasted_iota(jnp.int32, (RANK, RANK), 1)).astype(F32)
    for t in range(3):
        h, m, l = [p.astype(F32) for p in split(zown[:, t].reshape(rows, RANK), 3)]
        none = jnp.zeros_like(h)
        pairs = [jnp.concatenate(pair, 1) for pair in ((h, l), (h, m), (h, none), (m, none))]
        stacked[t] = jnp.concatenate(pairs, 0).T.astype(BF16)

    half = RANK // 4

    def spot(t, j1, j2, whose, part=None):
        where = [slice(None)] * 3
        for p, j in ((1, j1), (2, j2)):
            where[axis_of(t, p)] = place.far(axis_of(t, p), OFF[j])
        return (t, *where, whose, slice(None) if part is None else pl.ds(part * half, half))

    def unit(t, j, part=None):
        where = list(place.at)
        where[axis_of(t, 0)] = place.far(axis_of(t, 0), OFF[j])
        return (t, *where, core, slice(None) if part is None else pl.ds(part * half, half))

    def swap(t, j1, j2):
        return pltpu.make_async_remote_copy(
            full.at[spot(t, j1, j2, 1 - core)], other.at[t, j1, j2], d_send.at[t, j1, j2], d_recv.at[t, j1, j2],
            device_id=place.sibling(), device_id_type=MESH)

    def hop(t, p, d, kind, j, src, dst):
        return pltpu.make_async_remote_copy(
            src, dst, s_send.at[t, p, kind, j, d], s_recv.at[t, p, kind, j, d],
            device_id=place.chip(axis_of(t, p), 1 if d == 0 else 3), device_id_type=MESH)

    def far_a(t, j, d):
        return hop(t, 2, d, 0, j, full.at[spot(t, j, 3, core, d)], ra0.at[t, d, j])

    def far_b(t, j, d):
        return hop(t, 2, d, 1, j, full.at[spot(t, j, d + 1, core)], rb0.at[t, d, j])

    def mid_a(t, d):
        return hop(t, 1, d, 0, 0, full.at[spot(t, 3, 0, core, d)], ra1.at[t, d])

    def mid_b(t, d):
        return hop(t, 1, d, 1, 0, full.at[spot(t, d + 1, 0, core)], rb1.at[t, d])

    def end_a(t, d):
        return hop(t, 0, d, 0, 0, full.at[unit(t, 3, d)], ra2.at[t, d])

    def end_b(t, d):
        return hop(t, 0, d, 1, 0, full.at[unit(t, d + 1)], rb2.at[t, d])

    def multiply(j1, j2):
        @pl.loop(0, 3)
        def _(t):
            where = [place.line(t, j1, j2, i) for i in range(N)]
            right = [parts[t, :, pl.ds(pl.multiple_of(((cz * N + cx) * N + cy) * RANK, RANK), RANK)] for cz, cx, cy in where]
            right = jnp.concatenate(right, 1)
            out = dot(stacked[t], jnp.concatenate([right, right[:rows]], 0))
            out = out[:RANK] + out[RANK:]
            for i, (cz, cx, cy) in enumerate(where):
                full[t, cz, cx, cy] = out[:, i * RANK:(i + 1) * RANK].reshape(2, RANK // 2, RANK)
        for t in range(3):
            swap(t, j1, j2).start()

    def settle(j1, j2):
        for t in range(3):
            swap(t, j1, j2).wait_recv()
            here = spot(t, j1, j2, core)
            full[here] = full[here] + other[t, j1, j2]
            if j2 == 3:
                for d in range(2):
                    far_a(t, j1, d).start()
            elif j2 > 0:
                d = j2 - 1
                far_a(t, j1, d).wait_recv()
                here = spot(t, j1, j2, core, d)
                full[here] = full[here] + ra0[t, d, j1]
                far_b(t, j1, d).start()

    lines = [(j1, j2) for j2 in (3, 2, 1, 0) for j1 in (3, 2, 1, 0)]
    for i, line in enumerate(lines):
        multiply(*line)
        if i:
            settle(*lines[i - 1])
        next(rest, None)
    settle(*lines[-1])
    for _ in rest:
        pass

    def ring_ends():
        for j in (3, 2, 1, 0):
            for t in range(3):
                here = spot(t, j, 0, core)
                for d in range(2):
                    far_b(t, j, d).wait_recv()
                full[here] = full[here] + (rb0[t, 0, j] + rb0[t, 1, j])
                if j == 3:
                    for d in range(2):
                        mid_a(t, d).start()
        yield
        for t in range(3):
            for d in range(2):
                mid_a(t, d).wait_recv()
                here = spot(t, d + 1, 0, core, d)
                full[here] = full[here] + ra1[t, d]
                mid_b(t, d).start()
        yield
        for t in range(3):
            here = spot(t, 0, 0, core)
            for d in range(2):
                mid_b(t, d).wait_recv()
            full[here] = full[here] + (rb1[t, 0] + rb1[t, 1])
            for d in range(2):
                end_a(t, d).start()
        yield
        for t in range(3):
            for d in range(2):
                end_a(t, d).wait_recv()
                here = unit(t, d + 1, d)
                full[here] = full[here] + ra2[t, d]
                end_b(t, d).start()
        yield
        for t in range(3):
            here = unit(t, 0)
            for d in range(2):
                end_b(t, d).wait_recv()
            pair[t, core] = full[here] + (rb2[t, 0] + rb2[t, 1])
        half_swap.start()
        yield

    half_swap = pltpu.make_async_remote_copy(
        pair.at[:, core], pair.at[:, core], x_send, x_recv, device_id=place.sibling(), device_id_type=MESH)

    def grams(inverse):
        if inverse:
            for t in range(3):
                h, m, l = split(mix[t].T, 3)
                wide[t] = jnp.concatenate([jnp.concatenate([h, m, l], 1), jnp.concatenate([m, h, h], 1)], 0)

        def add(i, grams):
            out = []
            for t in range(3):
                whole, low = grams[t]
                some = raw[t, i].reshape(512, RANK)
                if inverse:
                    h, m, l = split(some, 3)
                    main = dot(jnp.concatenate([h, m], 1), wide[t, :, :2 * RANK])
                    rest = dot(jnp.concatenate([h, l], 1), wide[t, :, 2 * RANK:])
                    some = main[:, :RANK] + (main[:, RANK:] + rest)
                all_ = dot(jnp.concatenate(split(some.T, 3), 0), jnp.concatenate(split(some, 2), 1))
                tile = lambda i, j: all_[i * RANK:(i + 1) * RANK, j * RANK:(j + 1) * RANK]
                out.append((whole + (tile(0, 0) + ((tile(0, 1) + tile(1, 0)) + tile(1, 1))), low + tile(2, 0)))
            return tuple(out)

        zero = jnp.zeros((RANK, RANK), F32)
        for t, (whole, low) in enumerate(lax.fori_loop(0, N, add, ((zero, zero),) * 3)):
            both[t, :, :RANK] = whole + (low + low.T)
            both[t, :, RANK:] = eye

    grams(False)
    ends = ring_ends()
    for i in range(0, 8, 2):
        pl.loop(i, i + 2)(lambda i: factor_block(both, i))
        next(ends)
    for t in range(3):
        mix[t] = both[t, :, RANK:]
    grams(True)
    next(ends)
    pl.loop(0, 8)(lambda i: factor_block(both, i))
    for t in range(3):
        left = dot(zown[:, t].reshape(rows, RANK), mix[t], NT, HIGH)
        inv = both[t, :, RANK:]
        left_ref[t] = dot(left, inv, NT, HIGH)
        mix[t] = dot(inv, mix[t], precision=HIGH) * (1.0 / N)
    pltpu.make_async_remote_copy(
        pair.at[:, 1 - core], pair.at[:, 1 - core], x_send, x_recv, device_id=place.sibling(),
        device_id_type=MESH).wait_recv()
    half_swap.wait_send()
    for send in sends:
        send.wait_send()
    for t in range(3):
        for d in range(2):
            for j in range(N):
                far_a(t, j, d).wait_send()
                far_b(t, j, d).wait_send()
            for copy in (mid_a, mid_b, end_a, end_b):
                copy(t, d).wait_send()
        for j1, j2 in lines:
            swap(t, j1, j2).wait_send()

    term = qbuf
    mine = pl.ds(pl.multiple_of(core * (RANK // 2), RANK // 2), RANK // 2)
    ones = jnp.ones((8, RANK), F32)
    own = lax.broadcasted_iota(jnp.int32, (RANK, RANK), 0) // (RANK // 2) == core
    for t in range(3):
        whole = dot(mix[t], pair[t].reshape(RANK, RANK), precision=HIGH)
        pair[t] = whole.reshape(2, RANK // 2, RANK)
        term[t, z, x, y, core] = pair[t, core]
        norms[0, core, t] = dot(ones, jnp.where(own, whole * whole, 0.0), NT, HIGH)

    def tell(stage, where, peer, sem):
        return pltpu.make_async_remote_copy(norms.at[stage, where], norms.at[stage, where], n_send.at[stage, sem],
                                            n_recv.at[stage, sem], device_id=peer, device_id_type=MESH)

    def sum_norms():
        tell(0, core, place.sibling(), 0).start()
        yield
        tell(0, 1 - core, place.sibling(), 0).wait_recv()
        total = norms[0, 0] + norms[0, 1]
        for axis in range(3):
            stage = 1 + axis
            here = place.at[axis]
            norms[stage, here] = total
            for d in (1, 2, 3):
                tell(stage, here, place.chip(axis, d), d).start()
            yield
            for d in (1, 2, 3):
                tell(stage, place.far(axis, N - d), place.chip(axis, d), d).wait_recv()
            total = (norms[stage, 0] + norms[stage, 1]) + (norms[stage, 2] + norms[stage, 3])
        scales = 1.0 / jnp.sqrt(total + 1e-6)
        for t in range(3):
            scale = scales[t, 0:1]
            left = left_ref[t]
            high, low = split(jnp.concatenate([left * 0.05, left * (scale * gain)], 0), 2)
            lhs[t] = jnp.concatenate(
                [jnp.concatenate([high, high], 1), jnp.concatenate([low, jnp.zeros_like(low)], 1)], 0)
            basis = pair[t].reshape(RANK, RANK).T * scale
            basis_ref[:, t * RANK:(t + 1) * RANK] = jnp.where(core == 0, basis[:RANK // 2], basis[RANK // 2:])
        tell(0, core, place.sibling(), 0).wait_send()
        for axis in range(3):
            for d in (1, 2, 3):
                tell(1 + axis, place.at[axis], place.chip(axis, d), d).wait_send()
        yield

    def emit(j1, j2):
        @pl.loop(0, 3)
        def _(t):
            where = [place.line(t, j1, j2, i) for i in range(N)]
            block = jnp.concatenate([term[t, cz, cx, cy].reshape(RANK, RANK) for cz, cx, cy in where], 1)
            out = dot(lhs[t], jnp.concatenate(split(block, 2), 0))
            out = out[:RANK] + out[RANK:]
            for i, (cz, cx, cy) in enumerate(where):
                column = pl.ds(pl.multiple_of(((cz * N + cx) * N + cy) * RANK, RANK), RANK)
                tile = slice(i * RANK, (i + 1) * RANK)
                h, m, l = [parts[t, k * rows:(k + 1) * rows, column].astype(F32) for k in range(3)]
                full[t, cz, cx, cy, 0] = (h + (m + l)) - out[:rows, tile]
                full[t, cz, cx, cy, 1] = out[rows:, tile]

    norm_steps = sum_norms()
    next(norm_steps)
    for _ in gather(place, term, sems_term, emit):
        next(norm_steps, None)


def last_kernel(both_ref, basis_in, next_ref, update_ref, basis_ref):
    t, i = pl.program_id(0), pl.program_id(1)
    count = update_ref.shape[2] // RANK
    for j in range(count):
        chip = i * count + j
        where = (t, chip // (N * N), lax.rem(chip // N, N), lax.rem(chip, N))
        next_ref[0, 0, :, j * RANK:(j + 1) * RANK] = both_ref[(*where, 0)]
        update_ref[0, :, j * RANK:(j + 1) * RANK] = both_ref[(*where, 1)]
    basis_ref[...] = basis_in[...]


def body(momentum, gradient, basis):
    momentum, gradient = momentum[0], gradient[0]
    count, rows, width = momentum.shape
    chips = (N, N, N, 2)
    dma = pltpu.SemaphoreType.DMA
    f32 = lambda *shape: jax.ShapeDtypeStruct(shape, F32)
    room = lambda *shape: pltpu.VMEM(shape, F32)
    gain = float((2048 * 8192 / RANK) ** 0.5)
    full, basis_next = pl.pallas_call(
        functools.partial(main_kernel, gain),
        name="dion",
        out_shape=[room(3, *chips, 64, RANK), room(64, 3 * RANK)],
        in_specs=[ANY] * 3,
        out_specs=[VMEM] * 2,
        scratch_shapes=[
            pltpu.VMEM((count, 3 * rows, width), BF16), room(3, *chips, 64, RANK), room(3, rows, RANK),
            pltpu.VMEM((3, 2 * RANK, 2 * RANK), BF16), room(4, N, 3, 8, RANK),
            room(4, count, rows, 512), room(4, count, rows, 512),
            room(count, rows, RANK), room(N, 3, 16, RANK), room(N, 3, 16, RANK), room(3, *chips, 16, RANK),
            pltpu.VMEM((3, 2 * RANK, 4 * rows), BF16), room(3, RANK, 2 * RANK),
            room(3, N, N, N, 64, RANK),
            room(3, 2, N, N, 32, RANK), room(3, 2, N, N, 64, RANK),
            room(3, 2, N, 32, RANK), room(3, 2, N, 64, RANK),
            room(3, 2, 32, RANK), room(3, 2, 64, RANK),
            room(3, 2, 64, RANK), room(3, RANK, RANK),
            pltpu.VMEM((3, 2 * RANK, 3 * RANK), BF16),
            dma((3,)), dma((2, 4)), dma((2, 4)), dma((2, 4)),
            dma((3, N, N)), dma((3, N, N)), dma((3, 3, 2, N, 2)), dma((3, 3, 2, N, 2)), dma, dma, dma((4, 4)), dma((4, 4))] + gather_sems() * 3,
        compiler_params=pltpu.CompilerParams(collective_id=0, has_side_effects=True, vmem_limit_bytes=49 * 2 ** 20),
    )(momentum, gradient, basis)
    span = 2048
    full, basis_next = [pltpu.with_memory_space_constraint(a, pltpu.VMEM) for a in (full, basis_next)]
    return pl.pallas_call(
        last_kernel,
        name="outputs",
        grid=(3, width // span),
        out_shape=[f32(1, count, rows, width), f32(count, rows, width), f32(64, 3 * RANK)],
        in_specs=[VMEM] * 2,
        out_specs=[
            pl.BlockSpec((1, 1, rows, span), lambda t, i: (0, t, 0, i)),
            pl.BlockSpec((1, rows, span), lambda t, i: (t, 0, i)),
            pl.BlockSpec((64, 3 * RANK), lambda t, i: (0, 0)),
        ],
        compiler_params=pltpu.CompilerParams(vmem_limit_bytes=16 * 2 ** 20),
    )(full, basis_next)


def solution(mesh):
    placed = (P("rep", None, "fsdp", None), P("rep", None, "fsdp", None), P(("rep", "fsdp"), None))
    return jax.shard_map(
        body,
        mesh=mesh,
        in_specs=placed,
        out_specs=(P("rep", None, "fsdp", None), P(None, "fsdp", None), P(("rep", "fsdp"), None)),
        check_vma=False,
    )
```

```python
import functools

import jax
import jax.numpy as jnp
from jax import lax
from jax.experimental import pallas as pl
from jax.experimental.pallas import tpu as pltpu
from jax.sharding import PartitionSpec as P

MESH = pl.DeviceIdType.MESH
HIGH = lax.Precision.HIGHEST
F32 = jnp.float32
BF16 = jnp.bfloat16
RANK = 128
N = 4
ANY = pl.BlockSpec(memory_space=pl.ANY)
VMEM = pl.BlockSpec(memory_space=pltpu.VMEM)


def axis_of(third, phase):
    return (2, 1, 0)[(third + phase) % 3]


class Place:
    def __init__(self):
        self.rep = lax.axis_index("rep")
        self.fsdp = lax.axis_index("fsdp")
        self.core = lax.rem(self.fsdp, 2)
        self.at = (self.rep, lax.div(self.fsdp, 8), lax.rem(lax.div(self.fsdp, 2), N))

    def far(self, axis, distance):
        if isinstance(distance, int) and distance == 0:
            return self.at[axis]
        return lax.rem(self.at[axis] + distance, N)

    def chip(self, axis, distance):
        at = list(self.at)
        at[axis] = self.far(axis, distance)
        return (at[0], (at[1] * N + at[2]) * 2 + self.core)

    def sibling(self):
        return (self.rep, self.fsdp + 1 - 2 * self.core)

    def chips(self, t, j1, j2):
        where = [None] * 3
        where[axis_of(t, 1)] = self.far(axis_of(t, 1), dyn_off(j1))
        where[axis_of(t, 2)] = self.far(axis_of(t, 2), dyn_off(j2))
        out = []
        for i in range(N):
            where[axis_of(t, 0)] = i
            out.append(tuple(where))
        return out

    def line(self, third, middle, distance, i):
        places = []
        for t in range(3):
            where = [None] * 3
            where[axis_of(t, 0)] = i
            where[axis_of(t, 1)] = middle
            where[axis_of(t, 2)] = self.far(axis_of(t, 2), distance)
            places.append(where)
        return [jnp.where(third == 0, a, jnp.where(third == 1, b, c)) for a, b, c in zip(*places)]


def dyn_off(j):
    return OFF[j] if isinstance(j, int) else j + (j // 2) * (5 - 2 * j)


def greet(place, distances):
    barrier = pltpu.get_barrier_semaphore()
    peers = [place.sibling()] + [place.chip(axis, d) for axis, d in distances]
    for peer in peers:
        pl.semaphore_signal(barrier, inc=1, device_id=peer, device_id_type=MESH)
    pl.semaphore_wait(barrier, len(peers))


OFF = (0, 1, 3, 2)
NEAR = [(axis, d) for axis in range(3) for d in (1, 3)]


def await_landed(place, spot, sem):
    pltpu.make_async_remote_copy(spot, spot, sem, sem, device_id=place.sibling(), device_id_type=MESH).wait_recv()


def await_sent(place, spot, sem):
    pltpu.make_async_remote_copy(spot, spot, sem, sem, device_id=place.sibling(), device_id_type=MESH).wait_send()


def gather_sems():
    dma = pltpu.SemaphoreType.DMA
    return [dma((3,)), dma((3, 4)), dma((3, 2)), dma, dma((7,))]


def gather(place, buf, sems, hook=None):
    sent, recv_a, recv_b, sent_d, recv_d = sems
    core = place.core
    half = buf.shape[5] // 2
    thirds = range(3)

    def spot(t, p, distance, whose, part=None, middle=slice(None)):
        where = [None] * 3
        for q in range(3):
            axis = axis_of(t, q)
            if q < p:
                where[axis] = middle if q == 1 else slice(None)
            elif q == p:
                where[axis] = place.far(axis, distance)
            else:
                where[axis] = place.at[axis]
        return buf.at[(t, *where, whose, slice(None) if part is None else pl.ds(part * half, half))]

    def send(t, p, d, block, sem):
        pltpu.make_async_remote_copy(
            block, block, sent.at[p], sem,
            device_id=place.chip(axis_of(t, p), 1 if d == 0 else 3), device_id_type=MESH).start()

    def share(block, n):
        pltpu.make_async_remote_copy(
            block, block, sent_d, recv_d.at[n], device_id=place.sibling(), device_id_type=MESH).start()

    def size(p, whose, pieces=N):
        if p == 0:
            return buf.at[:, 0, 0, 0, whose]
        if p == 1:
            return buf.at[:, 0, 0, :, whose]
        return buf.at[:, 0, pl.ds(0, pieces), :, whose]

    came = (3, 1)
    for p in (0, 1):
        for t in thirds:
            for d in range(2):
                send(t, p, d, spot(t, p, 0, core), recv_a.at[p, d])
        yield
        for d in range(2):
            await_landed(place, size(p, core), recv_a.at[p, d])
            for t in thirds:
                send(t, p, d, spot(t, p, came[d], core, d), recv_b.at[p, 0])
        yield
        await_landed(place, size(p, core), recv_b.at[p, 0])
    run = hook if hook is not None else lambda *_: None
    piece = lambda c: pl.ds(2 * c, 2)
    for c in range(2):
        for t in thirds:
            for d in range(2):
                send(t, 2, d, spot(t, 2, 0, core, None, piece(c)), recv_a.at[2, 2 * c + d])
    for t in thirds:
        share(spot(t, 2, 0, core), 0)
    yield
    await_landed(place, size(2, 1 - core), recv_d.at[0])
    run(0, 0, N)
    for c in range(2):
        for d in range(2):
            await_landed(place, size(2, core, 2), recv_a.at[2, 2 * c + d])
            for t in thirds:
                send(t, 2, d, spot(t, 2, came[d], core, d, piece(c)), recv_b.at[2, c])
        for d in range(2):
            for t in thirds:
                share(spot(t, 2, came[d], core, None, piece(c)), 1 + 2 * c + d)
        yield
        if c == 0:
            for d in range(2):
                await_landed(place, size(2, 1 - core, 2), recv_d.at[1 + d])
                run(came[d], 0, 2)
    for c in range(2):
        await_landed(place, size(2, core, 2), recv_b.at[2, c])
        for t in thirds:
            share(spot(t, 2, 2, core, None, piece(c)), 5 + c)
        await_landed(place, size(2, 1 - core, 2), recv_d.at[3 + c])
        run(came[c], 2, 2)
    for c in range(2):
        await_landed(place, size(2, 1 - core, 2), recv_d.at[5 + c])
        run(2, 2 * c, 2)
    await_sent(place, buf.at[:, 0, 0, pl.ds(0, 3), core], sent.at[0])
    await_sent(place, buf.at[:, 0, pl.ds(0, 3), :, core], sent.at[1])
    await_sent(place, buf.at[:, pl.ds(0, 3), :, :, core], sent.at[2])
    await_sent(place, buf.at[:, :, :, :, core], sent_d)


def fine_sems():
    dma = pltpu.SemaphoreType.DMA
    return [dma((3, 3, 4, 2))] * 4 + [dma((3, 4, 4))] * 2


def fine_gather(place, buf, sems, hook):
    send_a, recv_a, send_b, recv_b, send_d, recv_d = sems
    core = place.core
    rows = buf.shape[5]
    half = rows // 2

    def index(t, p, j, da, part=None):
        where = [None] * 3
        for q in range(3):
            axis = axis_of(t, q)
            if q < p - 1:
                where[axis] = slice(None)
            elif q == p - 1:
                where[axis] = place.far(axis, dyn_off(j))
            elif q == p:
                where[axis] = place.far(axis, da)
            else:
                where[axis] = place.at[axis]
        span = slice(None) if part is None else pl.ds(part * half, half)
        return (t, *where, core, span)

    def copy_a(t, p, j, d, da):
        spot = buf.at[index(t, p, j, da)]
        return pltpu.make_async_remote_copy(
            spot, spot, send_a.at[t, p, j, d], recv_a.at[t, p, j, d],
            device_id=place.chip(axis_of(t, p), 1 if d == 0 else 3), device_id_type=MESH)

    def copy_b(t, p, j, d, da):
        spot = buf.at[index(t, p, j, da, d)]
        return pltpu.make_async_remote_copy(
            spot, spot, send_b.at[t, p, j, d], recv_b.at[t, p, j, d],
            device_id=place.chip(axis_of(t, p), 1 if d == 0 else 3), device_id_type=MESH)

    def copy_d(t, j1, j2, whose):
        where = [None] * 3
        where[axis_of(t, 0)] = slice(None)
        where[axis_of(t, 1)] = place.far(axis_of(t, 1), dyn_off(j1))
        where[axis_of(t, 2)] = place.far(axis_of(t, 2), dyn_off(j2))
        spot = buf.at[(t, *where, whose)]
        return pltpu.make_async_remote_copy(
            spot, spot, send_d.at[t, j1, j2], recv_d.at[t, j1, j2],
            device_id=place.sibling(), device_id_type=MESH)

    def start_a(t, p, j):
        for d in range(2):
            copy_a(t, p, j, d, 0).start()

    def land_a(t, p, j, d):
        copy_a(t, p, j, d, 3 if d == 0 else 1).wait_recv()
        copy_b(t, p, j, d, 3 if d == 0 else 1).start()

    def land_b(t, p, j):
        for d in range(2):
            copy_b(t, p, j, d, 2).wait_recv()

    def line_done(j1, j2):
        for t in range(3):
            copy_d(t, j1, j2, 1 - core).wait_recv()
        hook(j1, j2)

    thirds = range(3)
    for t in thirds:
        start_a(t, 0, 0)
    for t in thirds:
        start_a(t, 1, 0)
    yield
    for d in range(2):
        for t in thirds:
            land_a(t, 0, 0, d)
            start_a(t, 1, 2 - d)
    yield
    for t in thirds:
        land_b(t, 0, 0)
        start_a(t, 1, 3)
    for t in thirds:
        start_a(t, 2, 0)
        copy_d(t, 0, 0, core).start()
    yield
    for j in range(4):
        for t in thirds:
            for d in range(2):
                land_a(t, 1, j, d)
        yield
    for j1 in (1, 2):
        for t in thirds:
            start_a(t, 2, j1)
            copy_d(t, j1, 0, core).start()
    for j in range(4):
        for t in thirds:
            land_b(t, 1, j)
    for t in thirds:
        start_a(t, 2, 3)
        copy_d(t, 3, 0, core).start()
    yield

    @pl.loop(0, 4)
    def _(j):
        for t in thirds:
            for d in range(2):
                land_a(t, 2, j, d)
                copy_d(t, j, 2 - d, core).start()
        line_done(j, 0)

        @pl.when(j >= 1)
        def _():
            line_done(j - 1, 1)
            line_done(j - 1, 2)

    line_done(3, 1)
    line_done(3, 2)

    @pl.loop(0, 4)
    def _(j):
        for t in thirds:
            land_b(t, 2, j)
            copy_d(t, j, 3, core).start()
        pl.when(j >= 1)(lambda: line_done(j - 1, 3))

    line_done(3, 3)
    for t in thirds:
        for p in range(3):
            for j in range(1 if p == 0 else 4):
                for d in range(2):
                    copy_a(t, p, j, d, 0).wait_send()
                    copy_b(t, p, j, d, 3 if d == 0 else 1).wait_send()

    @pl.loop(0, 4)
    def _(j1):
        @pl.loop(0, 4)
        def _(j2):
            for t in thirds:
                copy_d(t, j1, j2, core).wait_send()


def split(values, parts):
    out = []
    for _ in range(parts):
        out.append(values.astype(BF16))
        values = values - out[-1].astype(F32)
    return out


def dot(left, right, dims=((1,), (0,)), precision=None):
    return lax.dot_general(left, right, (dims, ((), ())), precision=precision, preferred_element_type=F32)


NT = ((1,), (1,))
TN = ((0,), (0,))


def factor_block(both, step):
    count, size, _ = both.shape
    block, piece = 16, 8
    lane = lax.broadcasted_iota(jnp.int32, (count, block, size), 2)
    base = pl.multiple_of(step * block, block)
    band = both[:, pl.ds(base, block), :]
    upper, lower = band[:, :, :size], band[:, :, size:]
    inverses, done = [], []
    for part in range(block // piece):
        rows = block - part * piece
        shape = (count, rows, size)
        sub = lax.broadcasted_iota(jnp.int32, shape, 1)
        spread = lambda a, i: jnp.broadcast_to(a[:, i:i + 1, :], shape)
        turned = jnp.stack([pltpu.roll(upper[k], lax.rem(size - base, size), 1) for k in range(count)])
        columns = [jnp.broadcast_to(turned[:, :, part * piece + i:part * piece + i + 1], shape) for i in range(piece)]
        inverse = jnp.zeros((count, piece, size), F32)
        for i in range(piece):
            pivot = jnp.broadcast_to(columns[i][:, i:i + 1, :], (count, piece, size))
            recip = pl.reciprocal(pivot, approx=True)
            recip = recip * (2.0 - pivot * recip)
            recip = recip * (2.0 - pivot * recip)
            inverse = jnp.where(sub[:, :piece] == i, recip, inverse)
            factor = jnp.where(sub > i, columns[i] * jnp.concatenate([recip] * (rows // piece), 1), 0.0)
            for q in range(i + 1, piece):
                columns[q] = columns[q] - factor * spread(columns[q], i)
            upper = upper - factor * spread(upper, i)
            lower = lower - factor * spread(lower, i)
        inverses.append(inverse)
        done.append((upper[:, :piece], lower[:, :piece]))
        upper, lower = upper[:, piece:], lower[:, piece:]
    upper, lower = [jnp.concatenate(half, 1) for half in zip(*done)]
    inverse = jnp.concatenate(inverses, 1)
    factors = jnp.where(lane >= base + block, upper * inverse, 0.0)
    rows = jnp.concatenate([upper, lower], 2)
    less = []
    for k in range(count):
        h, m, l = split(factors[k], 3)
        first = jnp.concatenate([h, h, h, m, m, l], 0)
        h, m, l = split(rows[k], 3)
        less.append(dot(first, jnp.concatenate([h, m, l, h, m, h], 0), TN))
    for k in range(count):
        both[k] = both[k] - less[k]
    both[:, pl.ds(base, block), :] = jnp.concatenate([upper, lower * jnp.sqrt(inverse)], 2)


def main_kernel(gain, m_hbm, g_hbm, q_hbm, full, basis_ref, parts, qbuf, left_ref, lhs, norms,
                mbuf, gbuf, part, zbuf, zown, raw, stacked, both, other,
                ra0, rb0, ra1, rb1, ra2, rb2, pair, held, mix, wide,
                q_sem, load_sem, z_send, z_recv, d_send, d_recv, s_send, s_recv, x_send, x_recv, n_send, n_recv, *sems):
    place = Place()
    z, x, y = place.at
    core = place.core
    sems_q, sems_raw, sems_term = sems[:6], sems[6:11], sems[11:]
    count, stack_rows, width = parts.shape
    slots, _, rows, span = mbuf.shape
    chunks = width // span

    def columns(i):
        return pl.ds(pl.multiple_of(i * span, span), span)

    def load(i):
        slot = lax.rem(i, slots)
        return (pltpu.make_async_copy(m_hbm.at[:, :, columns(i)], mbuf.at[slot], load_sem.at[0, slot]),
                pltpu.make_async_copy(g_hbm.at[:, :, columns(i)], gbuf.at[slot], load_sem.at[1, slot]))

    def blend(first, last):
        @pl.loop(first, last)
        def _(i):
            slot = lax.rem(i, slots)
            for copy in load(i):
                copy.wait()
            for t in range(count):
                parts[t, :, columns(i)] = jnp.concatenate(split(mbuf[slot, t] + gbuf[slot, t], 3), 0)

            @pl.when(i + slots < chunks)
            def _():
                for copy in load(i + slots):
                    copy.start()

    loads = [pltpu.make_async_copy(q_hbm.at[:, pl.ds(t * RANK, RANK)], qbuf.at[t, z, x, y, core], q_sem.at[t])
             for t in range(3)]
    for copy in loads:
        copy.start()
    for i in range(slots):
        for copy in load(i):
            copy.start()
    greet(place, NEAR + [(0, 2), (1, 2), (2, 2)])
    for copy in loads:
        copy.wait()
    part[...] = jnp.zeros_like(part)

    def hook(j1, j2):
        for t in range(3):
            left, right = [], []
            for cz, cx, cy in place.chips(t, j1, j2):
                column = pl.multiple_of(((cz * N + cx) * N + cy) * RANK, RANK)
                left.append(parts[t, :, pl.ds(column, RANK)])
                right.append(qbuf[t, cz, cx, cy].reshape(RANK, RANK))
            left = jnp.concatenate(left, 1)
            h, m, l = split(jnp.concatenate(right, 0), 3)
            out = dot(left, jnp.concatenate([h, m], 1))
            tile = lambda i, j: out[i * rows:(i + 1) * rows, j * RANK:(j + 1) * RANK]
            small = (tile(2, 0) + tile(1, 1)) + dot(left[:rows], l)
            part[t] += (small + (tile(1, 0) + tile(0, 1))) + tile(0, 0)

    done = 0
    for _ in fine_gather(place, qbuf, sems_q, hook):
        if done < chunks:
            blend(done, min(done + 4, chunks))
            done += 4

    quarter = rows // N
    sends = []
    for d in (1, 2, 3):
        to = place.far(0, d)
        sends.append(pltpu.make_async_remote_copy(
            part.at[:, pl.ds(pl.multiple_of(to * quarter, quarter), quarter)], zbuf.at[d],
            z_send.at[0, d], z_recv.at[0, d], device_id=place.chip(0, d), device_id_type=MESH))
        sends[-1].start()
    zbuf[0] = part[:, pl.ds(pl.multiple_of(z * quarter, quarter), quarter)]
    for send in sends:
        send.wait_recv()
    total = ((zbuf[0] + zbuf[1]) + (zbuf[2] + zbuf[3])) * (1.0 / N)
    zown[z] = total
    for t in range(3):
        raw[t, z, x, y, core] = total[t]
    for d in (1, 2, 3):
        sends.append(pltpu.make_async_remote_copy(
            zown.at[z], zown.at[z], z_send.at[1, d], z_recv.at[1, d],
            device_id=place.chip(0, d), device_id_type=MESH))
        sends[-1].start()
    rest = gather(place, raw, sems_raw)
    next(rest)
    for d in (1, 2, 3):
        spot = zown.at[place.far(0, N - d)]
        pltpu.make_async_remote_copy(spot, spot, z_send.at[1, d], z_recv.at[1, d],
                                     device_id=place.chip(0, d), device_id_type=MESH).wait_recv()
    eye = (lax.broadcasted_iota(jnp.int32, (RANK, RANK), 0) == lax.broadcasted_iota(jnp.int32, (RANK, RANK), 1)).astype(F32)
    for t in range(3):
        h, m, l = [p.astype(F32) for p in split(zown[:, t].reshape(rows, RANK), 3)]
        none = jnp.zeros_like(h)
        pairs = [jnp.concatenate(pair, 1) for pair in ((h, l), (h, m), (h, none), (m, none))]
        stacked[t] = jnp.concatenate(pairs, 0).T.astype(BF16)

    half = RANK // 4

    def plane(t, distance, whose, part=None):
        where = [slice(None)] * 3
        where[axis_of(t, 2)] = place.far(axis_of(t, 2), distance)
        return (t, *where, whose, slice(None) if part is None else pl.ds(part * half, half))

    def line(t, distance, part=None):
        where = list(place.at)
        where[axis_of(t, 0)] = slice(None)
        where[axis_of(t, 1)] = place.far(axis_of(t, 1), distance)
        return (t, *where, core, slice(None) if part is None else pl.ds(part * half, half))

    def unit(t, distance, part=None):
        where = list(place.at)
        where[axis_of(t, 0)] = place.far(axis_of(t, 0), distance)
        return (t, *where, core, slice(None) if part is None else pl.ds(part * half, half))

    spots = (plane, line, unit)
    went = (1, 3)
    first, whole = (ra0, ra1, ra2), (rb0, rb1, rb2)

    def swap(t, n, distance):
        where = plane(t, distance, 1 - core)
        pltpu.make_async_remote_copy(
            full.at[where], other.at[where[:4]], d_send, d_recv.at[n],
            device_id=place.sibling(), device_id_type=MESH).start()

    def block(t, step, distance, part=None):
        return plane(t, distance, core, part) if step == 0 else spots[step](t, distance, part)

    def start(step, kind, d):
        for t in range(3):
            src = block(t, step, 2, d) if kind == 0 else block(t, step, went[d])
            dst = (first, whole)[kind][step].at[t, d]
            pltpu.make_async_remote_copy(
                full.at[src], dst, s_send.at[step, kind], s_recv.at[step, kind, d],
                device_id=place.chip(axis_of(t, 2 - step), 1 if d == 0 else 3), device_id_type=MESH).start()

    def take_first(step, d):
        await_landed(place, first[step].at[:, d], s_recv.at[step, 0, d])
        for t in range(3):
            here = block(t, step, went[d], d)
            full[here] = full[here] + first[step][t, d]
        start(step, 1, d)

    def take_whole(step):
        for d in range(2):
            await_landed(place, whole[step].at[:, d], s_recv.at[step, 1, d])
        for t in range(3):
            here = block(t, step, 0)
            full[here] = full[here] + (whole[step][t, 0] + whole[step][t, 1])

    def multiply(t, middle, distance):
        where = [place.line(t, middle, distance, c) for c in range(N)]
        right = [parts[t, :, pl.ds(pl.multiple_of(((cz * N + cx) * N + cy) * RANK, RANK), RANK)] for cz, cx, cy in where]
        right = jnp.concatenate(right, 1)
        out = dot(stacked[t], jnp.concatenate([right, right[:rows]], 0))
        out = out[:RANK] + out[RANK:]
        for c, (cz, cx, cy) in enumerate(where):
            full[t, cz, cx, cy] = out[:, c * RANK:(c + 1) * RANK].reshape(2, RANK // 2, RANK)

    def multiply_plane(n, distance):
        @pl.loop(0, 3)
        def _(t):
            for middle in range(N):
                multiply(t, middle, distance)
        for t in range(3):
            swap(t, n, distance)

    def settle(n, distance):
        await_landed(place, other.at[:, 0], d_recv.at[n])

        @pl.loop(0, 3 * N)
        def _(i):
            t, middle = i // N, lax.rem(i, N)
            for c in range(N):
                cz, cx, cy = place.line(t, middle, distance, c)
                full[t, cz, cx, cy, core] += other[t, cz, cx, cy]

    order = (2, 3, 1, 0)
    multiply_plane(0, 2)
    next(rest, None)
    next(rest, None)
    multiply_plane(1, 3)
    settle(0, 2)
    start(0, 0, 0)
    start(0, 0, 1)
    next(rest, None)
    multiply_plane(2, 1)
    next(rest, None)
    settle(1, 3)
    for _ in rest:
        pass
    take_first(0, 1)
    settle(2, 1)
    take_first(0, 0)

    def ring_ends():
        take_whole(0)
        start(1, 0, 0)
        start(1, 0, 1)
        yield
        take_first(1, 0)
        take_first(1, 1)
        yield
        take_whole(1)
        start(2, 0, 0)
        start(2, 0, 1)
        yield
        take_first(2, 0)
        take_first(2, 1)
        yield
        take_whole(2)
        for t in range(3):
            held[t] = full[unit(t, 0)]
            pair[t, core] = held[t]
        half_swap.start()
        yield

    half_swap = pltpu.make_async_remote_copy(
        held, pair.at[:, core], x_send, x_recv, device_id=place.sibling(), device_id_type=MESH)

    def grams(inverse):
        if inverse:
            for t in range(3):
                h, m, l = split(mix[t].T, 3)
                wide[t] = jnp.concatenate([jnp.concatenate([h, m, l], 1), jnp.concatenate([m, h, h], 1)], 0)

        def add(i, grams):
            out = []
            for t in range(3):
                whole, low = grams[t]
                some = raw[t, i].reshape(512, RANK)
                if inverse:
                    h, m, l = split(some, 3)
                    main = dot(jnp.concatenate([h, m], 1), wide[t, :, :2 * RANK])
                    rest = dot(jnp.concatenate([h, l], 1), wide[t, :, 2 * RANK:])
                    some = main[:, :RANK] + (main[:, RANK:] + rest)
                all_ = dot(jnp.concatenate(split(some.T, 3), 0), jnp.concatenate(split(some, 2), 1))
                tile = lambda i, j: all_[i * RANK:(i + 1) * RANK, j * RANK:(j + 1) * RANK]
                out.append((whole + (tile(0, 0) + ((tile(0, 1) + tile(1, 0)) + tile(1, 1))), low + tile(2, 0)))
            return tuple(out)

        zero = jnp.zeros((RANK, RANK), F32)
        for t, (whole, low) in enumerate(lax.fori_loop(0, N, add, ((zero, zero),) * 3)):
            both[t, :, :RANK] = whole + (low + low.T)
            both[t, :, RANK:] = eye

    grams(False)
    ends = ring_ends()

    @pl.loop(0, N)
    def _(i):
        for t in range(3):
            multiply(t, i, 0)
        factor_block(both, i)

    for t in range(3):
        swap(t, 3, 0)
    pl.loop(N, 8)(lambda i: factor_block(both, i))
    settle(3, 0)
    next(ends)
    for t in range(3):
        mix[t] = both[t, :, RANK:]
    grams(True)
    for i in (0, 2, 4):
        next(ends)
        pl.loop(i, i + 2)(lambda i: factor_block(both, i))
    next(ends)
    factor_block(both, 6)
    await_landed(place, pair.at[:, 1 - core], x_recv)
    for t in range(3):
        pair[t] = dot(mix[t] * (1.0 / N), pair[t].reshape(RANK, RANK), precision=HIGH).reshape(2, RANK // 2, RANK)
    factor_block(both, 7)
    half_swap.wait_send()
    for send in sends:
        send.wait_send()
    for step in range(3):
        await_sent(place, first[step], s_send.at[step, 0])
        await_sent(place, whole[step], s_send.at[step, 1])
    await_sent(place, other, d_send)

    term = qbuf
    mine = pl.ds(pl.multiple_of(core * (RANK // 2), RANK // 2), RANK // 2)
    ones = jnp.ones((8, RANK), F32)
    own = lax.broadcasted_iota(jnp.int32, (RANK, RANK), 0) // (RANK // 2) == core
    for t in range(3):
        pair[t] = dot(both[t, :, RANK:], pair[t].reshape(RANK, RANK), precision=HIGH).reshape(2, RANK // 2, RANK)
        term[t, z, x, y, core] = pair[t, core]

    def tell(stage, where, peer, sem):
        return pltpu.make_async_remote_copy(norms.at[stage, where], norms.at[stage, where], n_send.at[stage, sem],
                                            n_recv.at[stage, sem], device_id=peer, device_id_type=MESH)

    def sum_norms():
        for t in range(3):
            product = pair[t].reshape(RANK, RANK)
            norms[0, core, t] = dot(ones, jnp.where(own, product * product, 0.0), NT, HIGH)
        tell(0, core, place.sibling(), 0).start()
        yield
        tell(0, 1 - core, place.sibling(), 0).wait_recv()
        total = norms[0, 0] + norms[0, 1]
        for axis in range(3):
            stage = 1 + axis
            here = place.at[axis]
            norms[stage, here] = total
            for d in (1, 2, 3):
                tell(stage, here, place.chip(axis, d), d).start()
            yield
            for d in (1, 2, 3):
                tell(stage, place.far(axis, N - d), place.chip(axis, d), d).wait_recv()
            total = (norms[stage, 0] + norms[stage, 1]) + (norms[stage, 2] + norms[stage, 3])
            if axis == 0:
                for t in range(3):
                    left = dot(zown[:, t].reshape(rows, RANK), mix[t], NT, HIGH)
                    left_ref[t] = dot(left, both[t, :, RANK:], NT, HIGH)
        scales = 1.0 / jnp.sqrt(total + 1e-6)
        for t in range(3):
            scale = scales[t, 0:1]
            left = left_ref[t]
            high, low = split(jnp.concatenate([left * 0.05, left * (scale * gain)], 0), 2)
            lhs[t] = jnp.concatenate(
                [jnp.concatenate([high, high], 1), jnp.concatenate([low, jnp.zeros_like(low)], 1)], 0)
            basis = pair[t].reshape(RANK, RANK).T * scale
            basis_ref[:, t * RANK:(t + 1) * RANK] = jnp.where(core == 0, basis[:RANK // 2], basis[RANK // 2:])
        tell(0, core, place.sibling(), 0).wait_send()
        for axis in range(3):
            for d in (1, 2, 3):
                tell(1 + axis, place.at[axis], place.chip(axis, d), d).wait_send()
        yield

    def emit(j1, j2):
        for t in range(3):
            where = place.chips(t, j1, j2)
            block = jnp.concatenate([term[(t, *chip)].reshape(RANK, RANK) for chip in where], 1)
            out = dot(lhs[t], jnp.concatenate(split(block, 2), 0))
            out = out[:RANK] + out[RANK:]
            for i, (cz, cx, cy) in enumerate(where):
                column = pl.ds(pl.multiple_of(((cz * N + cx) * N + cy) * RANK, RANK), RANK)
                tile = slice(i * RANK, (i + 1) * RANK)
                h, m, l = [parts[t, j * rows:(j + 1) * rows, column].astype(F32) for j in range(3)]
                full[t, cz, cx, cy, 0] = (h + (m + l)) - out[:rows, tile]
                full[t, cz, cx, cy, 1] = out[rows:, tile]

    norm_steps = sum_norms()
    for _ in fine_gather(place, term, sems_term, emit):
        next(norm_steps, None)


def last_kernel(both_ref, basis_in, next_ref, update_ref, basis_ref):
    t, i = pl.program_id(0), pl.program_id(1)
    count = update_ref.shape[2] // RANK
    for j in range(count):
        chip = i * count + j
        where = (t, chip // (N * N), lax.rem(chip // N, N), lax.rem(chip, N))
        next_ref[0, 0, :, j * RANK:(j + 1) * RANK] = both_ref[(*where, 0)]
        update_ref[0, :, j * RANK:(j + 1) * RANK] = both_ref[(*where, 1)]
    basis_ref[...] = basis_in[...]


def body(momentum, gradient, basis):
    momentum, gradient = momentum[0], gradient[0]
    count, rows, width = momentum.shape
    chips = (N, N, N, 2)
    dma = pltpu.SemaphoreType.DMA
    f32 = lambda *shape: jax.ShapeDtypeStruct(shape, F32)
    room = lambda *shape: pltpu.VMEM(shape, F32)
    gain = float((2048 * 8192 / RANK) ** 0.5)
    full, basis_next = pl.pallas_call(
        functools.partial(main_kernel, gain),
        name="dion",
        out_shape=[room(3, *chips, 64, RANK), room(64, 3 * RANK)],
        in_specs=[ANY] * 3,
        out_specs=[VMEM] * 2,
        scratch_shapes=[
            pltpu.VMEM((count, 3 * rows, width), BF16), room(3, *chips, 64, RANK), room(3, rows, RANK),
            pltpu.VMEM((3, 2 * RANK, 2 * RANK), BF16), room(4, N, 3, 8, RANK),
            room(4, count, rows, 512), room(4, count, rows, 512),
            room(count, rows, RANK), room(N, 3, 16, RANK), room(N, 3, 16, RANK), room(3, *chips, 16, RANK),
            pltpu.VMEM((3, 2 * RANK, 4 * rows), BF16), room(3, RANK, 2 * RANK),
            room(3, N, N, N, 64, RANK),
            room(3, 2, N, N, 32, RANK), room(3, 2, N, N, 64, RANK),
            room(3, 2, N, 32, RANK), room(3, 2, N, 64, RANK),
            room(3, 2, 32, RANK), room(3, 2, 64, RANK),
            room(3, 2, 64, RANK), room(3, 64, RANK), room(3, RANK, RANK),
            pltpu.VMEM((3, 2 * RANK, 3 * RANK), BF16),
            dma((3,)), dma((2, 4)), dma((2, 4)), dma((2, 4)),
            dma, dma((N,)), dma((3, 2)), dma((3, 2, 2)), dma, dma, dma((4, 4)), dma((4, 4))] + fine_sems() + gather_sems() + fine_sems(),
        compiler_params=pltpu.CompilerParams(collective_id=0, has_side_effects=True, vmem_limit_bytes=49 * 2 ** 20),
    )(momentum, gradient, basis)
    span = 2048
    full, basis_next = [pltpu.with_memory_space_constraint(a, pltpu.VMEM) for a in (full, basis_next)]
    return pl.pallas_call(
        last_kernel,
        name="outputs",
        grid=(3, width // span),
        out_shape=[f32(1, count, rows, width), f32(count, rows, width), f32(64, 3 * RANK)],
        in_specs=[VMEM] * 2,
        out_specs=[
            pl.BlockSpec((1, 1, rows, span), lambda t, i: (0, t, 0, i)),
            pl.BlockSpec((1, rows, span), lambda t, i: (t, 0, i)),
            pl.BlockSpec((64, 3 * RANK), lambda t, i: (0, 0)),
        ],
        compiler_params=pltpu.CompilerParams(vmem_limit_bytes=16 * 2 ** 20),
    )(full, basis_next)


def solution(mesh):
    placed = (P("rep", None, "fsdp", None), P("rep", None, "fsdp", None), P(("rep", "fsdp"), None))
    return jax.shard_map(
        body,
        mesh=mesh,
        in_specs=placed,
        out_specs=(P("rep", None, "fsdp", None), P(None, "fsdp", None), P(("rep", "fsdp"), None)),
        check_vma=False,
    )
```

```python
import functools

import jax
import jax.numpy as jnp
from jax import lax
from jax.experimental import pallas as pl
from jax.experimental.pallas import tpu as pltpu
from jax.sharding import PartitionSpec as P

MESH = pl.DeviceIdType.MESH
HIGH = lax.Precision.HIGHEST
F32 = jnp.float32
BF16 = jnp.bfloat16
RANK = 128
N = 4
ANY = pl.BlockSpec(memory_space=pl.ANY)
VMEM = pl.BlockSpec(memory_space=pltpu.VMEM)


def axis_of(third, phase):
    return (2, 1, 0)[(third + phase) % 3]


class Place:
    def __init__(self):
        self.rep = lax.axis_index("rep")
        self.fsdp = lax.axis_index("fsdp")
        self.core = lax.rem(self.fsdp, 2)
        self.at = (self.rep, lax.div(self.fsdp, 8), lax.rem(lax.div(self.fsdp, 2), N))

    def far(self, axis, distance):
        if isinstance(distance, int) and distance == 0:
            return self.at[axis]
        return lax.rem(self.at[axis] + distance, N)

    def chip(self, axis, distance):
        at = list(self.at)
        at[axis] = self.far(axis, distance)
        return (at[0], (at[1] * N + at[2]) * 2 + self.core)

    def sibling(self):
        return (self.rep, self.fsdp + 1 - 2 * self.core)

    def chips(self, t, j1, j2):
        where = [None] * 3
        where[axis_of(t, 1)] = self.far(axis_of(t, 1), dyn_off(j1))
        where[axis_of(t, 2)] = self.far(axis_of(t, 2), dyn_off(j2))
        out = []
        for i in range(N):
            where[axis_of(t, 0)] = i
            out.append(tuple(where))
        return out

    def line(self, third, middle, distance, i):
        places = []
        for t in range(3):
            where = [None] * 3
            where[axis_of(t, 0)] = i
            where[axis_of(t, 1)] = middle
            where[axis_of(t, 2)] = self.far(axis_of(t, 2), distance)
            places.append(where)
        return [jnp.where(third == 0, a, jnp.where(third == 1, b, c)) for a, b, c in zip(*places)]


def dyn_off(j):
    return OFF[j] if isinstance(j, int) else j + (j // 2) * (5 - 2 * j)


def greet(place, distances):
    barrier = pltpu.get_barrier_semaphore()
    peers = [place.sibling()] + [place.chip(axis, d) for axis, d in distances]
    for peer in peers:
        pl.semaphore_signal(barrier, inc=1, device_id=peer, device_id_type=MESH)
    pl.semaphore_wait(barrier, len(peers))


OFF = (0, 1, 3, 2)
NEAR = [(axis, d) for axis in range(3) for d in (1, 3)]


def await_landed(place, spot, sem):
    pltpu.make_async_remote_copy(spot, spot, sem, sem, device_id=place.sibling(), device_id_type=MESH).wait_recv()


def await_sent(place, spot, sem):
    pltpu.make_async_remote_copy(spot, spot, sem, sem, device_id=place.sibling(), device_id_type=MESH).wait_send()


def gather_sems():
    dma = pltpu.SemaphoreType.DMA
    return [dma((3,)), dma((3, 4)), dma((3, 2)), dma, dma((7,))]


def gather(place, buf, sems, hook=None):
    sent, recv_a, recv_b, sent_d, recv_d = sems
    core = place.core
    half = buf.shape[5] // 2
    thirds = range(3)

    def spot(t, p, distance, whose, part=None, middle=slice(None)):
        where = [None] * 3
        for q in range(3):
            axis = axis_of(t, q)
            if q < p:
                where[axis] = middle if q == 1 else slice(None)
            elif q == p:
                where[axis] = place.far(axis, distance)
            else:
                where[axis] = place.at[axis]
        return buf.at[(t, *where, whose, slice(None) if part is None else pl.ds(part * half, half))]

    def send(t, p, d, block, sem):
        pltpu.make_async_remote_copy(
            block, block, sent.at[p], sem,
            device_id=place.chip(axis_of(t, p), 1 if d == 0 else 3), device_id_type=MESH).start()

    def share(block, n):
        pltpu.make_async_remote_copy(
            block, block, sent_d, recv_d.at[n], device_id=place.sibling(), device_id_type=MESH).start()

    def size(p, whose, pieces=N):
        if p == 0:
            return buf.at[:, 0, 0, 0, whose]
        if p == 1:
            return buf.at[:, 0, 0, :, whose]
        return buf.at[:, 0, pl.ds(0, pieces), :, whose]

    came = (3, 1)
    for p in (0, 1):
        for t in thirds:
            for d in range(2):
                send(t, p, d, spot(t, p, 0, core), recv_a.at[p, d])
        yield
        for d in range(2):
            await_landed(place, size(p, core), recv_a.at[p, d])
            for t in thirds:
                send(t, p, d, spot(t, p, came[d], core, d), recv_b.at[p, 0])
        yield
        await_landed(place, size(p, core), recv_b.at[p, 0])
    run = hook if hook is not None else lambda *_: None
    piece = lambda c: pl.ds(2 * c, 2)
    for c in range(2):
        for t in thirds:
            for d in range(2):
                send(t, 2, d, spot(t, 2, 0, core, None, piece(c)), recv_a.at[2, 2 * c + d])
    for t in thirds:
        share(spot(t, 2, 0, core), 0)
    yield
    await_landed(place, size(2, 1 - core), recv_d.at[0])
    run(0, 0, N)
    for c in range(2):
        for d in range(2):
            await_landed(place, size(2, core, 2), recv_a.at[2, 2 * c + d])
            for t in thirds:
                send(t, 2, d, spot(t, 2, came[d], core, d, piece(c)), recv_b.at[2, c])
        for d in range(2):
            for t in thirds:
                share(spot(t, 2, came[d], core, None, piece(c)), 1 + 2 * c + d)
        yield
        if c == 0:
            for d in range(2):
                await_landed(place, size(2, 1 - core, 2), recv_d.at[1 + d])
                run(came[d], 0, 2)
    for c in range(2):
        await_landed(place, size(2, core, 2), recv_b.at[2, c])
        for t in thirds:
            share(spot(t, 2, 2, core, None, piece(c)), 5 + c)
        await_landed(place, size(2, 1 - core, 2), recv_d.at[3 + c])
        run(came[c], 2, 2)
    for c in range(2):
        await_landed(place, size(2, 1 - core, 2), recv_d.at[5 + c])
        run(2, 2 * c, 2)
    await_sent(place, buf.at[:, 0, 0, pl.ds(0, 3), core], sent.at[0])
    await_sent(place, buf.at[:, 0, pl.ds(0, 3), :, core], sent.at[1])
    await_sent(place, buf.at[:, pl.ds(0, 3), :, :, core], sent.at[2])
    await_sent(place, buf.at[:, :, :, :, core], sent_d)


def fine_sems():
    dma = pltpu.SemaphoreType.DMA
    return [dma((3, 3, 4, 2))] * 4 + [dma((3, 4, 4))] * 2


def fine_gather(place, buf, sems, hook):
    send_a, recv_a, send_b, recv_b, send_d, recv_d = sems
    core = place.core
    rows = buf.shape[5]
    half = rows // 2

    def index(t, p, j, da, part=None):
        where = [None] * 3
        for q in range(3):
            axis = axis_of(t, q)
            if q < p - 1:
                where[axis] = slice(None)
            elif q == p - 1:
                where[axis] = place.far(axis, dyn_off(j))
            elif q == p:
                where[axis] = place.far(axis, da)
            else:
                where[axis] = place.at[axis]
        span = slice(None) if part is None else pl.ds(part * half, half)
        return (t, *where, core, span)

    def copy_a(t, p, j, d, da):
        spot = buf.at[index(t, p, j, da)]
        return pltpu.make_async_remote_copy(
            spot, spot, send_a.at[t, p, j, d], recv_a.at[t, p, j, d],
            device_id=place.chip(axis_of(t, p), 1 if d == 0 else 3), device_id_type=MESH)

    def copy_b(t, p, j, d, da):
        spot = buf.at[index(t, p, j, da, d)]
        return pltpu.make_async_remote_copy(
            spot, spot, send_b.at[t, p, j, d], recv_b.at[t, p, j, d],
            device_id=place.chip(axis_of(t, p), 1 if d == 0 else 3), device_id_type=MESH)

    def copy_d(t, j1, j2, whose):
        where = [None] * 3
        where[axis_of(t, 0)] = slice(None)
        where[axis_of(t, 1)] = place.far(axis_of(t, 1), dyn_off(j1))
        where[axis_of(t, 2)] = place.far(axis_of(t, 2), dyn_off(j2))
        spot = buf.at[(t, *where, whose)]
        return pltpu.make_async_remote_copy(
            spot, spot, send_d.at[t, j1, j2], recv_d.at[t, j1, j2],
            device_id=place.sibling(), device_id_type=MESH)

    def start_a(t, p, j):
        for d in range(2):
            copy_a(t, p, j, d, 0).start()

    def land_a(t, p, j, d):
        copy_a(t, p, j, d, 3 if d == 0 else 1).wait_recv()
        copy_b(t, p, j, d, 3 if d == 0 else 1).start()

    def land_b(t, p, j):
        for d in range(2):
            copy_b(t, p, j, d, 2).wait_recv()

    def line_done(j1, j2):
        for t in range(3):
            copy_d(t, j1, j2, 1 - core).wait_recv()
        hook(j1, j2)

    thirds = range(3)
    for t in thirds:
        start_a(t, 0, 0)
    for t in thirds:
        start_a(t, 1, 0)
    yield
    for d in range(2):
        for t in thirds:
            land_a(t, 0, 0, d)
            start_a(t, 1, 2 - d)
    yield
    for t in thirds:
        land_b(t, 0, 0)
        start_a(t, 1, 3)
    for t in thirds:
        start_a(t, 2, 0)
        copy_d(t, 0, 0, core).start()
    yield
    for j in range(4):
        for t in thirds:
            for d in range(2):
                land_a(t, 1, j, d)
        yield
    for j1 in (1, 2):
        for t in thirds:
            start_a(t, 2, j1)
            copy_d(t, j1, 0, core).start()
    for j in range(4):
        for t in thirds:
            land_b(t, 1, j)
    for t in thirds:
        start_a(t, 2, 3)
        copy_d(t, 3, 0, core).start()
    yield

    @pl.loop(0, 4)
    def _(j):
        for t in thirds:
            for d in range(2):
                land_a(t, 2, j, d)
                copy_d(t, j, 2 - d, core).start()
        line_done(j, 0)

        @pl.when(j >= 1)
        def _():
            line_done(j - 1, 1)
            line_done(j - 1, 2)

    line_done(3, 1)
    line_done(3, 2)

    @pl.loop(0, 4)
    def _(j):
        for t in thirds:
            land_b(t, 2, j)
            copy_d(t, j, 3, core).start()
        pl.when(j >= 1)(lambda: line_done(j - 1, 3))

    line_done(3, 3)
    for t in thirds:
        for p in range(3):
            for j in range(1 if p == 0 else 4):
                for d in range(2):
                    copy_a(t, p, j, d, 0).wait_send()
                    copy_b(t, p, j, d, 3 if d == 0 else 1).wait_send()

    @pl.loop(0, 4)
    def _(j1):
        @pl.loop(0, 4)
        def _(j2):
            for t in thirds:
                copy_d(t, j1, j2, core).wait_send()


def split(values, parts):
    out = []
    for _ in range(parts):
        out.append(values.astype(BF16))
        values = values - out[-1].astype(F32)
    return out


def dot(left, right, dims=((1,), (0,)), precision=None):
    return lax.dot_general(left, right, (dims, ((), ())), precision=precision, preferred_element_type=F32)


NT = ((1,), (1,))
TN = ((0,), (0,))


def factor_block(both, step):
    count, size, _ = both.shape
    block, piece = 16, 8
    lane = lax.broadcasted_iota(jnp.int32, (count, block, size), 2)
    base = pl.multiple_of(step * block, block)
    band = both[:, pl.ds(base, block), :]
    upper, lower = band[:, :, :size], band[:, :, size:]
    inverses, done = [], []
    for part in range(block // piece):
        rows = block - part * piece
        shape = (count, rows, size)
        sub = lax.broadcasted_iota(jnp.int32, shape, 1)
        spread = lambda a, i: jnp.broadcast_to(a[:, i:i + 1, :], shape)
        turned = jnp.stack([pltpu.roll(upper[k], lax.rem(size - base, size), 1) for k in range(count)])
        columns = [jnp.broadcast_to(turned[:, :, part * piece + i:part * piece + i + 1], shape) for i in range(piece)]
        inverse = jnp.zeros((count, piece, size), F32)
        for i in range(piece):
            pivot = jnp.broadcast_to(columns[i][:, i:i + 1, :], (count, piece, size))
            recip = pl.reciprocal(pivot, approx=True)
            recip = recip * (2.0 - pivot * recip)
            recip = recip * (2.0 - pivot * recip)
            inverse = jnp.where(sub[:, :piece] == i, recip, inverse)
            factor = jnp.where(sub > i, columns[i] * jnp.concatenate([recip] * (rows // piece), 1), 0.0)
            for q in range(i + 1, piece):
                columns[q] = columns[q] - factor * spread(columns[q], i)
            upper = upper - factor * spread(upper, i)
            lower = lower - factor * spread(lower, i)
        inverses.append(inverse)
        done.append((upper[:, :piece], lower[:, :piece]))
        upper, lower = upper[:, piece:], lower[:, piece:]
    upper, lower = [jnp.concatenate(half, 1) for half in zip(*done)]
    inverse = jnp.concatenate(inverses, 1)
    factors = jnp.where(lane >= base + block, upper * inverse, 0.0)
    rows = jnp.concatenate([upper, lower], 2)
    less = []
    for k in range(count):
        h, m, l = split(factors[k], 3)
        first = jnp.concatenate([h, h, h, m, m, l], 0)
        h, m, l = split(rows[k], 3)
        less.append(dot(first, jnp.concatenate([h, m, l, h, m, h], 0), TN))
    for k in range(count):
        both[k] = both[k] - less[k]
    both[:, pl.ds(base, block), :] = jnp.concatenate([upper, lower * jnp.sqrt(inverse)], 2)


def main_kernel(gain, m_hbm, g_hbm, q_hbm, full, basis_ref, parts, qbuf, left_ref, lhs, norms,
                mbuf, gbuf, part, zbuf, zown, raw, stacked, both, other,
                ra0, rb0, ra1, rb1, ra2, rb2, pair, held, mix, sums, wide,
                q_sem, load_sem, z_send, z_recv, d_send, d_recv, s_send, s_recv, x_send, x_recv, g_send, g_recv, n_send, n_recv, *sems):
    place = Place()
    z, x, y = place.at
    core = place.core
    sems_q, sems_raw, sems_term = sems[:6], sems[6:11], sems[11:]
    count, stack_rows, width = parts.shape
    slots, _, rows, span = mbuf.shape
    chunks = width // span

    def columns(i):
        return pl.ds(pl.multiple_of(i * span, span), span)

    def load(i):
        slot = lax.rem(i, slots)
        return (pltpu.make_async_copy(m_hbm.at[:, :, columns(i)], mbuf.at[slot], load_sem.at[0, slot]),
                pltpu.make_async_copy(g_hbm.at[:, :, columns(i)], gbuf.at[slot], load_sem.at[1, slot]))

    def blend(first, last):
        @pl.loop(first, last)
        def _(i):
            slot = lax.rem(i, slots)
            for copy in load(i):
                copy.wait()
            for t in range(count):
                parts[t, :, columns(i)] = jnp.concatenate(split(mbuf[slot, t] + gbuf[slot, t], 3), 0)

            @pl.when(i + slots < chunks)
            def _():
                for copy in load(i + slots):
                    copy.start()

    loads = [pltpu.make_async_copy(q_hbm.at[:, pl.ds(t * RANK, RANK)], qbuf.at[t, z, x, y, core], q_sem.at[t])
             for t in range(3)]
    for copy in loads:
        copy.start()
    for i in range(slots):
        for copy in load(i):
            copy.start()
    greet(place, NEAR + [(0, 2), (1, 2), (2, 2)])
    for copy in loads:
        copy.wait()
    part[...] = jnp.zeros_like(part)

    def hook(j1, j2):
        for t in range(3):
            left, right = [], []
            for cz, cx, cy in place.chips(t, j1, j2):
                column = pl.multiple_of(((cz * N + cx) * N + cy) * RANK, RANK)
                left.append(parts[t, :, pl.ds(column, RANK)])
                right.append(qbuf[t, cz, cx, cy].reshape(RANK, RANK))
            left = jnp.concatenate(left, 1)
            h, m, l = split(jnp.concatenate(right, 0), 3)
            out = dot(left, jnp.concatenate([h, m], 1))
            tile = lambda i, j: out[i * rows:(i + 1) * rows, j * RANK:(j + 1) * RANK]
            small = (tile(2, 0) + tile(1, 1)) + dot(left[:rows], l)
            part[t] += (small + (tile(1, 0) + tile(0, 1))) + tile(0, 0)

    done = 0
    for _ in fine_gather(place, qbuf, sems_q, hook):
        if done < chunks:
            blend(done, min(done + 2, chunks))
            done += 2

    quarter = rows // N
    sends = []
    for d in (1, 2, 3):
        to = place.far(0, d)
        sends.append(pltpu.make_async_remote_copy(
            part.at[:, pl.ds(pl.multiple_of(to * quarter, quarter), quarter)], zbuf.at[d],
            z_send.at[0, d], z_recv.at[0, d], device_id=place.chip(0, d), device_id_type=MESH))
        sends[-1].start()
    zbuf[0] = part[:, pl.ds(pl.multiple_of(z * quarter, quarter), quarter)]
    for send in sends:
        send.wait_recv()
    total = ((zbuf[0] + zbuf[1]) + (zbuf[2] + zbuf[3])) * (1.0 / N)
    zown[z] = total
    for t in range(3):
        raw[t, z, x, y, core] = total[t]
    for d in (1, 2, 3):
        sends.append(pltpu.make_async_remote_copy(
            zown.at[z], zown.at[z], z_send.at[1, d], z_recv.at[1, d],
            device_id=place.chip(0, d), device_id_type=MESH))
        sends[-1].start()
    rest = gather(place, raw, sems_raw)
    next(rest)
    for d in (1, 2, 3):
        spot = zown.at[place.far(0, N - d)]
        pltpu.make_async_remote_copy(spot, spot, z_send.at[1, d], z_recv.at[1, d],
                                     device_id=place.chip(0, d), device_id_type=MESH).wait_recv()
    eye = (lax.broadcasted_iota(jnp.int32, (RANK, RANK), 0) == lax.broadcasted_iota(jnp.int32, (RANK, RANK), 1)).astype(F32)
    for t in range(3):
        h, m, l = [p.astype(F32) for p in split(zown[:, t].reshape(rows, RANK), 3)]
        none = jnp.zeros_like(h)
        pairs = [jnp.concatenate(pair, 1) for pair in ((h, l), (h, m), (h, none), (m, none))]
        stacked[t] = jnp.concatenate(pairs, 0).T.astype(BF16)

    half = RANK // 4

    def plane(t, distance, whose, part=None):
        where = [slice(None)] * 3
        where[axis_of(t, 2)] = place.far(axis_of(t, 2), distance)
        return (t, *where, whose, slice(None) if part is None else pl.ds(part * half, half))

    def line(t, distance, part=None):
        where = list(place.at)
        where[axis_of(t, 0)] = slice(None)
        where[axis_of(t, 1)] = place.far(axis_of(t, 1), distance)
        return (t, *where, core, slice(None) if part is None else pl.ds(part * half, half))

    def unit(t, distance, part=None):
        where = list(place.at)
        where[axis_of(t, 0)] = place.far(axis_of(t, 0), distance)
        return (t, *where, core, slice(None) if part is None else pl.ds(part * half, half))

    spots = (plane, line, unit)
    went = (1, 3)
    first, whole = (ra0, ra1, ra2), (rb0, rb1, rb2)

    def swap(t, n, distance):
        where = plane(t, distance, 1 - core)
        pltpu.make_async_remote_copy(
            full.at[where], other.at[where[:4]], d_send, d_recv.at[n],
            device_id=place.sibling(), device_id_type=MESH).start()

    def block(t, step, distance, part=None):
        return plane(t, distance, core, part) if step == 0 else spots[step](t, distance, part)

    def start(step, kind, d):
        for t in range(3):
            src = block(t, step, 2, d) if kind == 0 else block(t, step, went[d])
            dst = (first, whole)[kind][step].at[t, d]
            pltpu.make_async_remote_copy(
                full.at[src], dst, s_send.at[step, kind], s_recv.at[step, kind, d],
                device_id=place.chip(axis_of(t, 2 - step), 1 if d == 0 else 3), device_id_type=MESH).start()

    def take_first(step, d):
        await_landed(place, first[step].at[:, d], s_recv.at[step, 0, d])
        for t in range(3):
            here = block(t, step, went[d], d)
            full[here] = full[here] + first[step][t, d]
        start(step, 1, d)

    def take_whole(step):
        for d in range(2):
            await_landed(place, whole[step].at[:, d], s_recv.at[step, 1, d])
        for t in range(3):
            here = block(t, step, 0)
            full[here] = full[here] + (whole[step][t, 0] + whole[step][t, 1])

    def multiply(t, middle, distance):
        where = [place.line(t, middle, distance, c) for c in range(N)]
        right = [parts[t, :, pl.ds(pl.multiple_of(((cz * N + cx) * N + cy) * RANK, RANK), RANK)] for cz, cx, cy in where]
        right = jnp.concatenate(right, 1)
        out = dot(stacked[t], jnp.concatenate([right, right[:rows]], 0))
        out = out[:RANK] + out[RANK:]
        for c, (cz, cx, cy) in enumerate(where):
            full[t, cz, cx, cy] = out[:, c * RANK:(c + 1) * RANK].reshape(2, RANK // 2, RANK)

    def multiply_plane(n, distance):
        @pl.loop(0, 3)
        def _(t):
            for middle in range(N):
                multiply(t, middle, distance)
        for t in range(3):
            swap(t, n, distance)

    def settle(n, distance):
        await_landed(place, other.at[:, 0], d_recv.at[n])

        @pl.loop(0, 3 * N)
        def _(i):
            t, middle = i // N, lax.rem(i, N)
            for c in range(N):
                cz, cx, cy = place.line(t, middle, distance, c)
                full[t, cz, cx, cy, core] += other[t, cz, cx, cy]

    order = (2, 3, 1, 0)
    multiply_plane(0, 2)
    next(rest, None)
    next(rest, None)
    multiply_plane(1, 3)
    settle(0, 2)
    start(0, 0, 0)
    start(0, 0, 1)
    next(rest, None)
    multiply_plane(2, 1)
    next(rest, None)
    settle(1, 3)
    for _ in rest:
        pass
    take_first(0, 1)
    settle(2, 1)
    take_first(0, 0)

    def ring_ends():
        take_whole(0)
        start(1, 0, 0)
        start(1, 0, 1)
        yield
        take_first(1, 0)
        take_first(1, 1)
        yield
        take_whole(1)
        start(2, 0, 0)
        start(2, 0, 1)
        yield
        take_first(2, 0)
        take_first(2, 1)
        yield
        take_whole(2)
        for t in range(3):
            held[t] = full[unit(t, 0)]
            pair[t, core] = held[t]
        half_swap.start()
        yield

    half_swap = pltpu.make_async_remote_copy(
        held, pair.at[:, core], x_send, x_recv, device_id=place.sibling(), device_id_type=MESH)

    def grams(inverse):
        if inverse:
            for t in range(3):
                h, m, l = split(mix[t].T, 3)
                wide[t] = jnp.concatenate([jnp.concatenate([h, m, l], 1), jnp.concatenate([m, h, h], 1)], 0)

        first, many = (core * 2, 2) if inverse else (0, N)

        def add(i, grams):
            out = []
            for t in range(3):
                whole, low = grams[t]
                some = raw[t, first + i].reshape(512, RANK)
                if inverse:
                    h, m, l = split(some, 3)
                    main = dot(jnp.concatenate([h, m], 1), wide[t, :, :2 * RANK])
                    rest = dot(jnp.concatenate([h, l], 1), wide[t, :, 2 * RANK:])
                    some = main[:, :RANK] + (main[:, RANK:] + rest)
                all_ = dot(jnp.concatenate(split(some.T, 3), 0), jnp.concatenate(split(some, 2), 1))
                tile = lambda i, j: all_[i * RANK:(i + 1) * RANK, j * RANK:(j + 1) * RANK]
                out.append((whole + (tile(0, 0) + ((tile(0, 1) + tile(1, 0)) + tile(1, 1))), low + tile(2, 0)))
            return tuple(out)

        zero = jnp.zeros((RANK, RANK), F32)
        for t, (whole, low) in enumerate(lax.fori_loop(0, many, add, ((zero, zero),) * 3)):
            both[t, :, RANK:] = eye
            if inverse:
                sums[0, t] = whole + (low + low.T)
            else:
                both[t, :, :RANK] = whole + (low + low.T)
        if inverse:
            trade = pltpu.make_async_remote_copy(sums.at[0], sums.at[1], g_send, g_recv, device_id=place.sibling(),
                                                 device_id_type=MESH)
            trade.start()
            trade.wait()
            for t in range(3):
                both[t, :, :RANK] = sums[0, t] + sums[1, t]

    grams(False)
    ends = ring_ends()

    @pl.loop(0, N)
    def _(i):
        for t in range(3):
            multiply(t, i, 0)
        factor_block(both, i)

    for t in range(3):
        swap(t, 3, 0)
    pl.loop(N, 8)(lambda i: factor_block(both, i))
    settle(3, 0)
    next(ends)
    for t in range(3):
        mix[t] = both[t, :, RANK:]
    grams(True)
    for i in (0, 2, 4):
        next(ends)
        pl.loop(i, i + 2)(lambda i: factor_block(both, i))
    next(ends)
    factor_block(both, 6)
    await_landed(place, pair.at[:, 1 - core], x_recv)
    for t in range(3):
        pair[t] = dot(mix[t] * (1.0 / N), pair[t].reshape(RANK, RANK), precision=HIGH).reshape(2, RANK // 2, RANK)
    factor_block(both, 7)
    half_swap.wait_send()
    for send in sends:
        send.wait_send()
    for step in range(3):
        await_sent(place, first[step], s_send.at[step, 0])
        await_sent(place, whole[step], s_send.at[step, 1])
    await_sent(place, other, d_send)

    term = qbuf
    mine = pl.ds(pl.multiple_of(core * (RANK // 2), RANK // 2), RANK // 2)
    ones = jnp.ones((8, RANK), F32)
    own = lax.broadcasted_iota(jnp.int32, (RANK, RANK), 0) // (RANK // 2) == core
    for t in range(3):
        pair[t] = dot(both[t, :, RANK:], pair[t].reshape(RANK, RANK), precision=HIGH).reshape(2, RANK // 2, RANK)
        term[t, z, x, y, core] = pair[t, core]

    def tell(stage, where, peer, sem):
        return pltpu.make_async_remote_copy(norms.at[stage, where], norms.at[stage, where], n_send.at[stage, sem],
                                            n_recv.at[stage, sem], device_id=peer, device_id_type=MESH)

    def sum_norms():
        for t in range(3):
            product = pair[t].reshape(RANK, RANK)
            norms[0, core, t] = dot(ones, jnp.where(own, product * product, 0.0), NT, HIGH)
        tell(0, core, place.sibling(), 0).start()
        yield
        tell(0, 1 - core, place.sibling(), 0).wait_recv()
        total = norms[0, 0] + norms[0, 1]
        for axis in range(3):
            stage = 1 + axis
            here = place.at[axis]
            norms[stage, here] = total
            for d in (1, 2, 3):
                tell(stage, here, place.chip(axis, d), d).start()
            yield
            for d in (1, 2, 3):
                tell(stage, place.far(axis, N - d), place.chip(axis, d), d).wait_recv()
            total = (norms[stage, 0] + norms[stage, 1]) + (norms[stage, 2] + norms[stage, 3])
            if axis == 0:
                for t in range(3):
                    left = dot(zown[:, t].reshape(rows, RANK), mix[t], NT, HIGH)
                    left_ref[t] = dot(left, both[t, :, RANK:], NT, HIGH)
        scales = 1.0 / jnp.sqrt(total + 1e-6)
        for t in range(3):
            scale = scales[t, 0:1]
            left = left_ref[t]
            high, low = split(jnp.concatenate([left * 0.05, left * (scale * gain)], 0), 2)
            lhs[t] = jnp.concatenate(
                [jnp.concatenate([high, high], 1), jnp.concatenate([low, jnp.zeros_like(low)], 1)], 0)
            basis = pair[t].reshape(RANK, RANK).T * scale
            basis_ref[:, t * RANK:(t + 1) * RANK] = jnp.where(core == 0, basis[:RANK // 2], basis[RANK // 2:])
        tell(0, core, place.sibling(), 0).wait_send()
        for axis in range(3):
            for d in (1, 2, 3):
                tell(1 + axis, place.at[axis], place.chip(axis, d), d).wait_send()
        yield

    def emit(j1, j2):
        for t in range(3):
            where = place.chips(t, j1, j2)
            block = jnp.concatenate([term[(t, *chip)].reshape(RANK, RANK) for chip in where], 1)
            out = dot(lhs[t], jnp.concatenate(split(block, 2), 0))
            out = out[:RANK] + out[RANK:]
            for i, (cz, cx, cy) in enumerate(where):
                column = pl.ds(pl.multiple_of(((cz * N + cx) * N + cy) * RANK, RANK), RANK)
                tile = slice(i * RANK, (i + 1) * RANK)
                h, m, l = [parts[t, j * rows:(j + 1) * rows, column].astype(F32) for j in range(3)]
                full[t, cz, cx, cy, 0] = (h + (m + l)) - out[:rows, tile]
                full[t, cz, cx, cy, 1] = out[rows:, tile]

    norm_steps = sum_norms()
    for _ in fine_gather(place, term, sems_term, emit):
        next(norm_steps, None)


def last_kernel(both_ref, basis_in, next_ref, update_ref, basis_ref):
    t, i = pl.program_id(0), pl.program_id(1)
    count = update_ref.shape[2] // RANK
    for j in range(count):
        chip = i * count + j
        where = (t, chip // (N * N), lax.rem(chip // N, N), lax.rem(chip, N))
        next_ref[0, 0, :, j * RANK:(j + 1) * RANK] = both_ref[(*where, 0)]
        update_ref[0, :, j * RANK:(j + 1) * RANK] = both_ref[(*where, 1)]
    basis_ref[...] = basis_in[...]


def body(momentum, gradient, basis):
    momentum, gradient = momentum[0], gradient[0]
    count, rows, width = momentum.shape
    chips = (N, N, N, 2)
    dma = pltpu.SemaphoreType.DMA
    f32 = lambda *shape: jax.ShapeDtypeStruct(shape, F32)
    room = lambda *shape: pltpu.VMEM(shape, F32)
    gain = float((2048 * 8192 / RANK) ** 0.5)
    full, basis_next = pl.pallas_call(
        functools.partial(main_kernel, gain),
        name="dion",
        out_shape=[room(3, *chips, 64, RANK), room(64, 3 * RANK)],
        in_specs=[ANY] * 3,
        out_specs=[VMEM] * 2,
        scratch_shapes=[
            pltpu.VMEM((count, 3 * rows, width), BF16), room(3, *chips, 64, RANK), room(3, rows, RANK),
            pltpu.VMEM((3, 2 * RANK, 2 * RANK), BF16), room(4, N, 3, 8, RANK),
            room(4, count, rows, 512), room(4, count, rows, 512),
            room(count, rows, RANK), room(N, 3, 16, RANK), room(N, 3, 16, RANK), room(3, *chips, 16, RANK),
            pltpu.VMEM((3, 2 * RANK, 4 * rows), BF16), room(3, RANK, 2 * RANK),
            room(3, N, N, N, 64, RANK),
            room(3, 2, N, N, 32, RANK), room(3, 2, N, N, 64, RANK),
            room(3, 2, N, 32, RANK), room(3, 2, N, 64, RANK),
            room(3, 2, 32, RANK), room(3, 2, 64, RANK),
            room(3, 2, 64, RANK), room(3, 64, RANK), room(3, RANK, RANK), room(2, 3, RANK, RANK),
            pltpu.VMEM((3, 2 * RANK, 3 * RANK), BF16),
            dma((3,)), dma((2, 4)), dma((2, 4)), dma((2, 4)),
            dma, dma((N,)), dma((3, 2)), dma((3, 2, 2)), dma, dma, dma, dma, dma((4, 4)), dma((4, 4))] + fine_sems() + gather_sems() + fine_sems(),
        compiler_params=pltpu.CompilerParams(collective_id=0, has_side_effects=True, vmem_limit_bytes=49 * 2 ** 20),
    )(momentum, gradient, basis)
    span = 4096
    full, basis_next = [pltpu.with_memory_space_constraint(a, pltpu.VMEM) for a in (full, basis_next)]
    return pl.pallas_call(
        last_kernel,
        name="outputs",
        grid=(3, width // span),
        out_shape=[f32(1, count, rows, width), f32(count, rows, width), f32(64, 3 * RANK)],
        in_specs=[VMEM] * 2,
        out_specs=[
            pl.BlockSpec((1, 1, rows, span), lambda t, i: (0, t, 0, i)),
            pl.BlockSpec((1, rows, span), lambda t, i: (t, 0, i)),
            pl.BlockSpec((64, 3 * RANK), lambda t, i: (0, 0)),
        ],
        compiler_params=pltpu.CompilerParams(vmem_limit_bytes=16 * 2 ** 20),
    )(full, basis_next)


def solution(mesh):
    placed = (P("rep", None, "fsdp", None), P("rep", None, "fsdp", None), P(("rep", "fsdp"), None))
    return jax.shard_map(
        body,
        mesh=mesh,
        in_specs=placed,
        out_specs=(P("rep", None, "fsdp", None), P(None, "fsdp", None), P(("rep", "fsdp"), None)),
        check_vma=False,
    )
```

```python
import functools

import jax
import jax.numpy as jnp
from jax import lax
from jax.experimental import pallas as pl
from jax.experimental.pallas import tpu as pltpu
from jax.sharding import PartitionSpec as P

MESH = pl.DeviceIdType.MESH
HIGH = lax.Precision.HIGHEST
F32 = jnp.float32
BF16 = jnp.bfloat16
RANK = 128
N = 4
ANY = pl.BlockSpec(memory_space=pl.ANY)
VMEM = pl.BlockSpec(memory_space=pltpu.VMEM)


def axis_of(third, phase):
    return (2, 1, 0)[(third + phase) % 3]


class Place:
    def __init__(self):
        self.rep = lax.axis_index("rep")
        self.fsdp = lax.axis_index("fsdp")
        self.core = lax.rem(self.fsdp, 2)
        self.at = (self.rep, lax.div(self.fsdp, 8), lax.rem(lax.div(self.fsdp, 2), N))

    def far(self, axis, distance):
        if isinstance(distance, int) and distance == 0:
            return self.at[axis]
        return lax.rem(self.at[axis] + distance, N)

    def chip(self, axis, distance):
        at = list(self.at)
        at[axis] = self.far(axis, distance)
        return (at[0], (at[1] * N + at[2]) * 2 + self.core)

    def sibling(self):
        return (self.rep, self.fsdp + 1 - 2 * self.core)

    def chips(self, t, j1, j2):
        where = [None] * 3
        where[axis_of(t, 1)] = self.far(axis_of(t, 1), dyn_off(j1))
        where[axis_of(t, 2)] = self.far(axis_of(t, 2), dyn_off(j2))
        out = []
        for i in range(N):
            where[axis_of(t, 0)] = i
            out.append(tuple(where))
        return out

    def line(self, third, middle, distance, i):
        places = []
        for t in range(3):
            where = [None] * 3
            where[axis_of(t, 0)] = i
            where[axis_of(t, 1)] = middle
            where[axis_of(t, 2)] = self.far(axis_of(t, 2), distance)
            places.append(where)
        return [jnp.where(third == 0, a, jnp.where(third == 1, b, c)) for a, b, c in zip(*places)]


def dyn_off(j):
    return OFF[j] if isinstance(j, int) else j + (j // 2) * (5 - 2 * j)


def greet(place, distances):
    barrier = pltpu.get_barrier_semaphore()
    peers = [place.sibling()] + [place.chip(axis, d) for axis, d in distances]
    for peer in peers:
        pl.semaphore_signal(barrier, inc=1, device_id=peer, device_id_type=MESH)
    pl.semaphore_wait(barrier, len(peers))


OFF = (0, 1, 3, 2)
NEAR = [(axis, d) for axis in range(3) for d in (1, 3)]


def await_landed(place, spot, sem):
    pltpu.make_async_remote_copy(spot, spot, sem, sem, device_id=place.sibling(), device_id_type=MESH).wait_recv()


def await_sent(place, spot, sem):
    pltpu.make_async_remote_copy(spot, spot, sem, sem, device_id=place.sibling(), device_id_type=MESH).wait_send()


def gather_sems():
    dma = pltpu.SemaphoreType.DMA
    return [dma((3,)), dma((3, 4)), dma((3, 2)), dma, dma((7,))]


def gather(place, buf, sems, hook=None):
    sent, recv_a, recv_b, sent_d, recv_d = sems
    core = place.core
    half = buf.shape[5] // 2
    thirds = range(3)

    def spot(t, p, distance, whose, part=None, middle=slice(None)):
        where = [None] * 3
        for q in range(3):
            axis = axis_of(t, q)
            if q < p:
                where[axis] = middle if q == 1 else slice(None)
            elif q == p:
                where[axis] = place.far(axis, distance)
            else:
                where[axis] = place.at[axis]
        return buf.at[(t, *where, whose, slice(None) if part is None else pl.ds(part * half, half))]

    def send(t, p, d, block, sem):
        pltpu.make_async_remote_copy(
            block, block, sent.at[p], sem,
            device_id=place.chip(axis_of(t, p), 1 if d == 0 else 3), device_id_type=MESH).start()

    def share(block, n):
        pltpu.make_async_remote_copy(
            block, block, sent_d, recv_d.at[n], device_id=place.sibling(), device_id_type=MESH).start()

    def size(p, whose, pieces=N):
        if p == 0:
            return buf.at[:, 0, 0, 0, whose]
        if p == 1:
            return buf.at[:, 0, 0, :, whose]
        return buf.at[:, 0, pl.ds(0, pieces), :, whose]

    came = (3, 1)
    for p in (0, 1):
        for t in thirds:
            for d in range(2):
                send(t, p, d, spot(t, p, 0, core), recv_a.at[p, d])
        yield
        for d in range(2):
            await_landed(place, size(p, core), recv_a.at[p, d])
            for t in thirds:
                send(t, p, d, spot(t, p, came[d], core, d), recv_b.at[p, 0])
        yield
        await_landed(place, size(p, core), recv_b.at[p, 0])
    run = hook if hook is not None else lambda *_: None
    piece = lambda c: pl.ds(2 * c, 2)
    for c in range(2):
        for t in thirds:
            for d in range(2):
                send(t, 2, d, spot(t, 2, 0, core, None, piece(c)), recv_a.at[2, 2 * c + d])
    for t in thirds:
        share(spot(t, 2, 0, core), 0)
    yield
    await_landed(place, size(2, 1 - core), recv_d.at[0])
    run(0, 0, N)
    for c in range(2):
        for d in range(2):
            await_landed(place, size(2, core, 2), recv_a.at[2, 2 * c + d])
            for t in thirds:
                send(t, 2, d, spot(t, 2, came[d], core, d, piece(c)), recv_b.at[2, c])
        for d in range(2):
            for t in thirds:
                share(spot(t, 2, came[d], core, None, piece(c)), 1 + 2 * c + d)
        yield
        if c == 0:
            for d in range(2):
                await_landed(place, size(2, 1 - core, 2), recv_d.at[1 + d])
                run(came[d], 0, 2)
    for c in range(2):
        await_landed(place, size(2, core, 2), recv_b.at[2, c])
        for t in thirds:
            share(spot(t, 2, 2, core, None, piece(c)), 5 + c)
        await_landed(place, size(2, 1 - core, 2), recv_d.at[3 + c])
        run(came[c], 2, 2)
    for c in range(2):
        await_landed(place, size(2, 1 - core, 2), recv_d.at[5 + c])
        run(2, 2 * c, 2)
    await_sent(place, buf.at[:, 0, 0, pl.ds(0, 3), core], sent.at[0])
    await_sent(place, buf.at[:, 0, pl.ds(0, 3), :, core], sent.at[1])
    await_sent(place, buf.at[:, pl.ds(0, 3), :, :, core], sent.at[2])
    await_sent(place, buf.at[:, :, :, :, core], sent_d)


def fine_sems():
    dma = pltpu.SemaphoreType.DMA
    return [dma((3, 3, 4, 2))] * 4 + [dma((3, 4, 4))] * 2


def fine_gather(place, buf, sems, hook):
    send_a, recv_a, send_b, recv_b, send_d, recv_d = sems
    core = place.core
    rows = buf.shape[5]
    half = rows // 2

    def index(t, p, j, da, part=None):
        where = [None] * 3
        for q in range(3):
            axis = axis_of(t, q)
            if q < p - 1:
                where[axis] = slice(None)
            elif q == p - 1:
                where[axis] = place.far(axis, dyn_off(j))
            elif q == p:
                where[axis] = place.far(axis, da)
            else:
                where[axis] = place.at[axis]
        span = slice(None) if part is None else pl.ds(part * half, half)
        return (t, *where, core, span)

    def copy_a(t, p, j, d, da):
        spot = buf.at[index(t, p, j, da)]
        return pltpu.make_async_remote_copy(
            spot, spot, send_a.at[t, p, j, d], recv_a.at[t, p, j, d],
            device_id=place.chip(axis_of(t, p), 1 if d == 0 else 3), device_id_type=MESH)

    def copy_b(t, p, j, d, da):
        spot = buf.at[index(t, p, j, da, d)]
        return pltpu.make_async_remote_copy(
            spot, spot, send_b.at[t, p, j, d], recv_b.at[t, p, j, d],
            device_id=place.chip(axis_of(t, p), 1 if d == 0 else 3), device_id_type=MESH)

    def copy_d(t, j1, j2, whose):
        where = [None] * 3
        where[axis_of(t, 0)] = slice(None)
        where[axis_of(t, 1)] = place.far(axis_of(t, 1), dyn_off(j1))
        where[axis_of(t, 2)] = place.far(axis_of(t, 2), dyn_off(j2))
        spot = buf.at[(t, *where, whose)]
        return pltpu.make_async_remote_copy(
            spot, spot, send_d.at[t, j1, j2], recv_d.at[t, j1, j2],
            device_id=place.sibling(), device_id_type=MESH)

    def start_a(t, p, j):
        for d in range(2):
            copy_a(t, p, j, d, 0).start()

    def land_a(t, p, j, d):
        copy_a(t, p, j, d, 3 if d == 0 else 1).wait_recv()
        copy_b(t, p, j, d, 3 if d == 0 else 1).start()

    def land_b(t, p, j):
        for d in range(2):
            copy_b(t, p, j, d, 2).wait_recv()

    def line_done(j1, j2):
        for t in range(3):
            copy_d(t, j1, j2, 1 - core).wait_recv()
        hook(j1, j2)

    thirds = range(3)
    for t in thirds:
        start_a(t, 0, 0)
    for t in thirds:
        start_a(t, 1, 0)
    yield
    for d in range(2):
        for t in thirds:
            land_a(t, 0, 0, d)
            start_a(t, 1, 2 - d)
    yield
    for t in thirds:
        land_b(t, 0, 0)
        start_a(t, 1, 3)
    for t in thirds:
        start_a(t, 2, 0)
        copy_d(t, 0, 0, core).start()
    yield
    for j in range(4):
        for t in thirds:
            for d in range(2):
                land_a(t, 1, j, d)
        yield
    for j1 in (1, 2):
        for t in thirds:
            start_a(t, 2, j1)
            copy_d(t, j1, 0, core).start()
    for j in range(4):
        for t in thirds:
            land_b(t, 1, j)
    for t in thirds:
        start_a(t, 2, 3)
        copy_d(t, 3, 0, core).start()
    yield

    @pl.loop(0, 4)
    def _(j):
        for t in thirds:
            for d in range(2):
                land_a(t, 2, j, d)
                copy_d(t, j, 2 - d, core).start()
        line_done(j, 0)

        @pl.when(j >= 1)
        def _():
            line_done(j - 1, 1)
            line_done(j - 1, 2)

    line_done(3, 1)
    line_done(3, 2)

    @pl.loop(0, 4)
    def _(j):
        for t in thirds:
            land_b(t, 2, j)
            copy_d(t, j, 3, core).start()
        pl.when(j >= 1)(lambda: line_done(j - 1, 3))

    line_done(3, 3)
    for t in thirds:
        for p in range(3):
            for j in range(1 if p == 0 else 4):
                for d in range(2):
                    copy_a(t, p, j, d, 0).wait_send()
                    copy_b(t, p, j, d, 3 if d == 0 else 1).wait_send()

    @pl.loop(0, 4)
    def _(j1):
        @pl.loop(0, 4)
        def _(j2):
            for t in thirds:
                copy_d(t, j1, j2, core).wait_send()


def split(values, parts):
    out = []
    for _ in range(parts):
        out.append(values.astype(BF16))
        values = values - out[-1].astype(F32)
    return out


def dot(left, right, dims=((1,), (0,)), precision=None):
    return lax.dot_general(left, right, (dims, ((), ())), precision=precision, preferred_element_type=F32)


NT = ((1,), (1,))
TN = ((0,), (0,))


def factor_block(both, step):
    count, size, _ = both.shape
    block, piece = 16, 8
    lane = lax.broadcasted_iota(jnp.int32, (count, block, size), 2)
    base = pl.multiple_of(step * block, block)
    band = both[:, pl.ds(base, block), :]
    upper, lower = band[:, :, :size], band[:, :, size:]
    inverses, done = [], []
    for part in range(block // piece):
        rows = block - part * piece
        shape = (count, rows, size)
        sub = lax.broadcasted_iota(jnp.int32, shape, 1)
        spread = lambda a, i: jnp.broadcast_to(a[:, i:i + 1, :], shape)
        turned = jnp.stack([pltpu.roll(upper[k], lax.rem(size - base, size), 1) for k in range(count)])
        columns = [jnp.broadcast_to(turned[:, :, part * piece + i:part * piece + i + 1], shape) for i in range(piece)]
        inverse = jnp.zeros((count, piece, size), F32)
        for i in range(piece):
            pivot = jnp.broadcast_to(columns[i][:, i:i + 1, :], (count, piece, size))
            recip = pl.reciprocal(pivot, approx=True)
            recip = recip * (2.0 - pivot * recip)
            recip = recip * (2.0 - pivot * recip)
            inverse = jnp.where(sub[:, :piece] == i, recip, inverse)
            factor = jnp.where(sub > i, columns[i] * jnp.concatenate([recip] * (rows // piece), 1), 0.0)
            for q in range(i + 1, piece):
                columns[q] = columns[q] - factor * spread(columns[q], i)
            upper = upper - factor * spread(upper, i)
            lower = lower - factor * spread(lower, i)
        inverses.append(inverse)
        done.append((upper[:, :piece], lower[:, :piece]))
        upper, lower = upper[:, piece:], lower[:, piece:]
    upper, lower = [jnp.concatenate(half, 1) for half in zip(*done)]
    inverse = jnp.concatenate(inverses, 1)
    factors = jnp.where(lane >= base + block, upper * inverse, 0.0)
    rows = jnp.concatenate([upper, lower], 2)
    less = []
    for k in range(count):
        h, m, l = split(factors[k], 3)
        first = jnp.concatenate([h, h, h, m, m, l], 0)
        h, m, l = split(rows[k], 3)
        less.append(dot(first, jnp.concatenate([h, m, l, h, m, h], 0), TN))
    for k in range(count):
        both[k] = both[k] - less[k]
    both[:, pl.ds(base, block), :] = jnp.concatenate([upper, lower * jnp.sqrt(inverse)], 2)


def main_kernel(gain, m_hbm, g_hbm, q_hbm, full, basis_ref, parts, qbuf, left_ref, lhs, norms,
                mbuf, gbuf, part, zbuf, zown, raw, stacked, both, other,
                ra0, rb0, ra1, rb1, ra2, rb2, pair, held, inv, wide,
                q_sem, load_sem, z_send, z_recv, d_send, d_recv, s_send, s_recv, x_send, x_recv, g_send, g_recv, n_send, n_recv, *sems):
    place = Place()
    z, x, y = place.at
    core = place.core
    sems_q, sems_raw, sems_term = sems[:6], sems[6:11], sems[11:]
    count, stack_rows, width = parts.shape
    slots, _, rows, span = mbuf.shape
    chunks = width // span

    def columns(i):
        return pl.ds(pl.multiple_of(i * span, span), span)

    def load(i):
        slot = lax.rem(i, slots)
        return (pltpu.make_async_copy(m_hbm.at[:, :, columns(i)], mbuf.at[slot], load_sem.at[0, slot]),
                pltpu.make_async_copy(g_hbm.at[:, :, columns(i)], gbuf.at[slot], load_sem.at[1, slot]))

    def blend(first, last):
        @pl.loop(first, last)
        def _(i):
            slot = lax.rem(i, slots)
            for copy in load(i):
                copy.wait()
            for t in range(count):
                parts[t, :, columns(i)] = jnp.concatenate(split(mbuf[slot, t] + gbuf[slot, t], 3), 0)

            @pl.when(i + slots < chunks)
            def _():
                for copy in load(i + slots):
                    copy.start()

    loads = [pltpu.make_async_copy(q_hbm.at[:, pl.ds(t * RANK, RANK)], qbuf.at[t, z, x, y, core], q_sem.at[t])
             for t in range(3)]
    for copy in loads:
        copy.start()
    for i in range(slots):
        for copy in load(i):
            copy.start()
    greet(place, NEAR + [(0, 2), (1, 2), (2, 2)])
    for copy in loads:
        copy.wait()
    part[...] = jnp.zeros_like(part)

    def hook(j1, j2):
        for t in range(3):
            left, right = [], []
            for cz, cx, cy in place.chips(t, j1, j2):
                column = pl.multiple_of(((cz * N + cx) * N + cy) * RANK, RANK)
                left.append(parts[t, :, pl.ds(column, RANK)])
                right.append(qbuf[t, cz, cx, cy].reshape(RANK, RANK))
            left = jnp.concatenate(left, 1)
            h, m, l = split(jnp.concatenate(right, 0), 3)
            out = dot(left, jnp.concatenate([h, m], 1))
            tile = lambda i, j: out[i * rows:(i + 1) * rows, j * RANK:(j + 1) * RANK]
            small = (tile(2, 0) + tile(1, 1)) + dot(left[:rows], l)
            part[t] += (small + (tile(1, 0) + tile(0, 1))) + tile(0, 0)

    done = 0
    for _ in fine_gather(place, qbuf, sems_q, hook):
        if done < chunks:
            blend(done, min(done + 2, chunks))
            done += 2

    quarter = rows // N
    sends = []
    for d in (1, 2, 3):
        to = place.far(0, d)
        sends.append(pltpu.make_async_remote_copy(
            part.at[:, pl.ds(pl.multiple_of(to * quarter, quarter), quarter)], zbuf.at[d],
            z_send.at[0, d], z_recv.at[0, d], device_id=place.chip(0, d), device_id_type=MESH))
        sends[-1].start()
    zbuf[0] = part[:, pl.ds(pl.multiple_of(z * quarter, quarter), quarter)]
    for send in sends:
        send.wait_recv()
    total = ((zbuf[0] + zbuf[1]) + (zbuf[2] + zbuf[3])) * (1.0 / N)
    zown[z] = total
    for t in range(3):
        raw[t, z, x, y, core] = total[t]
    for d in (1, 2, 3):
        sends.append(pltpu.make_async_remote_copy(
            zown.at[z], zown.at[z], z_send.at[1, d], z_recv.at[1, d],
            device_id=place.chip(0, d), device_id_type=MESH))
        sends[-1].start()
    rest = gather(place, raw, sems_raw)
    next(rest)
    for d in (1, 2, 3):
        spot = zown.at[place.far(0, N - d)]
        pltpu.make_async_remote_copy(spot, spot, z_send.at[1, d], z_recv.at[1, d],
                                     device_id=place.chip(0, d), device_id_type=MESH).wait_recv()
    eye = (lax.broadcasted_iota(jnp.int32, (RANK, RANK), 0) == lax.broadcasted_iota(jnp.int32, (RANK, RANK), 1)).astype(F32)
    for t in range(3):
        h, m, l = [p.astype(F32) for p in split(zown[:, t].reshape(rows, RANK), 3)]
        none = jnp.zeros_like(h)
        pairs = [jnp.concatenate(pair, 1) for pair in ((h, l), (h, m), (h, none), (m, none))]
        stacked[t] = jnp.concatenate(pairs, 0).T.astype(BF16)

    half = RANK // 4

    def plane(t, distance, whose, part=None):
        where = [slice(None)] * 3
        where[axis_of(t, 2)] = place.far(axis_of(t, 2), distance)
        return (t, *where, whose, slice(None) if part is None else pl.ds(part * half, half))

    def line(t, distance, part=None):
        where = list(place.at)
        where[axis_of(t, 0)] = slice(None)
        where[axis_of(t, 1)] = place.far(axis_of(t, 1), distance)
        return (t, *where, core, slice(None) if part is None else pl.ds(part * half, half))

    def unit(t, distance, part=None):
        where = list(place.at)
        where[axis_of(t, 0)] = place.far(axis_of(t, 0), distance)
        return (t, *where, core, slice(None) if part is None else pl.ds(part * half, half))

    spots = (plane, line, unit)
    went = (1, 3)
    first, whole = (ra0, ra1, ra2), (rb0, rb1, rb2)

    def swap(t, n, distance):
        where = plane(t, distance, 1 - core)
        pltpu.make_async_remote_copy(
            full.at[where], other.at[where[:4]], d_send, d_recv.at[n],
            device_id=place.sibling(), device_id_type=MESH).start()

    def block(t, step, distance, part=None):
        return plane(t, distance, core, part) if step == 0 else spots[step](t, distance, part)

    def start(step, kind, d):
        for t in range(3):
            src = block(t, step, 2, d) if kind == 0 else block(t, step, went[d])
            dst = (first, whole)[kind][step].at[t, d]
            pltpu.make_async_remote_copy(
                full.at[src], dst, s_send.at[step, kind], s_recv.at[step, kind, d],
                device_id=place.chip(axis_of(t, 2 - step), 1 if d == 0 else 3), device_id_type=MESH).start()

    def take_first(step, d):
        await_landed(place, first[step].at[:, d], s_recv.at[step, 0, d])
        for t in range(3):
            here = block(t, step, went[d], d)
            full[here] = full[here] + first[step][t, d]
        start(step, 1, d)

    def take_whole(step):
        for d in range(2):
            await_landed(place, whole[step].at[:, d], s_recv.at[step, 1, d])
        for t in range(3):
            here = block(t, step, 0)
            full[here] = full[here] + (whole[step][t, 0] + whole[step][t, 1])

    def multiply(t, middle, distance):
        where = [place.line(t, middle, distance, c) for c in range(N)]
        right = [parts[t, :, pl.ds(pl.multiple_of(((cz * N + cx) * N + cy) * RANK, RANK), RANK)] for cz, cx, cy in where]
        right = jnp.concatenate(right, 1)
        out = dot(stacked[t], jnp.concatenate([right, right[:rows]], 0))
        out = out[:RANK] + out[RANK:]
        for c, (cz, cx, cy) in enumerate(where):
            full[t, cz, cx, cy] = out[:, c * RANK:(c + 1) * RANK].reshape(2, RANK // 2, RANK)

    def multiply_plane(n, distance):
        @pl.loop(0, 3)
        def _(t):
            for middle in range(N):
                multiply(t, middle, distance)
        for t in range(3):
            swap(t, n, distance)

    def settle(n, distance):
        await_landed(place, other.at[:, 0], d_recv.at[n])

        @pl.loop(0, 3 * N)
        def _(i):
            t, middle = i // N, lax.rem(i, N)
            for c in range(N):
                cz, cx, cy = place.line(t, middle, distance, c)
                full[t, cz, cx, cy, core] += other[t, cz, cx, cy]

    order = (2, 3, 1, 0)
    multiply_plane(0, 2)
    next(rest, None)
    next(rest, None)
    multiply_plane(1, 3)
    settle(0, 2)
    start(0, 0, 0)
    start(0, 0, 1)
    next(rest, None)
    multiply_plane(2, 1)
    next(rest, None)
    settle(1, 3)
    for _ in rest:
        pass
    take_first(0, 1)
    settle(2, 1)
    take_first(0, 0)

    def ring_ends():
        take_whole(0)
        start(1, 0, 0)
        start(1, 0, 1)
        yield
        take_first(1, 0)
        take_first(1, 1)
        yield
        take_whole(1)
        start(2, 0, 0)
        start(2, 0, 1)
        yield
        take_first(2, 0)
        take_first(2, 1)
        yield
        take_whole(2)
        for t in range(3):
            held[t] = full[unit(t, 0)]
            pair[t, core] = held[t]
        half_swap.start()
        yield

    half_swap = pltpu.make_async_remote_copy(
        held, pair.at[:, core], x_send, x_recv, device_id=place.sibling(), device_id_type=MESH)

    mine_k = lax.rem(z, 3)

    def grams(inverse):
        if inverse:
            h, m, l = split(inv[0, z].T, 3)
            wide[...] = jnp.concatenate([jnp.concatenate([h, m, l], 1), jnp.concatenate([m, h, h], 1)], 0)

        def add(i, grams):
            whole, low = grams
            some = raw[mine_k, i].reshape(512, RANK)
            if inverse:
                h, m, l = split(some, 3)
                main = dot(jnp.concatenate([h, m], 1), wide[:, :2 * RANK])
                rest = dot(jnp.concatenate([h, l], 1), wide[:, 2 * RANK:])
                some = main[:, :RANK] + (main[:, RANK:] + rest)
            all_ = dot(jnp.concatenate(split(some.T, 3), 0), jnp.concatenate(split(some, 2), 1))
            tile = lambda i, j: all_[i * RANK:(i + 1) * RANK, j * RANK:(j + 1) * RANK]
            return whole + (tile(0, 0) + ((tile(0, 1) + tile(1, 0)) + tile(1, 1))), low + tile(2, 0)

        zero = jnp.zeros((RANK, RANK), F32)
        whole, low = lax.fori_loop(0, N, add, (zero, zero))
        both[0, :, :RANK] = whole + (low + low.T)
        both[0, :, RANK:] = eye

    def pass_on(sweep, d, whose):
        return pltpu.make_async_remote_copy(inv.at[sweep, whose], inv.at[sweep, whose], g_send.at[sweep, d],
                                            g_recv.at[sweep, d], device_id=place.chip(0, d), device_id_type=MESH)

    def publish(sweep):
        inv[sweep, z] = both[0, :, RANK:]
        for d in (1, 2, 3):
            pass_on(sweep, d, z).start()

    def learn(sweep):
        for d in (1, 2, 3):
            pass_on(sweep, d, place.far(0, N - d)).wait_recv()

    grams(False)
    ends = ring_ends()

    @pl.loop(0, N)
    def _(i):
        for t in range(3):
            multiply(t, i, 0)
        factor_block(both, i)

    for t in range(3):
        swap(t, 3, 0)
    pl.loop(N, 8)(lambda i: factor_block(both, i))
    settle(3, 0)
    next(ends)
    publish(0)
    grams(True)
    for i in (0, 2, 4):
        next(ends)
        pl.loop(i, i + 2)(lambda i: factor_block(both, i))
    next(ends)
    factor_block(both, 6)
    await_landed(place, pair.at[:, 1 - core], x_recv)
    learn(0)
    for t in range(3):
        pair[t] = dot(inv[0, t] * (1.0 / N), pair[t].reshape(RANK, RANK), precision=HIGH).reshape(2, RANK // 2, RANK)
    factor_block(both, 7)
    publish(1)
    half_swap.wait_send()
    for send in sends:
        send.wait_send()
    for step in range(3):
        await_sent(place, first[step], s_send.at[step, 0])
        await_sent(place, whole[step], s_send.at[step, 1])
    await_sent(place, other, d_send)

    learn(1)

    term = qbuf
    mine = pl.ds(pl.multiple_of(core * (RANK // 2), RANK // 2), RANK // 2)
    ones = jnp.ones((8, RANK), F32)
    own = lax.broadcasted_iota(jnp.int32, (RANK, RANK), 0) // (RANK // 2) == core
    for t in range(3):
        pair[t] = dot(inv[1, t], pair[t].reshape(RANK, RANK), precision=HIGH).reshape(2, RANK // 2, RANK)
        term[t, z, x, y, core] = pair[t, core]

    def tell(stage, where, peer, sem):
        return pltpu.make_async_remote_copy(norms.at[stage, where], norms.at[stage, where], n_send.at[stage, sem],
                                            n_recv.at[stage, sem], device_id=peer, device_id_type=MESH)

    def sum_norms():
        for t in range(3):
            product = pair[t].reshape(RANK, RANK)
            norms[0, core, t] = dot(ones, jnp.where(own, product * product, 0.0), NT, HIGH)
        tell(0, core, place.sibling(), 0).start()
        yield
        tell(0, 1 - core, place.sibling(), 0).wait_recv()
        total = norms[0, 0] + norms[0, 1]
        for axis in range(3):
            stage = 1 + axis
            here = place.at[axis]
            norms[stage, here] = total
            for d in (1, 2, 3):
                tell(stage, here, place.chip(axis, d), d).start()
            yield
            for d in (1, 2, 3):
                tell(stage, place.far(axis, N - d), place.chip(axis, d), d).wait_recv()
            total = (norms[stage, 0] + norms[stage, 1]) + (norms[stage, 2] + norms[stage, 3])
            if axis == 0:
                for t in range(3):
                    left = dot(zown[:, t].reshape(rows, RANK), inv[0, t], NT, HIGH)
                    left_ref[t] = dot(left, inv[1, t], NT, HIGH)
        scales = 1.0 / jnp.sqrt(total + 1e-6)
        for t in range(3):
            scale = scales[t, 0:1]
            left = left_ref[t]
            high, low = split(jnp.concatenate([left * 0.05, left * (scale * gain)], 0), 2)
            lhs[t] = jnp.concatenate(
                [jnp.concatenate([high, high], 1), jnp.concatenate([low, jnp.zeros_like(low)], 1)], 0)
            basis = pair[t].reshape(RANK, RANK).T * scale
            basis_ref[:, t * RANK:(t + 1) * RANK] = jnp.where(core == 0, basis[:RANK // 2], basis[RANK // 2:])
        for sweep in range(2):
            for d in (1, 2, 3):
                pass_on(sweep, d, z).wait_send()
        tell(0, core, place.sibling(), 0).wait_send()
        for axis in range(3):
            for d in (1, 2, 3):
                tell(1 + axis, place.at[axis], place.chip(axis, d), d).wait_send()
        yield

    def emit(j1, j2):
        for t in range(3):
            where = place.chips(t, j1, j2)
            block = jnp.concatenate([term[(t, *chip)].reshape(RANK, RANK) for chip in where], 1)
            out = dot(lhs[t], jnp.concatenate(split(block, 2), 0))
            out = out[:RANK] + out[RANK:]
            for i, (cz, cx, cy) in enumerate(where):
                column = pl.ds(pl.multiple_of(((cz * N + cx) * N + cy) * RANK, RANK), RANK)
                tile = slice(i * RANK, (i + 1) * RANK)
                h, m, l = [parts[t, j * rows:(j + 1) * rows, column].astype(F32) for j in range(3)]
                full[t, cz, cx, cy, 0] = (h + (m + l)) - out[:rows, tile]
                full[t, cz, cx, cy, 1] = out[rows:, tile]

    norm_steps = sum_norms()
    for _ in fine_gather(place, term, sems_term, emit):
        next(norm_steps, None)


def last_kernel(both_ref, basis_in, next_ref, update_ref, basis_ref):
    t, i = pl.program_id(0), pl.program_id(1)
    count = update_ref.shape[2] // RANK
    for j in range(count):
        chip = i * count + j
        where = (t, chip // (N * N), lax.rem(chip // N, N), lax.rem(chip, N))
        next_ref[0, 0, :, j * RANK:(j + 1) * RANK] = both_ref[(*where, 0)]
        update_ref[0, :, j * RANK:(j + 1) * RANK] = both_ref[(*where, 1)]
    basis_ref[...] = basis_in[...]


def body(momentum, gradient, basis):
    momentum, gradient = momentum[0], gradient[0]
    count, rows, width = momentum.shape
    chips = (N, N, N, 2)
    dma = pltpu.SemaphoreType.DMA
    f32 = lambda *shape: jax.ShapeDtypeStruct(shape, F32)
    room = lambda *shape: pltpu.VMEM(shape, F32)
    gain = float((2048 * 8192 / RANK) ** 0.5)
    full, basis_next = pl.pallas_call(
        functools.partial(main_kernel, gain),
        name="dion",
        out_shape=[room(3, *chips, 64, RANK), room(64, 3 * RANK)],
        in_specs=[ANY] * 3,
        out_specs=[VMEM] * 2,
        scratch_shapes=[
            pltpu.VMEM((count, 3 * rows, width), BF16), room(3, *chips, 64, RANK), room(3, rows, RANK),
            pltpu.VMEM((3, 2 * RANK, 2 * RANK), BF16), room(4, N, 3, 8, RANK),
            room(4, count, rows, 512), room(4, count, rows, 512),
            room(count, rows, RANK), room(N, 3, 16, RANK), room(N, 3, 16, RANK), room(3, *chips, 16, RANK),
            pltpu.VMEM((3, 2 * RANK, 4 * rows), BF16), room(1, RANK, 2 * RANK),
            room(3, N, N, N, 64, RANK),
            room(3, 2, N, N, 32, RANK), room(3, 2, N, N, 64, RANK),
            room(3, 2, N, 32, RANK), room(3, 2, N, 64, RANK),
            room(3, 2, 32, RANK), room(3, 2, 64, RANK),
            room(3, 2, 64, RANK), room(3, 64, RANK), room(2, N, RANK, RANK),
            pltpu.VMEM((2 * RANK, 3 * RANK), BF16),
            dma((3,)), dma((2, 4)), dma((2, 4)), dma((2, 4)),
            dma, dma((N,)), dma((3, 2)), dma((3, 2, 2)), dma, dma, dma((2, 4)), dma((2, 4)), dma((4, 4)), dma((4, 4))] + fine_sems() + gather_sems() + fine_sems(),
        compiler_params=pltpu.CompilerParams(collective_id=0, has_side_effects=True, vmem_limit_bytes=49 * 2 ** 20),
    )(momentum, gradient, basis)
    span = 4096
    full, basis_next = [pltpu.with_memory_space_constraint(a, pltpu.VMEM) for a in (full, basis_next)]
    return pl.pallas_call(
        last_kernel,
        name="outputs",
        grid=(3, width // span),
        out_shape=[f32(1, count, rows, width), f32(count, rows, width), f32(64, 3 * RANK)],
        in_specs=[VMEM] * 2,
        out_specs=[
            pl.BlockSpec((1, 1, rows, span), lambda t, i: (0, t, 0, i)),
            pl.BlockSpec((1, rows, span), lambda t, i: (t, 0, i)),
            pl.BlockSpec((64, 3 * RANK), lambda t, i: (0, 0)),
        ],
        compiler_params=pltpu.CompilerParams(vmem_limit_bytes=16 * 2 ** 20),
    )(full, basis_next)


def solution(mesh):
    placed = (P("rep", None, "fsdp", None), P("rep", None, "fsdp", None), P(("rep", "fsdp"), None))
    return jax.shard_map(
        body,
        mesh=mesh,
        in_specs=placed,
        out_specs=(P("rep", None, "fsdp", None), P(None, "fsdp", None), P(("rep", "fsdp"), None)),
        check_vma=False,
    )
```

```python
import functools

import jax
import jax.numpy as jnp
from jax import lax
from jax.experimental import pallas as pl
from jax.experimental.pallas import tpu as pltpu
from jax.sharding import PartitionSpec as P

MESH = pl.DeviceIdType.MESH
HIGH = lax.Precision.HIGHEST
F32 = jnp.float32
BF16 = jnp.bfloat16
RANK = 128
N = 4
ANY = pl.BlockSpec(memory_space=pl.ANY)
VMEM = pl.BlockSpec(memory_space=pltpu.VMEM)


def axis_of(third, phase):
    return (2, 1, 0)[(third + phase) % 3]


class Place:
    def __init__(self):
        self.rep = lax.axis_index("rep")
        self.fsdp = lax.axis_index("fsdp")
        self.core = lax.rem(self.fsdp, 2)
        self.at = (self.rep, lax.div(self.fsdp, 8), lax.rem(lax.div(self.fsdp, 2), N))

    def far(self, axis, distance):
        if isinstance(distance, int) and distance == 0:
            return self.at[axis]
        return lax.rem(self.at[axis] + distance, N)

    def chip(self, axis, distance):
        at = list(self.at)
        at[axis] = self.far(axis, distance)
        return (at[0], (at[1] * N + at[2]) * 2 + self.core)

    def sibling(self):
        return (self.rep, self.fsdp + 1 - 2 * self.core)

    def chips(self, t, j1, j2):
        where = [None] * 3
        where[axis_of(t, 1)] = self.far(axis_of(t, 1), dyn_off(j1))
        where[axis_of(t, 2)] = self.far(axis_of(t, 2), dyn_off(j2))
        out = []
        for i in range(N):
            where[axis_of(t, 0)] = i
            out.append(tuple(where))
        return out

    def line(self, third, middle, distance, i):
        places = []
        for t in range(3):
            where = [None] * 3
            where[axis_of(t, 0)] = i
            where[axis_of(t, 1)] = middle
            where[axis_of(t, 2)] = self.far(axis_of(t, 2), distance)
            places.append(where)
        return [jnp.where(third == 0, a, jnp.where(third == 1, b, c)) for a, b, c in zip(*places)]


def dyn_off(j):
    return OFF[j] if isinstance(j, int) else j + (j // 2) * (5 - 2 * j)


def greet(place, distances):
    barrier = pltpu.get_barrier_semaphore()
    peers = [place.sibling()] + [place.chip(axis, d) for axis, d in distances]
    for peer in peers:
        pl.semaphore_signal(barrier, inc=1, device_id=peer, device_id_type=MESH)
    pl.semaphore_wait(barrier, len(peers))


OFF = (0, 1, 3, 2)
NEAR = [(axis, d) for axis in range(3) for d in (1, 3)]


def await_landed(place, spot, sem):
    pltpu.make_async_remote_copy(spot, spot, sem, sem, device_id=place.sibling(), device_id_type=MESH).wait_recv()


def await_sent(place, spot, sem):
    pltpu.make_async_remote_copy(spot, spot, sem, sem, device_id=place.sibling(), device_id_type=MESH).wait_send()


def gather_sems():
    dma = pltpu.SemaphoreType.DMA
    return [dma((3,)), dma((3, 4)), dma((3, 2)), dma, dma((7,))]


def gather(place, buf, sems, hook=None):
    sent, recv_a, recv_b, sent_d, recv_d = sems
    core = place.core
    half = buf.shape[5] // 2
    thirds = range(3)

    def spot(t, p, distance, whose, part=None, middle=slice(None)):
        where = [None] * 3
        for q in range(3):
            axis = axis_of(t, q)
            if q < p:
                where[axis] = middle if q == 1 else slice(None)
            elif q == p:
                where[axis] = place.far(axis, distance)
            else:
                where[axis] = place.at[axis]
        return buf.at[(t, *where, whose, slice(None) if part is None else pl.ds(part * half, half))]

    def send(t, p, d, block, sem):
        pltpu.make_async_remote_copy(
            block, block, sent.at[p], sem,
            device_id=place.chip(axis_of(t, p), 1 if d == 0 else 3), device_id_type=MESH).start()

    def share(block, n):
        pltpu.make_async_remote_copy(
            block, block, sent_d, recv_d.at[n], device_id=place.sibling(), device_id_type=MESH).start()

    def size(p, whose, pieces=N):
        if p == 0:
            return buf.at[:, 0, 0, 0, whose]
        if p == 1:
            return buf.at[:, 0, 0, :, whose]
        return buf.at[:, 0, pl.ds(0, pieces), :, whose]

    came = (3, 1)
    for p in (0, 1):
        for t in thirds:
            for d in range(2):
                send(t, p, d, spot(t, p, 0, core), recv_a.at[p, d])
        yield
        for d in range(2):
            await_landed(place, size(p, core), recv_a.at[p, d])
            for t in thirds:
                send(t, p, d, spot(t, p, came[d], core, d), recv_b.at[p, 0])
        yield
        await_landed(place, size(p, core), recv_b.at[p, 0])
    run = hook if hook is not None else lambda *_: None
    piece = lambda c: pl.ds(2 * c, 2)
    for c in range(2):
        for t in thirds:
            for d in range(2):
                send(t, 2, d, spot(t, 2, 0, core, None, piece(c)), recv_a.at[2, 2 * c + d])
    for t in thirds:
        share(spot(t, 2, 0, core), 0)
    yield
    await_landed(place, size(2, 1 - core), recv_d.at[0])
    run(0, 0, N)
    for c in range(2):
        for d in range(2):
            await_landed(place, size(2, core, 2), recv_a.at[2, 2 * c + d])
            for t in thirds:
                send(t, 2, d, spot(t, 2, came[d], core, d, piece(c)), recv_b.at[2, c])
        for d in range(2):
            for t in thirds:
                share(spot(t, 2, came[d], core, None, piece(c)), 1 + 2 * c + d)
        yield
        if c == 0:
            for d in range(2):
                await_landed(place, size(2, 1 - core, 2), recv_d.at[1 + d])
                run(came[d], 0, 2)
    for c in range(2):
        await_landed(place, size(2, core, 2), recv_b.at[2, c])
        for t in thirds:
            share(spot(t, 2, 2, core, None, piece(c)), 5 + c)
        await_landed(place, size(2, 1 - core, 2), recv_d.at[3 + c])
        run(came[c], 2, 2)
    for c in range(2):
        await_landed(place, size(2, 1 - core, 2), recv_d.at[5 + c])
        run(2, 2 * c, 2)
    await_sent(place, buf.at[:, 0, 0, pl.ds(0, 3), core], sent.at[0])
    await_sent(place, buf.at[:, 0, pl.ds(0, 3), :, core], sent.at[1])
    await_sent(place, buf.at[:, pl.ds(0, 3), :, :, core], sent.at[2])
    await_sent(place, buf.at[:, :, :, :, core], sent_d)


def fine_sems():
    dma = pltpu.SemaphoreType.DMA
    return [dma((3, 3, 4, 2))] * 4 + [dma((3, 4, 4))] * 2


def fine_gather(place, buf, sems, hook):
    send_a, recv_a, send_b, recv_b, send_d, recv_d = sems
    core = place.core
    rows = buf.shape[5]
    half = rows // 2

    def index(t, p, j, da, part=None):
        where = [None] * 3
        for q in range(3):
            axis = axis_of(t, q)
            if q < p - 1:
                where[axis] = slice(None)
            elif q == p - 1:
                where[axis] = place.far(axis, dyn_off(j))
            elif q == p:
                where[axis] = place.far(axis, da)
            else:
                where[axis] = place.at[axis]
        span = slice(None) if part is None else pl.ds(part * half, half)
        return (t, *where, core, span)

    def copy_a(t, p, j, d, da):
        spot = buf.at[index(t, p, j, da)]
        return pltpu.make_async_remote_copy(
            spot, spot, send_a.at[t, p, j, d], recv_a.at[t, p, j, d],
            device_id=place.chip(axis_of(t, p), 1 if d == 0 else 3), device_id_type=MESH)

    def copy_b(t, p, j, d, da):
        spot = buf.at[index(t, p, j, da, d)]
        return pltpu.make_async_remote_copy(
            spot, spot, send_b.at[t, p, j, d], recv_b.at[t, p, j, d],
            device_id=place.chip(axis_of(t, p), 1 if d == 0 else 3), device_id_type=MESH)

    def copy_d(t, j1, j2, whose):
        where = [None] * 3
        where[axis_of(t, 0)] = slice(None)
        where[axis_of(t, 1)] = place.far(axis_of(t, 1), dyn_off(j1))
        where[axis_of(t, 2)] = place.far(axis_of(t, 2), dyn_off(j2))
        spot = buf.at[(t, *where, whose)]
        return pltpu.make_async_remote_copy(
            spot, spot, send_d.at[t, j1, j2], recv_d.at[t, j1, j2],
            device_id=place.sibling(), device_id_type=MESH)

    def start_a(t, p, j):
        for d in range(2):
            copy_a(t, p, j, d, 0).start()

    def land_a(t, p, j, d):
        copy_a(t, p, j, d, 3 if d == 0 else 1).wait_recv()
        copy_b(t, p, j, d, 3 if d == 0 else 1).start()

    def land_b(t, p, j):
        for d in range(2):
            copy_b(t, p, j, d, 2).wait_recv()

    def line_done(j1, j2):
        for t in range(3):
            copy_d(t, j1, j2, 1 - core).wait_recv()
        hook(j1, j2)

    thirds = range(3)
    for t in thirds:
        start_a(t, 0, 0)
    for t in thirds:
        start_a(t, 1, 0)
    yield
    for d in range(2):
        for t in thirds:
            land_a(t, 0, 0, d)
            start_a(t, 1, 2 - d)
    yield
    for t in thirds:
        land_b(t, 0, 0)
        start_a(t, 1, 3)
    for t in thirds:
        start_a(t, 2, 0)
        copy_d(t, 0, 0, core).start()
    yield
    for j in range(4):
        for t in thirds:
            for d in range(2):
                land_a(t, 1, j, d)
        yield
    for j1 in (1, 2):
        for t in thirds:
            start_a(t, 2, j1)
            copy_d(t, j1, 0, core).start()
    for j in range(4):
        for t in thirds:
            land_b(t, 1, j)
    for t in thirds:
        start_a(t, 2, 3)
        copy_d(t, 3, 0, core).start()
    yield

    @pl.loop(0, 4)
    def _(j):
        for t in thirds:
            for d in range(2):
                land_a(t, 2, j, d)
                copy_d(t, j, 2 - d, core).start()
        line_done(j, 0)

        @pl.when(j >= 1)
        def _():
            line_done(j - 1, 1)
            line_done(j - 1, 2)

    line_done(3, 1)
    line_done(3, 2)

    @pl.loop(0, 4)
    def _(j):
        for t in thirds:
            land_b(t, 2, j)
            copy_d(t, j, 3, core).start()
        pl.when(j >= 1)(lambda: line_done(j - 1, 3))

    line_done(3, 3)
    for t in thirds:
        for p in range(3):
            for j in range(1 if p == 0 else 4):
                for d in range(2):
                    copy_a(t, p, j, d, 0).wait_send()
                    copy_b(t, p, j, d, 3 if d == 0 else 1).wait_send()

    @pl.loop(0, 4)
    def _(j1):
        @pl.loop(0, 4)
        def _(j2):
            for t in thirds:
                copy_d(t, j1, j2, core).wait_send()


def split(values, parts):
    out = []
    for _ in range(parts):
        out.append(values.astype(BF16))
        values = values - out[-1].astype(F32)
    return out


def dot(left, right, dims=((1,), (0,)), precision=None):
    return lax.dot_general(left, right, (dims, ((), ())), precision=precision, preferred_element_type=F32)


NT = ((1,), (1,))
TN = ((0,), (0,))


def factor_block(both, step):
    count, size, _ = both.shape
    block, piece = 16, 8
    lane = lax.broadcasted_iota(jnp.int32, (count, block, size), 2)
    base = pl.multiple_of(step * block, block)
    band = both[:, pl.ds(base, block), :]
    upper, lower = band[:, :, :size], band[:, :, size:]
    inverses, done = [], []
    for part in range(block // piece):
        rows = block - part * piece
        shape = (count, rows, size)
        sub = lax.broadcasted_iota(jnp.int32, shape, 1)
        spread = lambda a, i: jnp.broadcast_to(a[:, i:i + 1, :], shape)
        turned = jnp.stack([pltpu.roll(upper[k], lax.rem(size - base, size), 1) for k in range(count)])
        columns = [jnp.broadcast_to(turned[:, :, part * piece + i:part * piece + i + 1], shape) for i in range(piece)]
        inverse = jnp.zeros((count, piece, size), F32)
        for i in range(piece):
            pivot = jnp.broadcast_to(columns[i][:, i:i + 1, :], (count, piece, size))
            recip = pl.reciprocal(pivot, approx=True)
            recip = recip * (2.0 - pivot * recip)
            recip = recip * (2.0 - pivot * recip)
            inverse = jnp.where(sub[:, :piece] == i, recip, inverse)
            factor = jnp.where(sub > i, columns[i] * jnp.concatenate([recip] * (rows // piece), 1), 0.0)
            for q in range(i + 1, piece):
                columns[q] = columns[q] - factor * spread(columns[q], i)
            upper = upper - factor * spread(upper, i)
            lower = lower - factor * spread(lower, i)
        inverses.append(inverse)
        done.append((upper[:, :piece], lower[:, :piece]))
        upper, lower = upper[:, piece:], lower[:, piece:]
    upper, lower = [jnp.concatenate(half, 1) for half in zip(*done)]
    inverse = jnp.concatenate(inverses, 1)
    factors = jnp.where(lane >= base + block, upper * inverse, 0.0)
    rows = jnp.concatenate([upper, lower], 2)
    less = []
    for k in range(count):
        h, m, l = split(factors[k], 3)
        first = jnp.concatenate([h, h, h, m, m, l], 0)
        h, m, l = split(rows[k], 3)
        less.append(dot(first, jnp.concatenate([h, m, l, h, m, h], 0), TN))
    for k in range(count):
        both[k] = both[k] - less[k]
    both[:, pl.ds(base, block), :] = jnp.concatenate([upper, lower * jnp.sqrt(inverse)], 2)


def main_kernel(gain, m_hbm, g_hbm, q_hbm, full, basis_ref, parts, qbuf, left_ref, lhs, norms,
                mbuf, gbuf, part, zbuf, zown, raw, stacked, both, other,
                ra0, rb0, ra1, rb1, ra2, rb2, pair, held, mix, sums, wide,
                q_sem, load_sem, z_send, z_recv, d_send, d_recv, s_send, s_recv, x_send, x_recv, g_send, g_recv, n_send, n_recv, *sems):
    place = Place()
    z, x, y = place.at
    core = place.core
    sems_q, sems_raw, sems_term = sems[:6], sems[6:11], sems[11:]
    count, stack_rows, width = parts.shape
    slots, _, rows, span = mbuf.shape
    chunks = width // span

    def columns(i):
        return pl.ds(pl.multiple_of(i * span, span), span)

    def load(i):
        slot = lax.rem(i, slots)
        return (pltpu.make_async_copy(m_hbm.at[:, :, columns(i)], mbuf.at[slot], load_sem.at[0, slot]),
                pltpu.make_async_copy(g_hbm.at[:, :, columns(i)], gbuf.at[slot], load_sem.at[1, slot]))

    def blend(first, last):
        @pl.loop(first, last)
        def _(i):
            slot = lax.rem(i, slots)
            for copy in load(i):
                copy.wait()
            for t in range(count):
                parts[t, :, columns(i)] = jnp.concatenate(split(mbuf[slot, t] + gbuf[slot, t], 3), 0)

            @pl.when(i + slots < chunks)
            def _():
                for copy in load(i + slots):
                    copy.start()

    loads = [pltpu.make_async_copy(q_hbm.at[:, pl.ds(t * RANK, RANK)], qbuf.at[t, z, x, y, core], q_sem.at[t])
             for t in range(3)]
    for copy in loads:
        copy.start()
    for i in range(slots):
        for copy in load(i):
            copy.start()
    greet(place, NEAR + [(0, 2), (1, 2), (2, 2)])
    for copy in loads:
        copy.wait()
    part[...] = jnp.zeros_like(part)

    def hook(j1, j2):
        for t in range(3):
            left, right = [], []
            for cz, cx, cy in place.chips(t, j1, j2):
                column = pl.multiple_of(((cz * N + cx) * N + cy) * RANK, RANK)
                left.append(parts[t, :, pl.ds(column, RANK)])
                right.append(qbuf[t, cz, cx, cy].reshape(RANK, RANK))
            left = jnp.concatenate(left, 1)
            h, m, l = split(jnp.concatenate(right, 0), 3)
            out = dot(left, jnp.concatenate([h, m], 1))
            tile = lambda i, j: out[i * rows:(i + 1) * rows, j * RANK:(j + 1) * RANK]
            small = (tile(2, 0) + tile(1, 1)) + dot(left[:rows], l)
            part[t] += (small + (tile(1, 0) + tile(0, 1))) + tile(0, 0)

    done = 0
    for _ in fine_gather(place, qbuf, sems_q, hook):
        if done < chunks:
            blend(done, min(done + 2, chunks))
            done += 2

    quarter = rows // N
    sends = []
    for d in (1, 2, 3):
        to = place.far(0, d)
        sends.append(pltpu.make_async_remote_copy(
            part.at[:, pl.ds(pl.multiple_of(to * quarter, quarter), quarter)], zbuf.at[d],
            z_send.at[0, d], z_recv.at[0, d], device_id=place.chip(0, d), device_id_type=MESH))
        sends[-1].start()
    zbuf[0] = part[:, pl.ds(pl.multiple_of(z * quarter, quarter), quarter)]
    for send in sends:
        send.wait_recv()
    total = ((zbuf[0] + zbuf[1]) + (zbuf[2] + zbuf[3])) * (1.0 / N)
    zown[z] = total
    for t in range(3):
        raw[t, z, x, y, core] = total[t]
    for d in (1, 2, 3):
        sends.append(pltpu.make_async_remote_copy(
            zown.at[z], zown.at[z], z_send.at[1, d], z_recv.at[1, d],
            device_id=place.chip(0, d), device_id_type=MESH))
        sends[-1].start()
    rest = gather(place, raw, sems_raw)
    next(rest)
    for d in (1, 2, 3):
        spot = zown.at[place.far(0, N - d)]
        pltpu.make_async_remote_copy(spot, spot, z_send.at[1, d], z_recv.at[1, d],
                                     device_id=place.chip(0, d), device_id_type=MESH).wait_recv()
    eye = (lax.broadcasted_iota(jnp.int32, (RANK, RANK), 0) == lax.broadcasted_iota(jnp.int32, (RANK, RANK), 1)).astype(F32)
    for t in range(3):
        h, m, l = [p.astype(F32) for p in split(zown[:, t].reshape(rows, RANK), 3)]
        none = jnp.zeros_like(h)
        pairs = [jnp.concatenate(pair, 1) for pair in ((h, l), (h, m), (h, none), (m, none))]
        stacked[t] = jnp.concatenate(pairs, 0).T.astype(BF16)

    half = RANK // 4

    def plane(t, distance, whose, part=None):
        where = [slice(None)] * 3
        where[axis_of(t, 2)] = place.far(axis_of(t, 2), distance)
        return (t, *where, whose, slice(None) if part is None else pl.ds(part * half, half))

    def line(t, distance, part=None):
        where = list(place.at)
        where[axis_of(t, 0)] = slice(None)
        where[axis_of(t, 1)] = place.far(axis_of(t, 1), distance)
        return (t, *where, core, slice(None) if part is None else pl.ds(part * half, half))

    def unit(t, distance, part=None):
        where = list(place.at)
        where[axis_of(t, 0)] = place.far(axis_of(t, 0), distance)
        return (t, *where, core, slice(None) if part is None else pl.ds(part * half, half))

    spots = (plane, line, unit)
    went = (1, 3)
    first, whole = (ra0, ra1, ra2), (rb0, rb1, rb2)

    def swap(t, n, distance):
        where = plane(t, distance, 1 - core)
        pltpu.make_async_remote_copy(
            full.at[where], other.at[where[:4]], d_send, d_recv.at[n],
            device_id=place.sibling(), device_id_type=MESH).start()

    def block(t, step, distance, part=None):
        return plane(t, distance, core, part) if step == 0 else spots[step](t, distance, part)

    def start(step, kind, d):
        for t in range(3):
            src = block(t, step, 2, d) if kind == 0 else block(t, step, went[d])
            dst = (first, whole)[kind][step].at[t, d]
            pltpu.make_async_remote_copy(
                full.at[src], dst, s_send.at[step, kind], s_recv.at[step, kind, d],
                device_id=place.chip(axis_of(t, 2 - step), 1 if d == 0 else 3), device_id_type=MESH).start()

    def take_first(step, d):
        await_landed(place, first[step].at[:, d], s_recv.at[step, 0, d])
        for t in range(3):
            here = block(t, step, went[d], d)
            full[here] = full[here] + first[step][t, d]
        start(step, 1, d)

    def take_whole(step):
        for d in range(2):
            await_landed(place, whole[step].at[:, d], s_recv.at[step, 1, d])
        for t in range(3):
            here = block(t, step, 0)
            full[here] = full[here] + (whole[step][t, 0] + whole[step][t, 1])

    def multiply(t, middle, distance):
        where = [place.line(t, middle, distance, c) for c in range(N)]
        right = [parts[t, :, pl.ds(pl.multiple_of(((cz * N + cx) * N + cy) * RANK, RANK), RANK)] for cz, cx, cy in where]
        right = jnp.concatenate(right, 1)
        out = dot(stacked[t], jnp.concatenate([right, right[:rows]], 0))
        out = out[:RANK] + out[RANK:]
        for c, (cz, cx, cy) in enumerate(where):
            full[t, cz, cx, cy] = out[:, c * RANK:(c + 1) * RANK].reshape(2, RANK // 2, RANK)

    def multiply_plane(n, distance):
        for t in range(3):
            @pl.loop(0, 2)
            def _(i):
                multiply(t, 2 * i, distance)
                multiply(t, 2 * i + 1, distance)
            swap(t, n, distance)
            next(rest, None)

    def settle(n, distance):
        await_landed(place, other.at[:, 0], d_recv.at[n])

        @pl.loop(0, 3 * N)
        def _(i):
            t, middle = i // N, lax.rem(i, N)
            for c in range(N):
                cz, cx, cy = place.line(t, middle, distance, c)
                full[t, cz, cx, cy, core] += other[t, cz, cx, cy]

    order = (2, 3, 1, 0)
    multiply_plane(0, 2)
    multiply_plane(1, 3)
    settle(0, 2)
    start(0, 0, 0)
    start(0, 0, 1)
    for _ in rest:
        pass
    settle(1, 3)

    def ring_ends():
        take_whole(0)
        start(1, 0, 0)
        start(1, 0, 1)
        yield
        take_first(1, 0)
        take_first(1, 1)
        yield
        take_whole(1)
        start(2, 0, 0)
        start(2, 0, 1)
        yield
        take_first(2, 0)
        take_first(2, 1)
        yield
        take_whole(2)
        for t in range(3):
            held[t] = full[unit(t, 0)]
            pair[t, core] = held[t]
        half_swap.start()
        yield

    half_swap = pltpu.make_async_remote_copy(
        held, pair.at[:, core], x_send, x_recv, device_id=place.sibling(), device_id_type=MESH)

    def grams(inverse):
        if inverse:
            for t in range(3):
                h, m, l = split(mix[t].T, 3)
                wide[t] = jnp.concatenate([jnp.concatenate([h, m, l], 1), jnp.concatenate([m, h, h], 1)], 0)

        first, many = (core * 2, 2) if inverse else (0, N)

        def add(i, grams):
            out = []
            for t in range(3):
                whole, low = grams[t]
                some = raw[t, first + i].reshape(512, RANK)
                if inverse:
                    h, m, l = split(some, 3)
                    main = dot(jnp.concatenate([h, m], 1), wide[t, :, :2 * RANK])
                    rest = dot(jnp.concatenate([h, l], 1), wide[t, :, 2 * RANK:])
                    some = main[:, :RANK] + (main[:, RANK:] + rest)
                all_ = dot(jnp.concatenate(split(some.T, 3), 0), jnp.concatenate(split(some, 2), 1))
                tile = lambda i, j: all_[i * RANK:(i + 1) * RANK, j * RANK:(j + 1) * RANK]
                out.append((whole + (tile(0, 0) + ((tile(0, 1) + tile(1, 0)) + tile(1, 1))), low + tile(2, 0)))
            return tuple(out)

        zero = jnp.zeros((RANK, RANK), F32)
        for t, (whole, low) in enumerate(lax.fori_loop(0, many, add, ((zero, zero),) * 3)):
            both[t, :, RANK:] = eye
            if inverse:
                sums[0, t] = whole + (low + low.T)
            else:
                both[t, :, :RANK] = whole + (low + low.T)
        if inverse:
            trade = pltpu.make_async_remote_copy(sums.at[0], sums.at[1], g_send, g_recv, device_id=place.sibling(),
                                                 device_id_type=MESH)
            trade.start()
            trade.wait()
            for t in range(3):
                both[t, :, :RANK] = sums[0, t] + sums[1, t]

    grams(False)
    ends = ring_ends()

    def beside(low, high, distance, shift):
        @pl.loop(low, high)
        def _(i):
            for t in range(3):
                multiply(t, i, distance)
            factor_block(both, i + shift)

    beside(0, N, 1, 0)
    for t in range(3):
        swap(t, 2, 1)
    take_first(0, 1)
    beside(0, 2, 0, N)
    settle(2, 1)
    take_first(0, 0)
    beside(2, N, 0, N)
    for t in range(3):
        swap(t, 3, 0)
    for t in range(3):
        mix[t] = both[t, :, RANK:]
    grams(True)
    settle(3, 0)
    for i in (0, 2, 4):
        next(ends)
        pl.loop(i, i + 2)(lambda i: factor_block(both, i))
    next(ends)
    factor_block(both, 6)
    next(ends)
    factor_block(both, 7)
    await_landed(place, pair.at[:, 1 - core], x_recv)
    for t in range(3):
        pair[t] = dot(mix[t] * (1.0 / N), pair[t].reshape(RANK, RANK), precision=HIGH).reshape(2, RANK // 2, RANK)
    half_swap.wait_send()
    for send in sends:
        send.wait_send()
    for step in range(3):
        await_sent(place, first[step], s_send.at[step, 0])
        await_sent(place, whole[step], s_send.at[step, 1])
    await_sent(place, other, d_send)

    term = qbuf
    mine = pl.ds(pl.multiple_of(core * (RANK // 2), RANK // 2), RANK // 2)
    ones = jnp.ones((8, RANK), F32)
    own = lax.broadcasted_iota(jnp.int32, (RANK, RANK), 0) // (RANK // 2) == core
    for t in range(3):
        pair[t] = dot(both[t, :, RANK:], pair[t].reshape(RANK, RANK), precision=HIGH).reshape(2, RANK // 2, RANK)
        term[t, z, x, y, core] = pair[t, core]

    def tell(stage, where, peer, sem):
        return pltpu.make_async_remote_copy(norms.at[stage, where], norms.at[stage, where], n_send.at[stage, sem],
                                            n_recv.at[stage, sem], device_id=peer, device_id_type=MESH)

    def sum_norms():
        for t in range(3):
            product = pair[t].reshape(RANK, RANK)
            norms[0, core, t] = dot(ones, jnp.where(own, product * product, 0.0), NT, HIGH)
        tell(0, core, place.sibling(), 0).start()
        yield
        tell(0, 1 - core, place.sibling(), 0).wait_recv()
        total = norms[0, 0] + norms[0, 1]
        for axis in range(3):
            stage = 1 + axis
            here = place.at[axis]
            norms[stage, here] = total
            for d in (1, 2, 3):
                tell(stage, here, place.chip(axis, d), d).start()
            yield
            for d in (1, 2, 3):
                tell(stage, place.far(axis, N - d), place.chip(axis, d), d).wait_recv()
            total = (norms[stage, 0] + norms[stage, 1]) + (norms[stage, 2] + norms[stage, 3])
            if axis == 0:
                for t in range(3):
                    left = dot(zown[:, t].reshape(rows, RANK), mix[t], NT, HIGH)
                    left_ref[t] = dot(left, both[t, :, RANK:], NT, HIGH)
        scales = 1.0 / jnp.sqrt(total + 1e-6)
        for t in range(3):
            scale = scales[t, 0:1]
            left = left_ref[t]
            high, low = split(jnp.concatenate([left * 0.05, left * (scale * gain)], 0), 2)
            lhs[t] = jnp.concatenate(
                [jnp.concatenate([high, high], 1), jnp.concatenate([low, jnp.zeros_like(low)], 1)], 0)
            basis = pair[t].reshape(RANK, RANK).T * scale
            basis_ref[:, t * RANK:(t + 1) * RANK] = jnp.where(core == 0, basis[:RANK // 2], basis[RANK // 2:])
        tell(0, core, place.sibling(), 0).wait_send()
        for axis in range(3):
            for d in (1, 2, 3):
                tell(1 + axis, place.at[axis], place.chip(axis, d), d).wait_send()
        yield

    def emit(j1, j2):
        for t in range(3):
            where = place.chips(t, j1, j2)
            block = jnp.concatenate([term[(t, *chip)].reshape(RANK, RANK) for chip in where], 1)
            out = dot(lhs[t], jnp.concatenate(split(block, 2), 0))
            out = out[:RANK] + out[RANK:]
            for i, (cz, cx, cy) in enumerate(where):
                column = pl.ds(pl.multiple_of(((cz * N + cx) * N + cy) * RANK, RANK), RANK)
                tile = slice(i * RANK, (i + 1) * RANK)
                h, m, l = [parts[t, j * rows:(j + 1) * rows, column].astype(F32) for j in range(3)]
                full[t, cz, cx, cy, 0] = (h + (m + l)) - out[:rows, tile]
                full[t, cz, cx, cy, 1] = out[rows:, tile]

    norm_steps = sum_norms()
    for _ in fine_gather(place, term, sems_term, emit):
        next(norm_steps, None)


def last_kernel(both_ref, basis_in, next_ref, update_ref, basis_ref):
    t, i = pl.program_id(0), pl.program_id(1)
    count = update_ref.shape[2] // RANK
    for j in range(count):
        chip = i * count + j
        where = (t, chip // (N * N), lax.rem(chip // N, N), lax.rem(chip, N))
        next_ref[0, 0, :, j * RANK:(j + 1) * RANK] = both_ref[(*where, 0)]
        update_ref[0, :, j * RANK:(j + 1) * RANK] = both_ref[(*where, 1)]
    basis_ref[...] = basis_in[...]


def body(momentum, gradient, basis):
    momentum, gradient = momentum[0], gradient[0]
    count, rows, width = momentum.shape
    chips = (N, N, N, 2)
    dma = pltpu.SemaphoreType.DMA
    f32 = lambda *shape: jax.ShapeDtypeStruct(shape, F32)
    room = lambda *shape: pltpu.VMEM(shape, F32)
    gain = float((2048 * 8192 / RANK) ** 0.5)
    full, basis_next = pl.pallas_call(
        functools.partial(main_kernel, gain),
        name="dion",
        out_shape=[room(3, *chips, 64, RANK), room(64, 3 * RANK)],
        in_specs=[ANY] * 3,
        out_specs=[VMEM] * 2,
        scratch_shapes=[
            pltpu.VMEM((count, 3 * rows, width), BF16), room(3, *chips, 64, RANK), room(3, rows, RANK),
            pltpu.VMEM((3, 2 * RANK, 2 * RANK), BF16), room(4, N, 3, 8, RANK),
            room(4, count, rows, 512), room(4, count, rows, 512),
            room(count, rows, RANK), room(N, 3, 16, RANK), room(N, 3, 16, RANK), room(3, *chips, 16, RANK),
            pltpu.VMEM((3, 2 * RANK, 4 * rows), BF16), room(3, RANK, 2 * RANK),
            room(3, N, N, N, 64, RANK),
            room(3, 2, N, N, 32, RANK), room(3, 2, N, N, 64, RANK),
            room(3, 2, N, 32, RANK), room(3, 2, N, 64, RANK),
            room(3, 2, 32, RANK), room(3, 2, 64, RANK),
            room(3, 2, 64, RANK), room(3, 64, RANK), room(3, RANK, RANK), room(2, 3, RANK, RANK),
            pltpu.VMEM((3, 2 * RANK, 3 * RANK), BF16),
            dma((3,)), dma((2, 4)), dma((2, 4)), dma((2, 4)),
            dma, dma((N,)), dma((3, 2)), dma((3, 2, 2)), dma, dma, dma, dma, dma((4, 4)), dma((4, 4))] + fine_sems() + gather_sems() + fine_sems(),
        compiler_params=pltpu.CompilerParams(collective_id=0, has_side_effects=True, vmem_limit_bytes=49 * 2 ** 20),
    )(momentum, gradient, basis)
    span = 4096
    full, basis_next = [pltpu.with_memory_space_constraint(a, pltpu.VMEM) for a in (full, basis_next)]
    return pl.pallas_call(
        last_kernel,
        name="outputs",
        grid=(3, width // span),
        out_shape=[f32(1, count, rows, width), f32(count, rows, width), f32(64, 3 * RANK)],
        in_specs=[VMEM] * 2,
        out_specs=[
            pl.BlockSpec((1, 1, rows, span), lambda t, i: (0, t, 0, i)),
            pl.BlockSpec((1, rows, span), lambda t, i: (t, 0, i)),
            pl.BlockSpec((64, 3 * RANK), lambda t, i: (0, 0)),
        ],
        compiler_params=pltpu.CompilerParams(vmem_limit_bytes=16 * 2 ** 20),
    )(full, basis_next)


def solution(mesh):
    placed = (P("rep", None, "fsdp", None), P("rep", None, "fsdp", None), P(("rep", "fsdp"), None))
    return jax.shard_map(
        body,
        mesh=mesh,
        in_specs=placed,
        out_specs=(P("rep", None, "fsdp", None), P(None, "fsdp", None), P(("rep", "fsdp"), None)),
        check_vma=False,
    )
```
